128 devices in a mesh: dp: 16 (over x, y_hi, core), tensor: 8 (over y_lo, z).
Axes of the slice: x: 4, y: 4 (y_hi: 2, y_lo: 2; y = y_hi * 2 + y_lo), z: 4, core: 2. Of those that a mesh axis runs over, the one named last changes fastest.
Arguments:
- student_in: bfloat16 [16384, 4096], P(('dp', 'tensor')), may hold values from -24 to 24
- norm_gain: float32 [4096], replicated, may hold values from 0.5 to 1.5
- w_query: bfloat16 [4096, 4096], P(None, 'tensor'), may hold values from -0.09375 to 0.09375
- w_key: bfloat16 [4096, 1024], P(None, 'tensor'), may hold values from -2.90625 to 2.90625
- w_value: bfloat16 [4096, 1024], P(None, 'tensor'), may hold values from -0.09375 to 0.09375
- w_out: bfloat16 [4096, 4096], P('tensor'), may hold values from -0.09375 to 0.09375
- projection: bfloat16 [4096, 8192], P(None, 'tensor'), may hold values from -0.09375 to 0.09375
- teacher_rows: bfloat16 [16384, 8192], P('dp', 'tensor'), may hold values from -6 to 6
- lengths: int32 [16], P('dp'), may hold values from 256 to 1024, as said below
Outputs:
- proj_grad: float32 [4096, 8192], P('dp', 'tensor')
- seq_loss: float32 [16], P('dp')
The draws below stay inside these ranges and needn't reach their ends.
Inputs may be any that keep to these rules, and one draw needn't show every extreme that they name: `lengths`: at least one sequence is valid over all 1024 positions.
All inputs are finite; a program needn't handle non-finite values.
Results may differ from the reference program's by a relative error of at most 0.017.
Values may be sent and summed in bfloat16 or wider, within the bound.
No kernel may reach another device: no remote copies, remote signals or barrier semaphores. Data moves between devices by JAX's collectives and lax.ppermute only.
A program may use at most 128 MiB of HBM per device.

```python
import math
import jax
import jax.numpy as jnp
from jax import lax

D = 4096
HEADS = 32
KV_HEADS = 8
HEAD_DIM = 128
DT = 8192
SEQ = 1024
SEQUENCES = 16
N_TENSOR = 8


def shared_query(key):
    drawn = jax.random.normal(key, (D, HEADS * HEAD_DIM), jnp.float32)
    return jnp.clip(drawn, -6.0, 6.0) * D ** (-0.5)


def draw_w_query(key, part):
    return shared_query(key).astype(jnp.bfloat16)


def draw_w_key(key, part):
    key = jax.random.fold_in(key, 5)
    noise = jnp.clip(jax.random.normal(key, (D, KV_HEADS * HEAD_DIM), jnp.float32), -6.0, 6.0) * D ** (-0.5)
    drawn = noise
    return drawn.astype(jnp.bfloat16)


def draw_lengths(key, part):
    key = jax.random.fold_in(key, 7)
    first_key, second_key = jax.random.split(key)
    drawn = jax.random.randint(first_key, (SEQUENCES,), SEQ // 4, SEQ + 1)
    filled = jax.random.randint(second_key, (), 0, SEQUENCES)
    return jnp.where(jnp.arange(SEQUENCES) == filled, SEQ, drawn).astype(jnp.int32)


def with_spikes(entries, key, source, target, shards_of, factor):
    def block_of(position):
        return (jnp.arange(entries.shape[position]) // (entries.shape[position] // shards_of)).reshape((-1,) + (1,) * (entries.ndim - 1 - position))

    first = jax.random.permutation(key, shards_of)[block_of(target)]
    far = (block_of(target) + shards_of // 2) % shards_of
    return jnp.where((block_of(source) == first) | (block_of(source) == far), factor * entries, entries)


def shard_levels(own_key, shape, shards, smallest, high):
    def one(dim, shards_of):
        heights = jax.random.uniform(jax.random.fold_in(jax.random.fold_in(own_key, 6), dim), (shards_of,), jnp.float32, smallest / len(shards), high / len(shards))
        return jnp.repeat(jnp.exp(heights), shape[dim] // shards_of).reshape((-1,) + (1,) * (len(shape) - dim - 1))

    factor_of = one(*shards[0])
    for cut in shards[1:]:
        factor_of = factor_of * one(*cut)
    return factor_of


def centred(key, shape, scale, reach, pieces=(), kind=jnp.bfloat16):
    values = scale * jax.random.normal(key, shape, jnp.float32)
    if pieces:
        values = values * shard_levels(key, shape, pieces, -0.22, 0.18)
    return jnp.clip(values, -reach, reach).astype(kind)


def gaussian_with(stream_key, extent, deviation, most, shards, heavy, held_as=jnp.bfloat16):
    result = deviation * jax.random.normal(stream_key, extent, jnp.float32)
    if shards:
        result = result * shard_levels(stream_key, extent, shards, -0.22, 0.18)
    return jnp.clip(with_spikes(result, jax.random.fold_in(stream_key, 3), *heavy), -most, most).astype(held_as)


def setup_inputs(seed: int = 0) -> dict:
    splits = jax.random.split(jax.random.key(seed), 10)
    student_in = gaussian_with(splits[0], (SEQUENCES * SEQ, D), 1.0, 24.0, ((0, 128),), (0, 1, 128, 5.5))
    norm_gain = jnp.clip(1.0 + 0.1 * jax.random.normal(splits[1], (D,), jnp.float32), 0.5, 1.5)
    w_query = draw_w_query(jax.random.fold_in(splits[9], 71), 0)
    w_key = draw_w_key(jax.random.fold_in(splits[9], 71), 0)
    w_value = centred(splits[4], (D, KV_HEADS * HEAD_DIM), D ** -0.5, 0.09375, ((1, 8),))
    w_out = centred(splits[5], (HEADS * HEAD_DIM, D), (HEADS * HEAD_DIM) ** -0.5, 0.09375, ((0, 8),))
    projection = centred(splits[6], (D, DT), D ** -0.5, 0.09375, ((1, 8),))
    teacher_rows = centred(splits[7], (SEQUENCES * SEQ, DT), 1.0, 6.0, ((0, 16), (1, 8)))
    lengths = draw_lengths(jax.random.fold_in(splits[9], 71), 0)
    return {"student_in": student_in, "norm_gain": norm_gain, "w_query": w_query, "w_key": w_key, "w_value": w_value, "w_out": w_out, "projection": projection, "teacher_rows": teacher_rows, "lengths": lengths}


EPSILON = 1e-05
ROPE_BASE = 500000.0
NEG_LARGE = -1e+30

def root_norm(inputs, norm_gain):
    widened = inputs.astype(jnp.float32)
    mean_square = lax.optimization_barrier(jnp.mean(widened * widened, axis=-1, keepdims=True))
    return (widened * lax.rsqrt(mean_square + EPSILON) * norm_gain).astype(jnp.bfloat16)

def rotate(values):
    seq_len = values.shape[0]
    half_dim = HEAD_DIM // 2
    positions = jnp.arange(seq_len).astype(jnp.float32)[:, None]
    inverse = ROPE_BASE ** (-2.0 * jnp.arange(half_dim).astype(jnp.float32) / HEAD_DIM)
    angles = (positions * inverse)[:, None, :]
    cosine = jnp.cos(angles)
    sine_part = jnp.sin(angles)
    heads_view = values.reshape(seq_len, -1, HEAD_DIM)
    lower_half = heads_view[..., :half_dim]
    upper_half = heads_view[..., half_dim:]
    turned = jnp.concatenate([lower_half * cosine - upper_half * sine_part, upper_half * cosine + lower_half * sine_part], axis=-1)
    return turned.reshape(seq_len, -1).astype(jnp.bfloat16)

def attend(queries, keys_all, values_all, length):
    seq_len = queries.shape[0]
    kv_count = keys_all.shape[1] // HEAD_DIM
    group_size = queries.shape[1] // HEAD_DIM // kv_count
    block_len = min(512, seq_len)
    factor = 1.0 / math.sqrt(HEAD_DIM)
    outputs = []
    for number in range(seq_len // block_len):
        key_end = (number + 1) * block_len
        query_block = queries[number * block_len:key_end].reshape(block_len, kv_count, group_size, HEAD_DIM)
        key_block = keys_all[:key_end].reshape(key_end, kv_count, HEAD_DIM)
        value_block = values_all[:key_end].reshape(key_end, kv_count, HEAD_DIM)
        scores = jnp.einsum('qhgd,khd->hgqk', query_block.astype(jnp.float32), key_block.astype(jnp.float32)) * factor
        query_pos = number * block_len + jnp.arange(block_len)
        key_pos = jnp.arange(key_end)
        allowed = (query_pos[:, None] >= key_pos[None, :]) & (key_pos[None, :] < length)
        scores = jnp.where(allowed, scores, NEG_LARGE)
        highest = lax.optimization_barrier(jnp.max(scores, axis=-1, keepdims=True))
        weights = jnp.exp(scores - highest)
        weights_low = (weights / lax.optimization_barrier(jnp.sum(weights, axis=-1, keepdims=True))).astype(jnp.bfloat16)
        blended = jnp.einsum('hgqk,khd->qhgd', weights_low.astype(jnp.float32), value_block.astype(jnp.float32))
        outputs.append(blended.astype(jnp.bfloat16).reshape(block_len, -1))
    return jnp.concatenate(outputs, axis=0)

def reference(student_in, norm_gain, w_query, w_key, w_value, w_out, projection, teacher_rows, lengths):
    inputs_all = student_in.reshape(SEQUENCES, SEQ, D)
    teacher_all = teacher_rows.reshape(SEQUENCES, SEQ, DT)
    per_device = HEADS // N_TENSOR * HEAD_DIM

    def one_sequence(carried, packed):
        inputs, teacher, length = packed
        normed = root_norm(inputs, norm_gain)
        queries = rotate(jnp.dot(normed, w_query, preferred_element_type=jnp.float32))
        keys_all = rotate(jnp.dot(normed, w_key, preferred_element_type=jnp.float32))
        values_all = jnp.dot(normed, w_value, preferred_element_type=jnp.float32).astype(jnp.bfloat16)
        attended = attend(queries, keys_all, values_all, length)
        summed = jnp.zeros((SEQ, D), jnp.float32)
        for member in range(N_TENSOR):
            term = jnp.dot(attended[:, member * per_device:(member + 1) * per_device], w_out[member * per_device:(member + 1) * per_device], preferred_element_type=jnp.float32).astype(jnp.bfloat16)
            summed = summed + lax.optimization_barrier(term).astype(jnp.float32)
        layer = (inputs.astype(jnp.float32) + summed).astype(jnp.bfloat16)
        predicted = jnp.dot(layer, projection, preferred_element_type=jnp.float32)
        live = (jnp.arange(SEQ) < length)[:, None]
        residue = jnp.where(live, predicted - teacher.astype(jnp.float32), jnp.float32(0.0))
        scale_len = length.astype(jnp.float32)
        loss_value = jnp.sum(residue * residue) / (scale_len * DT)
        error_grad = (residue / scale_len).astype(jnp.bfloat16)
        updated = carried + lax.dot_general(layer, error_grad, (((0,), (0,)), ((), ())), preferred_element_type=jnp.float32)
        return (updated, loss_value)
    proj_grad, seq_loss = lax.scan(one_sequence, jnp.zeros((D, DT), jnp.float32), (inputs_all, teacher_all, lengths))
    return (proj_grad, seq_loss)
```

```python
import math

import jax
import jax.numpy as jnp
from jax import lax
from jax.sharding import Mesh, PartitionSpec as P

HEAD_DIM = 128
DT = 8192
EPSILON = 1e-05
ROPE_BASE = 500000.0
NEG_LARGE = -1e30
AXES = ("x", "yh", "c", "yl", "z")
SIZES = {"x": 4, "yh": 2, "c": 2, "yl": 2, "z": 4}
F32 = jnp.float32
BF16 = jnp.bfloat16


def shift(value, axis, step):
    count = SIZES[axis]
    return lax.ppermute(value, axis, [(i, (i + step) % count) for i in range(count)])


def shift_y(value, step):
    return lax.ppermute(value, ("yh", "yl"), [(i, (i + step) % 4) for i in range(4)])


def after(value, *others):
    return lax.optimization_barrier((value, *others))[0]


def rows_of(array, start, count):
    return lax.dynamic_slice_in_dim(array, start, count, 0)


def dot(left, right):
    return jnp.dot(left, right, preferred_element_type=F32)


def root_norm(inputs, norm_gain):
    widened = inputs.astype(F32)
    mean_square = jnp.mean(widened * widened, axis=-1, keepdims=True)
    return (widened * lax.rsqrt(mean_square + EPSILON) * norm_gain).astype(BF16)


def rotate(values, cosine, sine):
    rows = values.shape[0]
    half = HEAD_DIM // 2
    view = values.reshape(rows, -1, HEAD_DIM)
    lower, upper = view[..., :half], view[..., half:]
    cosine, sine = cosine[:, None, :], sine[:, None, :]
    turned = jnp.concatenate([lower * cosine - upper * sine, upper * cosine + lower * sine], axis=-1)
    return turned.reshape(rows, -1).astype(BF16)


def fetch(plus, minus):
    up, down = shift_y(plus, 1), shift_y(minus, -1)
    return up, down


def swap(pair):
    return tuple(shift(v, "c", 1) for v in pair)


def attend(queries, keys_own, values_own, keys_far, values_far, masks):
    rows = queries.shape[0]
    heads = queries.reshape(rows, 4, HEAD_DIM)
    keys = jnp.concatenate([keys_own, keys_far], axis=0)
    values = jnp.concatenate([values_own, values_far], axis=0)
    scores = jnp.einsum("qgd,kd->gqk", heads, keys, preferred_element_type=F32)
    scores = scores * (1.0 / math.sqrt(HEAD_DIM))
    scores = jnp.where(masks, scores, NEG_LARGE)
    highest = jnp.max(scores, axis=-1, keepdims=True)
    weights = jnp.exp(scores - highest)
    low = (weights / jnp.sum(weights, axis=-1, keepdims=True)).astype(BF16)
    blended = jnp.einsum("gqk,kd->qgd", low, values, preferred_element_type=F32)
    return blended.astype(BF16).reshape(rows, -1)


def shards(
    student_in, norm_gain, w_query, w_key, w_value, w_out, projection, teacher_rows, lengths
):
    x, yh, c, yl, z = (lax.axis_index(a) for a in AXES)
    length = lengths[0]

    normed_own = root_norm(student_in, norm_gain)
    pieces = [normed_own] + [shift(normed_own, "z", -j) for j in (1, 2, 3)]

    kv_own = jnp.concatenate([w_key, w_value], axis=1)
    q_part = lax.dynamic_slice_in_dim(w_query, c * 256, 256, 1)
    kv_part = rows_of(kv_own, c * 2048, 2048)
    first = fetch(
        jnp.concatenate([q_part[:2048], kv_part[:1024]], axis=0),
        jnp.concatenate([q_part[2048:], kv_part[1024:]], axis=0),
    )
    first_sib = swap(first)
    out_part = after(rows_of(w_out, c * 256, 256), *first)
    second = fetch(out_part[:128], out_part[128:])
    second_sib = swap(second)
    proj_view = projection.reshape(8, 2, 256, 1024)
    proj_part = lax.dynamic_index_in_dim(proj_view, c, 1, keepdims=False).reshape(2048, 1024)
    proj_part = after(proj_part, *second)
    third = fetch(proj_part[:1024], proj_part[1024:])
    third_sib = swap(third)
    teach_far = shift(after(rows_of(teacher_rows, (1 - yl) * 512, 512), *third), "yl", 1)

    q_far = jnp.concatenate(
        [
            jnp.concatenate([first[0][:2048], first[1][:2048]], axis=0),
            jnp.concatenate([first_sib[0][:2048], first_sib[1][:2048]], axis=0),
        ],
        axis=1,
    )
    kv_mine = jnp.concatenate([first[0][2048:], first[1][2048:]], axis=0)
    kv_sib = jnp.concatenate([first_sib[0][2048:], first_sib[1][2048:]], axis=0)
    kv_far = jnp.concatenate(
        [jnp.where(c == 0, kv_mine, kv_sib), jnp.where(c == 0, kv_sib, kv_mine)], axis=0
    )
    out_far = jnp.concatenate([*second, *second_sib], axis=0)

    ring = jnp.concatenate([((z + j) % 4) * 128 + jnp.arange(128) for j in range(4)])
    pos = yl * 512 + ring
    pos_far = (1 - yl) * 512 + ring
    inverse = ROPE_BASE ** (-2.0 * jnp.arange(HEAD_DIM // 2).astype(F32) / HEAD_DIM)
    angles = pos.astype(F32)[:, None] * inverse
    cosine, sine = jnp.cos(angles), jnp.sin(angles)
    key_pos = jnp.concatenate([pos, pos_far])
    masks = (pos[:, None] >= key_pos[None, :]) & (key_pos[None, :] < length)

    normed = jnp.concatenate(pieces, axis=0)
    q_own = rotate(dot(normed, w_query), cosine, sine)
    own_kv = dot(normed, kv_own)
    far_kv = dot(normed, kv_far)
    k_own, k_oth = (rotate(v[:, :128], cosine, sine) for v in (own_kv, far_kv))
    v_own, v_oth = (v[:, 128:].astype(BF16) for v in (own_kv, far_kv))
    q_oth = rotate(dot(normed, q_far), cosine, sine)
    sent = shift(jnp.concatenate([k_oth, v_oth, k_own, v_own], axis=1), "yl", 1)
    att_own = attend(q_own, k_own, v_own, sent[:, :128], sent[:, 128:256], masks)
    att_oth = attend(q_oth, k_oth, v_oth, sent[:, 256:384], sent[:, 384:], masks)
    partial = (dot(att_own, w_out) + dot(att_oth, out_far)).astype(BF16)
    blocks = [partial[j * 128 : (j + 1) * 128] for j in range(4)]
    arrived = [blocks[0]] + [shift(blocks[j], "z", j) for j in (1, 2, 3)]
    own_sum = sum(v.astype(F32) for v in arrived)
    own_layer = (student_in.astype(F32) + own_sum).astype(BF16)

    layers = [own_layer] + [shift(own_layer, "z", -j) for j in (1, 2, 3)]
    layer = jnp.concatenate(layers, axis=0)
    split = layer.reshape(512, 8, 2, 256)
    layer_c = lax.dynamic_index_in_dim(split, c, 2, keepdims=False).reshape(512, 2048)
    layer_s = lax.dynamic_index_in_dim(split, 1 - c, 2, keepdims=False).reshape(512, 2048)
    layer_both = jnp.concatenate([layer_c, shift(layer_s, "c", 1)], axis=0)

    def in_ring(array, base):
        return jnp.concatenate(
            [rows_of(array, base + ((z + j) % 4) * 128, 128) for j in range(4)], axis=0
        ).astype(F32)

    live = (pos < length)[:, None]
    scale = length.astype(F32)

    def errors(predicted, teacher):
        residue = jnp.where(live, predicted - teacher, F32(0.0))
        return (residue / scale).astype(BF16), jnp.sum(residue * residue)

    pred_far = dot(layer_c, jnp.concatenate(third, axis=0)) + dot(
        layer_s, jnp.concatenate(third_sib, axis=0)
    )
    err_far, sq_far = errors(pred_far, in_ring(teach_far, 0))
    err_own, sq_own = errors(dot(layer, projection), in_ring(teacher_rows, yl * 512))
    squared = lax.psum(sq_far + sq_own, ("yl", "z"))
    seq_loss = squared.reshape(1) / (lengths.astype(F32) * DT)

    def gradient(error):
        both = jnp.concatenate([error, shift(error, "c", 1)], axis=0)
        return lax.dot_general(
            layer_both, both, (((0,), (0,)), ((), ())), preferred_element_type=F32
        ).astype(BF16)

    grad_far = gradient(err_far).reshape(4, 2, 256, 1024)
    grad_own = gradient(err_own).reshape(4, 2, 256, 1024)
    to_up = jnp.where(yl == 0, yh, 1 - yh)

    def pick(array, at, axis):
        return lax.dynamic_index_in_dim(array, at, axis, keepdims=False)

    def sum_x(array):
        total = pick(array, x, 0).astype(F32)
        for step in (1, 2, 3):
            total = total + shift(pick(array, (x + step) % 4, 0), "x", step).astype(F32)
        return total

    def sum_y(own, far, axis):
        total = pick(own, yh, axis).astype(F32)
        total = total + shift_y(pick(own, 1 - yh, axis), 2).astype(F32)
        total = total + shift_y(pick(far, to_up, axis), 1).astype(F32)
        total = total + shift_y(pick(far, 1 - to_up, axis), -1).astype(F32)
        return total

    a_x = sum_x(
        jnp.concatenate([grad_own[..., :512], grad_far[..., :512]], axis=-1)
    ).astype(BF16)
    b_y = sum_y(grad_own[..., 512:], grad_far[..., 512:], 1).astype(BF16)
    a = sum_y(a_x[..., :512], a_x[..., 512:], 0)
    b = sum_x(b_y)
    return jnp.concatenate([a, b], axis=-1), seq_loss


def solution(mesh):
    split = Mesh(mesh.devices.reshape(4, 2, 2, 2, 4), AXES)
    dp, tensor = ("x", "yh", "c"), ("yl", "z")
    placed = (
        P(dp + tensor, None),
        P(),
        P(None, tensor),
        P(None, tensor),
        P(None, tensor),
        P(tensor, None),
        P(None, tensor),
        P(dp, tensor),
        P(dp),
    )
    return jax.shard_map(
        shards, mesh=split, in_specs=placed, out_specs=(P(dp, tensor), P(dp)), check_vma=False
    )
```

```python
import functools
import math

import jax
import jax.numpy as jnp
from jax import lax
from jax.experimental import pallas as pl
from jax.experimental.pallas import tpu as pltpu
from jax.sharding import Mesh, PartitionSpec as P

HEAD_DIM = 128
DT = 8192
EPSILON = 1e-05
ROPE_BASE = 500000.0
NEG_LARGE = -1e30
AXES = ("x", "yh", "c", "yl", "z")
SIZES = {"x": 4, "yh": 2, "c": 2, "yl": 2, "z": 4}
F32 = jnp.float32
BF16 = jnp.bfloat16
PARAMS = pltpu.CompilerParams(vmem_limit_bytes=48 * 2**20)


def shift(value, axis, step):
    count = SIZES[axis]
    return lax.ppermute(value, axis, [(i, (i + step) % count) for i in range(count)])


def shift_y(value, step):
    return lax.ppermute(value, ("yh", "yl"), [(i, (i + step) % 4) for i in range(4)])


def after(value, *others):
    return lax.optimization_barrier((value, *others))[0]


def rows_of(array, start, count):
    return lax.dynamic_slice_in_dim(array, start, count, 0)


def pick(array, at, axis):
    return lax.dynamic_index_in_dim(array, at, axis, keepdims=False)


def dot(left, right):
    return jnp.dot(left, right, preferred_element_type=F32)


def norm_kernel(in_ref, gain_ref, out_ref):
    widened = in_ref[...].astype(F32)
    mean_square = jnp.mean(widened * widened, axis=-1, keepdims=True)
    out_ref[...] = (widened * lax.rsqrt(mean_square + EPSILON) * gain_ref[...]).astype(BF16)


def root_norm(inputs, norm_gain):
    return pl.pallas_call(
        norm_kernel,
        grid=(4,),
        in_specs=[
            pl.BlockSpec((32, 4096), lambda i: (i, 0)),
            pl.BlockSpec((1, 4096), lambda i: (0, 0)),
        ],
        out_specs=pl.BlockSpec((32, 4096), lambda i: (i, 0)),
        out_shape=jax.ShapeDtypeStruct((128, 4096), BF16),
        compiler_params=PARAMS,
    )(inputs, norm_gain.reshape(1, 4096))


def ring_step(block):
    return block ^ (block // 2)


def ring_position(index, z):
    return ((z + ring_step(index // 128)) % 4) * 128 + index % 128


def turned(product, cosine, sine, last):
    def turn(head):
        return head * cosine + pltpu.roll(head, 64, 1) * sine

    left, right = product[:, :128], product[:, 128:]
    right = jnp.where(last, right, turn(right))
    return jnp.concatenate([turn(left), right], axis=1).astype(BF16)


def own_heads_kernel(*refs):
    *x_refs, q_ref, kv_ref, cos_ref, sin_ref, out_ref = refs
    x = jnp.concatenate([ref[...] for ref in x_refs if ref.shape[1] == 4096], axis=0)
    last = pl.program_id(0) == 2

    def finish(w_ref):
        out_ref[...] = turned(dot(x, w_ref[...]), cos_ref[...], sin_ref[...], last)

    pl.when(pl.program_id(0) < 2)(lambda: finish(q_ref))
    pl.when(last)(lambda: finish(kv_ref))


def own_heads_of(pieces, w_query, kv_own, cosine, sine, earlier=None):
    rows, at = 128 * len(pieces), 0 if earlier is None else 3
    whole = pl.BlockSpec((128, 4096), lambda n: (0, 0))
    turn = pl.BlockSpec((rows, 128), lambda n: (at, 0))
    kept, alias = [], {}
    if earlier is not None:
        kept, alias = [earlier], {0: 0}
    return pl.pallas_call(
        own_heads_kernel,
        grid=(3,),
        in_specs=[pl.BlockSpec(memory_space=pl.ANY)] * len(kept)
        + [whole] * len(pieces)
        + [
            pl.BlockSpec((4096, 256), lambda n: (0, jnp.minimum(n, 1))),
            pl.BlockSpec((4096, 256), lambda n: (0, 0)),
            turn,
            turn,
        ],
        out_specs=pl.BlockSpec((rows, 256), lambda n: (at, n)),
        out_shape=jax.ShapeDtypeStruct((512, 768), BF16),
        input_output_aliases=alias,
        compiler_params=PARAMS,
    )(*kept, *pieces, w_query, kv_own, cosine, sine)


def far_heads_kernel(at_ref, a, b, c, d, w0, w1, w2, w3, cos_ref, sin_ref, out_ref, x_ref):
    core = at_ref[3]

    @pl.when(pl.program_id(0) == 0)
    def _():
        for j, ref in enumerate((a, b, c, d)):
            for k in range(4):
                source = ((core + k // 2) % 2) * 2048 + (k % 2) * 1024
                x_ref[128 * j : 128 * j + 128, 1024 * k : 1024 * k + 1024] = ref[
                    :, pl.ds(pl.multiple_of(source, 1024), 1024)
                ]

    product = dot(x_ref[:, :1024], w0[...])
    for k, ref in ((1, w1), (2, w2), (3, w3)):
        product = product + dot(x_ref[:, 1024 * k : 1024 * k + 1024], ref[...])
    out_ref[...] = turned(product, cos_ref[...], sin_ref[...], pl.program_id(0) == 2)


def far_heads_of(place, pieces, quarters, cosine, sine):
    whole = pl.BlockSpec((128, 4096), lambda n, at: (0, 0))
    weight = pl.BlockSpec((1024, 256), lambda n, at: (0, n))
    turn = pl.BlockSpec((512, 128), lambda n, at: (0, 0))
    return pl.pallas_call(
        far_heads_kernel,
        grid_spec=pltpu.PrefetchScalarGridSpec(
            num_scalar_prefetch=1,
            grid=(3,),
            in_specs=[whole] * 4 + [weight] * 4 + [turn] * 2,
            out_specs=pl.BlockSpec((512, 256), lambda n, at: (0, n)),
            scratch_shapes=[pltpu.VMEM((512, 4096), BF16)],
        ),
        out_shape=jax.ShapeDtypeStruct((512, 768), BF16),
        compiler_params=PARAMS,
    )(place, *pieces, *quarters, cosine, sine)


def attend_kernel(at_ref, q_ref, own_ref, far_ref, out_ref):
    z, yl, length = at_ref[0], at_ref[1], at_ref[2]
    factor = math.log2(math.e) / math.sqrt(HEAD_DIM)
    q = jnp.concatenate([q_ref[:, 128 * h : 128 * h + 128] for h in range(4)], axis=0)
    shape = (512, 512)
    ring = ring_position(lax.broadcasted_iota(jnp.int32, (1, 512), 1), z)
    q_at = ((z + ring_step(pl.program_id(0))) % 4) * 128 + lax.broadcasted_iota(jnp.int32, (512, 1), 0) % 128
    contract = (((1,), (1,)), ((), ()))

    def scores(kv_ref):
        return factor * lax.dot_general(q, kv_ref[:, :128], contract, preferred_element_type=F32)

    own_ok = (ring <= q_at) & (ring + yl * 512 < length)
    own = jnp.where(jnp.broadcast_to(own_ok, shape), scores(own_ref), NEG_LARGE)
    top = jnp.max(own, axis=-1, keepdims=True)

    def store(total, blended):
        blended = (blended / total).astype(BF16)
        for h in range(4):
            out_ref[:, 128 * h : 128 * h + 128] = blended[128 * h : 128 * h + 128]

    @pl.when(yl == 0)
    def _():
        weights = jnp.exp2(own - top)
        store(
            jnp.sum(weights, axis=-1, keepdims=True), dot(weights.astype(BF16), own_ref[:, 128:])
        )

    @pl.when(yl == 1)
    def _():
        far = jnp.where(jnp.broadcast_to(ring < length, shape), scores(far_ref), NEG_LARGE)
        highest = jnp.maximum(top, jnp.max(far, axis=-1, keepdims=True))
        own_weights = jnp.exp2(own - highest)
        far_weights = jnp.exp2(far - highest)
        total = jnp.sum(own_weights, axis=-1, keepdims=True) + jnp.sum(
            far_weights, axis=-1, keepdims=True
        )
        store(
            total,
            dot(own_weights.astype(BF16), own_ref[:, 128:])
            + dot(far_weights.astype(BF16), far_ref[:, 128:]),
        )


def attend(place, heads, far_kv):
    return pl.pallas_call(
        attend_kernel,
        grid_spec=pltpu.PrefetchScalarGridSpec(
            num_scalar_prefetch=1,
            grid=(4,),
            in_specs=[
                pl.BlockSpec((128, 512), lambda j, at: (j, 0)),
                pl.BlockSpec((512, 256), lambda j, at: (0, 2)),
                pl.BlockSpec((512, 256), lambda j, at: (0, 0)),
            ],
            out_specs=pl.BlockSpec((128, 512), lambda j, at: (j, 0)),
        ),
        out_shape=jax.ShapeDtypeStruct((512, 512), BF16),
        compiler_params=PARAMS,
    )(place, heads, heads, far_kv)


def layer_kernel(at_ref, student_ref, *refs):
    *parts, out_ref = refs
    total = parts[0][...].astype(F32)
    for part in parts[1:]:
        total = total + part[...].astype(F32)
    layer = (student_ref[...].astype(F32) + total).astype(BF16)
    even = [layer[:, 512 * i : 512 * i + 256] for i in range(8)]
    odd = [layer[:, 512 * i + 256 : 512 * i + 512] for i in range(8)]

    @pl.when(at_ref[3] == 0)
    def _():
        out_ref[...] = jnp.concatenate(even + odd, axis=1)

    @pl.when(at_ref[3] == 1)
    def _():
        out_ref[...] = jnp.concatenate(odd + even, axis=1)


def make_layer(place, student_in, parts):
    spec = pl.BlockSpec((32, 4096), lambda i, at: (i, 0))
    return pl.pallas_call(
        layer_kernel,
        grid_spec=pltpu.PrefetchScalarGridSpec(
            num_scalar_prefetch=1, grid=(4,), in_specs=[spec] * 5, out_specs=spec
        ),
        out_shape=jax.ShapeDtypeStruct((128, 4096), BF16),
        compiler_params=PARAMS,
    )(place, student_in, *parts)


def out_kernel(at_ref, own, far, w, w0, w1, w2, w3, *out_refs):
    total = dot(own[...], w[...])
    for k, ref in enumerate((w0, w1, w2, w3)):
        source = ((at_ref[3] + k // 2) % 2) * 256 + (k % 2) * 128
        total = total + dot(far[:, pl.ds(pl.multiple_of(source, 128), 128)], ref[...])
    for j, ref in enumerate(out_refs):
        ref[...] = total[128 * j : 128 * j + 128].astype(BF16)


def out_blocks(place, own, far, w_out, quarters):
    att = pl.BlockSpec((512, 512), lambda n, at: (0, 0))
    quarter = pl.BlockSpec((128, 512), lambda n, at: (0, n))
    return pl.pallas_call(
        out_kernel,
        grid_spec=pltpu.PrefetchScalarGridSpec(
            num_scalar_prefetch=1,
            grid=(8,),
            in_specs=[att, att, pl.BlockSpec((512, 512), lambda n, at: (0, n))] + [quarter] * 4,
            out_specs=[quarter] * 4,
        ),
        out_shape=[jax.ShapeDtypeStruct((128, 4096), BF16)] * 4,
        compiler_params=PARAMS,
    )(place, own, far, w_out, *quarters)


def error_kernel(first, count, at_ref, *refs):
    kept = 0 if first == 0 else 2
    layers = refs[kept : kept + count]
    p_own, f0, f1, f2, f3, t_own, t_far, err_ref, sum_ref, x_ref, n_ref = refs[kept + count :]
    step = pl.program_id(0)
    z, yl, length, core = at_ref[0], at_ref[1], at_ref[2], at_ref[3]
    rows = 128 * count

    @pl.when(step == 0)
    def _():
        for j, ref in enumerate(layers):
            here = slice(128 * j, 128 * j + 128)
            x_ref[here, :] = ref[...]
            for i in range(16):
                block = i // 2 + 8 * ((core + i) % 2)
                n_ref[here, 256 * i : 256 * i + 256] = ref[
                    :, pl.ds(pl.multiple_of(block * 256, 256), 256)
                ]
        if first == 0:
            sum_ref[...] = jnp.zeros((1, 1), F32)
        else:
            sum_ref[...] = refs[1][...]

    index = 128 * first + lax.broadcasted_iota(jnp.int32, (rows, 1), 0)
    pos = yl * 512 + ring_position(index, z)
    live = jnp.broadcast_to(pos < length, (rows, 256))

    def part(predicted, t_ref):
        teacher = [
            t_ref[pl.ds(pl.multiple_of(((z + ring_step(first + j)) % 4) * 128, 128), 128), :]
            for j in range(count)
        ]
        residue = predicted - jnp.concatenate(teacher, axis=0).astype(F32)
        residue = jnp.where(live, residue, 0.0)
        err_ref[...] = (residue / length.astype(F32)).astype(BF16)
        sum_ref[...] += jnp.sum(residue * residue).reshape(1, 1)

    @pl.when(step < 2)
    def _():
        part(dot(n_ref[...], p_own[...]), t_own)

    @pl.when(step >= 2)
    def _():
        predicted = dot(x_ref[:, :1024], f0[...])
        for k, ref in ((1, f1), (2, f2), (3, f3)):
            predicted = predicted + dot(x_ref[:, 1024 * k : 1024 * k + 1024], ref[...])
        part(predicted, t_far)


def errors(half, place, layers, projection, p_far, t_own, t_far, earlier=None):
    def own(n, at):
        return (0, 2 * half + jnp.minimum(n, 1))

    def own_rows(n, at):
        return (at[1], 2 * half + jnp.minimum(n, 1))

    def far(n, at):
        return (0, 2 * half + jnp.maximum(n - 2, 0))

    count = len(layers)
    kept, alias, first = [], {}, 0
    kept_specs = []
    if earlier is not None:
        kept, alias, first = list(earlier), {1: 0}, 3
        kept_specs = [
            pl.BlockSpec(memory_space=pl.ANY),
            pl.BlockSpec((1, 1), lambda n, at: (0, 0)),
        ]
    whole = pl.BlockSpec((128, 4096), lambda n, at: (0, 0))
    return pl.pallas_call(
        functools.partial(error_kernel, first, count),
        grid_spec=pltpu.PrefetchScalarGridSpec(
            num_scalar_prefetch=1,
            grid=(4,),
            in_specs=kept_specs
            + [whole] * count
            + [pl.BlockSpec((4096, 256), own)]
            + [pl.BlockSpec((1024, 256), far)] * 4
            + [pl.BlockSpec((512, 256), own_rows), pl.BlockSpec((512, 256), far)],
            out_specs=[
                pl.BlockSpec((128 * count, 256), lambda n, at: (first, n)),
                pl.BlockSpec((1, 1), lambda n, at: (0, 0)),
            ],
            scratch_shapes=[pltpu.VMEM((128 * count, 4096), BF16)] * 2,
        ),
        out_shape=[
            jax.ShapeDtypeStruct((512, 1024), BF16),
            jax.ShapeDtypeStruct((1, 1), F32),
        ],
        input_output_aliases=alias,
        compiler_params=PARAMS,
    )(place, *kept, *layers, projection, *p_far, t_own, t_far)


def fetch(plus, minus):
    return shift_y(plus, 1), shift_y(minus, -1)


def swap(pair):
    return tuple(shift(v, "c", 1) for v in pair)


def shards(
    student_in, norm_gain, w_query, w_key, w_value, w_out, projection, teacher_rows, lengths
):
    x, yh, c, yl, z = (lax.axis_index(a) for a in AXES)
    length = lengths[0]
    place = jnp.stack([z, yl, length, c])

    def around(own):
        near, back = shift(own, "z", -1), shift(own, "z", 1)
        return [own, near, back, shift(after(own, near, back), "z", 2)]

    kv_own = jnp.concatenate([w_key, w_value], axis=1)

    def quarter(at):
        return jnp.concatenate([rows_of(w, at, 1024) for w in (w_query, w_key, w_value)], axis=1)

    first = fetch(quarter(c * 2048), quarter(c * 2048 + 1024))
    first_sib = swap(first)
    pieces = around(root_norm(student_in, norm_gain))

    inverse = ROPE_BASE ** (-2.0 * jnp.arange(HEAD_DIM // 2).astype(F32) / HEAD_DIM)
    pos = yl * 512 + ring_position(jnp.arange(512), z)
    angles = pos.astype(F32)[:, None] * inverse
    cosine, sine = jnp.cos(angles), jnp.sin(angles)
    cosine = jnp.concatenate([cosine, cosine], axis=1)
    sine = jnp.concatenate([-sine, sine], axis=1)

    out_part = after(rows_of(w_out, c * 256, 256), *first)
    second = fetch(out_part[:128], out_part[128:])

    near_heads = own_heads_of(pieces[:3], w_query, kv_own, cosine, sine)
    pieces[3] = after(pieces[3], near_heads)
    own_heads = own_heads_of(pieces[3:], w_query, kv_own, cosine, sine, near_heads)
    kv_early = shift(own_heads[:, 512:], "yl", 1)
    far_weights = [*first, *(after(v, own_heads) for v in first_sib)]
    far_heads = far_heads_of(place, pieces, far_weights, cosine, sine)
    kv_late = shift(far_heads[:, 512:], "yl", 1)
    att_far = attend(place, far_heads, kv_early)
    second = tuple(after(v, att_far) for v in second)
    second_sib = swap(second)
    kv_late = after(kv_late, att_far)
    att_own = attend(place, own_heads, kv_late)
    b0, b1, b2, b3 = out_blocks(place, att_own, att_far, w_out, [*second, *second_sib])

    proj_c = pick(projection.reshape(8, 2, 256, 1024), c, 1).reshape(2048, 1024)
    proj_c = after(proj_c, kv_late)
    third = fetch(proj_c[:1024], proj_c[1024:])
    teach_far = shift(after(rows_of(teacher_rows, (1 - yl) * 512, 512), *third), "yl", 1)

    parts = [b0, shift(b3, "z", 2), shift(b1, "z", 1), shift(b2, "z", -1)]
    own_layer = make_layer(place, student_in, parts)
    third_sib = swap(third)
    p_far = [*third, *third_sib]

    layers = around(own_layer)
    sib_near = shift(jnp.concatenate([v[:, 2048:] for v in layers[:3]], axis=0), "c", 1)

    near = [errors(h, place, layers[:3], projection, p_far, teacher_rows, teach_far) for h in (0, 1)]
    layers[3] = after(layers[3], near[0][0], near[1][0])
    sib_last = shift(layers[3][:, 2048:], "c", 1)
    layer_both = jnp.concatenate([v[:, :2048] for v in layers] + [sib_near, sib_last], axis=0)
    (err_a, sq_a), (err_b, sq_b) = (
        errors(h, place, layers[3:], projection, p_far, teacher_rows, teach_far, near[h])
        for h in (0, 1)
    )
    squared = sq_a + sq_b
    squared = lax.psum(squared + shift(squared, "yl", 1), "z")
    seq_loss = squared.reshape(1) / (lengths.astype(F32) * DT)

    def gradient(error):
        both = jnp.concatenate([error, shift(error, "c", 1)], axis=0)
        grad = lax.dot_general(
            layer_both, both, (((0,), (0,)), ((), ())), preferred_element_type=F32
        ).astype(BF16)
        return grad.reshape(4, 2, 256, 1024)

    to_up = jnp.where(yl == 0, yh, 1 - yh)

    def sum_x(array):
        total = pick(array, x, 0).astype(F32)
        for step in (1, 2, 3):
            total = total + shift(pick(array, (x + step) % 4, 0), "x", step).astype(F32)
        return total

    def sum_y(array, axis):
        own, far = array[..., :512], array[..., 512:]
        total = pick(own, yh, axis).astype(F32)
        total = total + shift_y(pick(own, 1 - yh, axis), 2).astype(F32)
        total = total + shift_y(pick(far, to_up, axis), 1).astype(F32)
        total = total + shift_y(pick(far, 1 - to_up, axis), -1).astype(F32)
        return total

    a_x = sum_x(gradient(err_a)).astype(BF16)
    b_y = sum_y(gradient(err_b), 1).astype(BF16)
    a = sum_y(after(a_x, seq_loss), 0)
    b = sum_x(after(b_y, seq_loss))
    return jnp.concatenate([a, b], axis=-1), seq_loss


def solution(mesh):
    split = Mesh(mesh.devices.reshape(4, 2, 2, 2, 4), AXES)
    dp, tensor = ("x", "yh", "c"), ("yl", "z")
    placed = (
        P(dp + tensor, None),
        P(),
        P(None, tensor),
        P(None, tensor),
        P(None, tensor),
        P(tensor, None),
        P(None, tensor),
        P(dp, tensor),
        P(dp),
    )
    return jax.shard_map(
        shards, mesh=split, in_specs=placed, out_specs=(P(dp, tensor), P(dp)), check_vma=False
    )
```

```python
import functools
import math

import jax
import jax.numpy as jnp
from jax import lax
from jax.experimental import pallas as pl
from jax.experimental.pallas import tpu as pltpu
from jax.sharding import Mesh, PartitionSpec as P

HEAD_DIM = 128
DT = 8192
EPSILON = 1e-05
ROPE_BASE = 500000.0
NEG_LARGE = -1e30
AXES = ("x", "yh", "c", "yl", "z")
SIZES = {"x": 4, "yh": 2, "c": 2, "yl": 2, "z": 4}
F32 = jnp.float32
BF16 = jnp.bfloat16
PARAMS = pltpu.CompilerParams(vmem_limit_bytes=48 * 2**20)


def shift(value, axis, step):
    count = SIZES[axis]
    return lax.ppermute(value, axis, [(i, (i + step) % count) for i in range(count)])


def shift_y(value, step):
    return lax.ppermute(value, ("yh", "yl"), [(i, (i + step) % 4) for i in range(4)])


def after(value, *others):
    return lax.optimization_barrier((value, *others))[0]


def rows_of(array, start, count):
    return lax.dynamic_slice_in_dim(array, start, count, 0)


def pick(array, at, axis):
    return lax.dynamic_index_in_dim(array, at, axis, keepdims=False)


def dot(left, right):
    return jnp.dot(left, right, preferred_element_type=F32)


HALVES = [jax.ShapeDtypeStruct((64, 4096), BF16)] * 2


def norm_kernel(top_ref, low_ref, gain_ref, out_top, out_low):
    for in_ref, out_ref in ((top_ref, out_top), (low_ref, out_low)):
        widened = in_ref[...].astype(F32)
        mean_square = jnp.mean(widened * widened, axis=-1, keepdims=True)
        out_ref[...] = (widened * lax.rsqrt(mean_square + EPSILON) * gain_ref[...]).astype(BF16)


def root_norm(inputs, norm_gain):
    top = pl.BlockSpec((32, 4096), lambda i: (i, 0))
    low = pl.BlockSpec((32, 4096), lambda i: (i + 2, 0))
    return pl.pallas_call(
        norm_kernel,
        grid=(2,),
        in_specs=[top, low, pl.BlockSpec((1, 4096), lambda i: (0, 0))],
        out_specs=[top, top],
        out_shape=HALVES,
        compiler_params=PARAMS,
    )(inputs, inputs, norm_gain.reshape(1, 4096))


def ring_step(block):
    return block ^ (block // 2)


def ring_position(index, z):
    return ((z + ring_step(index // 128)) % 4) * 128 + index % 128


def turned(product, cosine, sine, last):
    def turn(head):
        return head * cosine + pltpu.roll(head, 64, 1) * sine

    left, right = product[:, :128], product[:, 128:]
    right = jnp.where(last, right, turn(right))
    return jnp.concatenate([turn(left), right], axis=1).astype(BF16)


def own_heads_kernel(*refs):
    *x_refs, q_ref, kv_ref, cos_ref, sin_ref, out_ref = refs
    x = jnp.concatenate([ref[...] for ref in x_refs if ref.shape[1] == 4096], axis=0)
    last = pl.program_id(0) == 2

    def finish(w_ref):
        out_ref[...] = turned(dot(x, w_ref[...]), cos_ref[...], sin_ref[...], last)

    pl.when(pl.program_id(0) < 2)(lambda: finish(q_ref))
    pl.when(last)(lambda: finish(kv_ref))


def own_heads_of(pieces, w_query, kv_own, cosine, sine, earlier=None):
    rows, at = 64 * len(pieces), 0 if earlier is None else 3
    whole = pl.BlockSpec((64, 4096), lambda n: (0, 0))
    turn = pl.BlockSpec((rows, 128), lambda n: (at, 0))
    kept, alias = [], {}
    if earlier is not None:
        kept, alias = [earlier], {0: 0}
    return pl.pallas_call(
        own_heads_kernel,
        grid=(3,),
        in_specs=[pl.BlockSpec(memory_space=pl.ANY)] * len(kept)
        + [whole] * len(pieces)
        + [
            pl.BlockSpec((4096, 256), lambda n: (0, jnp.minimum(n, 1))),
            pl.BlockSpec((4096, 256), lambda n: (0, 0)),
            turn,
            turn,
        ],
        out_specs=pl.BlockSpec((rows, 256), lambda n: (at, n)),
        out_shape=jax.ShapeDtypeStruct((512, 768), BF16),
        input_output_aliases=alias,
        compiler_params=PARAMS,
    )(*kept, *pieces, w_query, kv_own, cosine, sine)


def far_heads_kernel(at_ref, *refs):
    *pieces, w0, w1, w2, w3, cos_ref, sin_ref, out_ref, x_ref = refs
    core = at_ref[3]

    @pl.when(pl.program_id(0) == 0)
    def _():
        for j, ref in enumerate(pieces):
            for k in range(4):
                source = ((core + k // 2) % 2) * 2048 + (k % 2) * 1024
                x_ref[64 * j : 64 * j + 64, 1024 * k : 1024 * k + 1024] = ref[
                    :, pl.ds(pl.multiple_of(source, 1024), 1024)
                ]

    product = dot(x_ref[:, :1024], w0[...])
    for k, ref in ((1, w1), (2, w2), (3, w3)):
        product = product + dot(x_ref[:, 1024 * k : 1024 * k + 1024], ref[...])
    out_ref[...] = turned(product, cos_ref[...], sin_ref[...], pl.program_id(0) == 2)


def far_heads_of(place, pieces, quarters, cosine, sine):
    whole = pl.BlockSpec((64, 4096), lambda n, at: (0, 0))
    weight = pl.BlockSpec((1024, 256), lambda n, at: (0, n))
    turn = pl.BlockSpec((512, 128), lambda n, at: (0, 0))
    return pl.pallas_call(
        far_heads_kernel,
        grid_spec=pltpu.PrefetchScalarGridSpec(
            num_scalar_prefetch=1,
            grid=(3,),
            in_specs=[whole] * 8 + [weight] * 4 + [turn] * 2,
            out_specs=pl.BlockSpec((512, 256), lambda n, at: (0, n)),
            scratch_shapes=[pltpu.VMEM((512, 4096), BF16)],
        ),
        out_shape=jax.ShapeDtypeStruct((512, 768), BF16),
        compiler_params=PARAMS,
    )(place, *pieces, *quarters, cosine, sine)


def attend_kernel(at_ref, q_ref, own_ref, far_ref, out_ref):
    z, yl, length = at_ref[0], at_ref[1], at_ref[2]
    factor = math.log2(math.e) / math.sqrt(HEAD_DIM)
    q = jnp.concatenate([q_ref[:, 128 * h : 128 * h + 128] for h in range(4)], axis=0)
    shape = (512, 512)
    ring = ring_position(lax.broadcasted_iota(jnp.int32, (1, 512), 1), z)
    q_at = ((z + ring_step(pl.program_id(0))) % 4) * 128 + lax.broadcasted_iota(jnp.int32, (512, 1), 0) % 128
    contract = (((1,), (1,)), ((), ()))

    def scores(kv_ref):
        return factor * lax.dot_general(q, kv_ref[:, :128], contract, preferred_element_type=F32)

    own_ok = (ring <= q_at) & (ring + yl * 512 < length)
    own = jnp.where(jnp.broadcast_to(own_ok, shape), scores(own_ref), NEG_LARGE)
    top = jnp.max(own, axis=-1, keepdims=True)

    def store(total, blended):
        blended = (blended / total).astype(BF16)
        for h in range(4):
            out_ref[:, 128 * h : 128 * h + 128] = blended[128 * h : 128 * h + 128]

    @pl.when(yl == 0)
    def _():
        weights = jnp.exp2(own - top)
        store(
            jnp.sum(weights, axis=-1, keepdims=True), dot(weights.astype(BF16), own_ref[:, 128:])
        )

    @pl.when(yl == 1)
    def _():
        far = jnp.where(jnp.broadcast_to(ring < length, shape), scores(far_ref), NEG_LARGE)
        highest = jnp.maximum(top, jnp.max(far, axis=-1, keepdims=True))
        own_weights = jnp.exp2(own - highest)
        far_weights = jnp.exp2(far - highest)
        total = jnp.sum(own_weights, axis=-1, keepdims=True) + jnp.sum(
            far_weights, axis=-1, keepdims=True
        )
        store(
            total,
            dot(own_weights.astype(BF16), own_ref[:, 128:])
            + dot(far_weights.astype(BF16), far_ref[:, 128:]),
        )


def attend(place, heads, far_kv):
    return pl.pallas_call(
        attend_kernel,
        grid_spec=pltpu.PrefetchScalarGridSpec(
            num_scalar_prefetch=1,
            grid=(4,),
            in_specs=[
                pl.BlockSpec((128, 512), lambda j, at: (j, 0)),
                pl.BlockSpec((512, 256), lambda j, at: (0, 2)),
                pl.BlockSpec((512, 256), lambda j, at: (0, 0)),
            ],
            out_specs=pl.BlockSpec((128, 512), lambda j, at: (j, 0)),
        ),
        out_shape=jax.ShapeDtypeStruct((512, 512), BF16),
        compiler_params=PARAMS,
    )(place, heads, heads, far_kv)


def layer_kernel(at_ref, *refs):
    *in_refs, out_top, out_low = refs

    def half(student_ref, parts, out_ref):
        total = parts[0][...].astype(F32)
        for part in parts[1:]:
            total = total + part[...].astype(F32)
        layer = (student_ref[...].astype(F32) + total).astype(BF16)
        even = [layer[:, 512 * i : 512 * i + 256] for i in range(8)]
        odd = [layer[:, 512 * i + 256 : 512 * i + 512] for i in range(8)]

        @pl.when(at_ref[3] == 0)
        def _():
            out_ref[...] = jnp.concatenate(even + odd, axis=1)

        @pl.when(at_ref[3] == 1)
        def _():
            out_ref[...] = jnp.concatenate(odd + even, axis=1)

    half(in_refs[0], in_refs[1:5], out_top)
    half(in_refs[5], in_refs[6:], out_low)


def make_layer(place, student_in, parts):
    top = pl.BlockSpec((32, 4096), lambda i, at: (i, 0))
    low = pl.BlockSpec((32, 4096), lambda i, at: (i + 2, 0))
    return pl.pallas_call(
        layer_kernel,
        grid_spec=pltpu.PrefetchScalarGridSpec(
            num_scalar_prefetch=1, grid=(2,), in_specs=[top] * 5 + [low] * 5, out_specs=[top, top]
        ),
        out_shape=HALVES,
        compiler_params=PARAMS,
    )(place, *[student_in, *parts] * 2)


def out_kernel(at_ref, own, far, w, w0, w1, w2, w3, *refs):
    *out_refs, x_ref = refs

    @pl.when(pl.program_id(0) == 0)
    def _():
        x_ref[:, :512] = own[...]
        for k in range(2):
            source = ((at_ref[3] + k) % 2) * 256
            x_ref[:, 512 + 256 * k : 768 + 256 * k] = far[:, pl.ds(pl.multiple_of(source, 256), 256)]

    weights = jnp.concatenate([ref[...] for ref in (w, w0, w1, w2, w3)], axis=0)
    total = dot(x_ref[...], weights)
    for j, ref in enumerate(out_refs):
        ref[...] = total[128 * j : 128 * j + 128].astype(BF16)


def out_blocks(place, own, far, w_out, quarters):
    att = pl.BlockSpec((512, 512), lambda n, at: (0, 0))
    quarter = pl.BlockSpec((128, 1024), lambda n, at: (0, n))
    return pl.pallas_call(
        out_kernel,
        grid_spec=pltpu.PrefetchScalarGridSpec(
            num_scalar_prefetch=1,
            grid=(4,),
            in_specs=[att, att, pl.BlockSpec((512, 1024), lambda n, at: (0, n))] + [quarter] * 4,
            out_specs=[quarter] * 4,
            scratch_shapes=[pltpu.VMEM((512, 1024), BF16)],
        ),
        out_shape=[jax.ShapeDtypeStruct((128, 4096), BF16)] * 4,
        compiler_params=PARAMS,
    )(place, own, far, w_out, *quarters)


def error_kernel(first, rows, kept, at_ref, *refs):
    layers = refs[kept:-11] if rows < 512 else refs[:2]
    p_own, f0, f1, t_own, t_far, err_ref, sum_ref = refs[len(layers) + kept :][:7]
    x_ref, n_ref = refs[-2:]
    step = pl.program_id(0)
    z, yl, length, core = at_ref[0], at_ref[1], at_ref[2], at_ref[3]

    @pl.when(step == 0)
    def _():
        if rows == 512:
            x_ref[:, :2048] = layers[0][...]
            x_ref[:, 2048:] = layers[1][...]
        else:
            for j, ref in enumerate(layers):
                x_ref[64 * j : 64 * j + 64, :] = ref[...]
            refs[-4][...] = x_ref[:, :2048]
            refs[-3][...] = x_ref[:, 2048:]
        for i in range(16):
            block = i // 2 + 8 * ((core + i) % 2)
            n_ref[:, 256 * i : 256 * i + 256] = x_ref[
                :, pl.ds(pl.multiple_of(block * 256, 256), 256)
            ]
        sum_ref[...] = refs[3][...] if kept else jnp.zeros((1, 1), F32)

    index = 128 * first + lax.broadcasted_iota(jnp.int32, (rows, 1), 0)
    pos = yl * 512 + ring_position(index, z)
    live = jnp.broadcast_to(pos < length, (rows, 256))

    def part(columns, predicted, t_ref):
        teacher = [
            t_ref[pl.ds(pl.multiple_of(((z + ring_step(first + j)) % 4) * 128, 128), 128), :]
            for j in range(rows // 128)
        ]
        residue = predicted - jnp.concatenate(teacher, axis=0).astype(F32)
        residue = jnp.where(live, residue, 0.0)
        err_ref[:, columns] = (residue / length.astype(F32)).astype(BF16)
        sum_ref[...] += jnp.sum(residue * residue).reshape(1, 1)

    part(slice(0, 256), dot(n_ref[...], p_own[...]), t_own)
    part(
        slice(256, 512),
        dot(x_ref[:, :2048], f0[...]) + dot(x_ref[:, 2048:], f1[...]),
        t_far,
    )


def errors(half, place, layers, projection, p_far, t_own, t_far, earlier=()):
    rows = 512 if layers[0].shape[0] == 512 else 64 * len(layers)
    first, kept = (3, 4) if earlier else (0, 0)

    def columns(n, at):
        return (0, 2 * half + n)

    def own_rows(n, at):
        return (at[1], 2 * half + n)

    def constant(n, at):
        return (0, 0)

    anywhere = pl.BlockSpec(memory_space=pl.ANY)
    kept_specs = [anywhere] * 3 + [pl.BlockSpec((1, 1), constant)] if earlier else []
    out_specs = [
        pl.BlockSpec((rows, 512), lambda n, at: (first, n)),
        pl.BlockSpec((1, 1), constant),
    ]
    out_shape = [
        jax.ShapeDtypeStruct((512, 1024), BF16),
        jax.ShapeDtypeStruct((1, 1), F32),
    ]
    if rows < 512:
        out_specs += [pl.BlockSpec((rows, 2048), lambda n, at: (first, 0))] * 2
        out_shape += [jax.ShapeDtypeStruct((512, 2048), BF16)] * 2
    if earlier:
        err, total, left, right = earlier
        earlier = (err, left, right, total)
    return pl.pallas_call(
        functools.partial(error_kernel, first, rows, kept),
        grid_spec=pltpu.PrefetchScalarGridSpec(
            num_scalar_prefetch=1,
            grid=(2,),
            in_specs=kept_specs
            + [pl.BlockSpec(v.shape, constant) for v in layers]
            + [pl.BlockSpec((4096, 256), columns)]
            + [pl.BlockSpec((2048, 256), columns)] * 2
            + [pl.BlockSpec((512, 256), own_rows), pl.BlockSpec((512, 256), columns)],
            out_specs=out_specs,
            scratch_shapes=[pltpu.VMEM((rows, 4096), BF16)] * 2,
        ),
        out_shape=out_shape,
        input_output_aliases={1: 0, 2: 2, 3: 3} if earlier else {},
        compiler_params=PARAMS,
    )(place, *earlier, *layers, projection, *p_far, t_own, t_far)


def split_columns(product):
    own = jnp.concatenate([product[:, :256], product[:, 512:768]], axis=1)
    far = jnp.concatenate([product[:, 256:512], product[:, 768:]], axis=1)
    return own, far


def by_y(at_ref, own, far, store):
    for t in (0, 1):
        this, that = slice(256 * t, 256 * t + 256), slice(256 - 256 * t, 512 - 256 * t)

        @pl.when(at_ref[5] == t)
        def _():
            store(0, own[this])
            store(1, own[that])

        @pl.when(at_ref[6] == t)
        def _():
            store(2, far[this])
            store(3, far[that])


def gradient_kernel(by_x, at_ref, mine, theirs, e_mine, e_theirs, *out_refs):
    contract = (((0,), (0,)), ((), ()))
    product = lax.dot_general(mine[...], e_mine[...], contract, preferred_element_type=F32)
    product = product + lax.dot_general(
        theirs[...], e_theirs[...], contract, preferred_element_type=F32
    )
    product = product.astype(BF16)
    if by_x:
        for k, ref in enumerate(out_refs):

            @pl.when(pl.program_id(0) == k)
            def _():
                ref[...] = product
    else:

        def store(k, value):
            out_refs[k][0] = value

        by_y(at_ref, *split_columns(product), store)


def gradient(by_x, place, mine, theirs, e_mine, e_theirs):
    rows = pl.BlockSpec((512, 512), lambda k, at: (0, (at[4] + k) % 4))
    error = pl.BlockSpec((512, 1024), lambda k, at: (0, 0))
    if by_x:
        out_spec = pl.BlockSpec((512, 1024), lambda k, at: (0, 0))
        shape = (512, 1024)
    else:
        out_spec = pl.BlockSpec((1, 256, 512), lambda k, at: (k, 0, 0))
        shape = (4, 256, 512)
    return pl.pallas_call(
        functools.partial(gradient_kernel, by_x),
        grid_spec=pltpu.PrefetchScalarGridSpec(
            num_scalar_prefetch=1,
            grid=(4,),
            in_specs=[rows, rows, error, error],
            out_specs=[out_spec] * 4,
        ),
        out_shape=[jax.ShapeDtypeStruct(shape, BF16)] * 4,
        compiler_params=PARAMS,
    )(place, mine, theirs, e_mine, e_theirs)


def total_of(refs):
    total = refs[0][...].astype(F32)
    for ref in refs[1:]:
        total = total + ref[...].astype(F32)
    return total


def sum_x_kernel(at_ref, *refs):
    def store(k, value):
        refs[4 + k][...] = value

    by_y(at_ref, *split_columns(total_of(refs[:4]).astype(BF16)), store)


def sum_y_kernel(at_ref, *refs):
    total = total_of(refs[:4]).astype(BF16)
    for k in range(4):
        refs[4 + k][...] = total[k]


def partial_sums(kernel, place, arrays):
    return pl.pallas_call(
        kernel,
        grid_spec=pltpu.PrefetchScalarGridSpec(
            num_scalar_prefetch=1,
            grid=(1,),
            in_specs=[pl.BlockSpec(memory_space=pltpu.VMEM)] * 4,
            out_specs=[pl.BlockSpec(memory_space=pltpu.VMEM)] * 4,
        ),
        out_shape=[jax.ShapeDtypeStruct((256, 512), BF16)] * 4,
        compiler_params=PARAMS,
    )(place, *arrays)


def last_kernel(*refs):
    refs[8][:, :512] = total_of(refs[:4])
    refs[8][:, 512:] = total_of(refs[4:8])


def last_sum(arrays):
    return pl.pallas_call(
        last_kernel,
        out_shape=jax.ShapeDtypeStruct((256, 1024), F32),
        compiler_params=PARAMS,
    )(*arrays)


def fetch(plus, minus):
    return shift_y(plus, 1), shift_y(minus, -1)


def swap(pair):
    return tuple(shift(v, "c", 1) for v in pair)


def shards(
    student_in, norm_gain, w_query, w_key, w_value, w_out, projection, teacher_rows, lengths
):
    x, yh, c, yl, z = (lax.axis_index(a) for a in AXES)
    length = lengths[0]
    to_up = jnp.where(yl == 0, yh, 1 - yh)
    place = jnp.stack([z, yl, length, c, x, yh, to_up])

    def around(top, low):
        top_up, low_down = shift(top, "z", 1), shift(low, "z", -1)
        low_up, top_down = shift(low, "z", 1), shift(top, "z", -1)
        ends = [shift(top_up, "z", 1), shift(low_down, "z", -1)]
        return [top, low, top_down, low_down, top_up, low_up], ends

    kv_own = jnp.concatenate([w_key, w_value], axis=1)

    def quarter(at):
        return jnp.concatenate([rows_of(w, at, 1024) for w in (w_query, w_key, w_value)], axis=1)

    first = fetch(quarter(c * 2048), quarter(c * 2048 + 1024))
    pieces, ends = around(*root_norm(student_in, norm_gain))
    first = tuple(after(v, *pieces[2:]) for v in first)
    first_sib = swap(first)

    inverse = ROPE_BASE ** (-2.0 * jnp.arange(HEAD_DIM // 2).astype(F32) / HEAD_DIM)
    pos = yl * 512 + ring_position(jnp.arange(512), z)
    angles = pos.astype(F32)[:, None] * inverse
    cosine, sine = jnp.cos(angles), jnp.sin(angles)
    cosine = jnp.concatenate([cosine, cosine], axis=1)
    sine = jnp.concatenate([-sine, sine], axis=1)

    out_part = after(rows_of(w_out, c * 256, 256), *first, *ends)
    second = fetch(out_part[:128], out_part[128:])

    near_heads = own_heads_of(pieces, w_query, kv_own, cosine, sine)
    ends = [after(v, near_heads) for v in ends]
    own_heads = own_heads_of(ends, w_query, kv_own, cosine, sine, near_heads)
    kv_early = shift(own_heads[:, 512:], "yl", 1)
    far_weights = [*first, *(after(v, own_heads) for v in first_sib)]
    far_heads = far_heads_of(place, pieces + ends, far_weights, cosine, sine)
    kv_late = shift(far_heads[:, 512:], "yl", 1)
    att_far = attend(place, far_heads, kv_early)
    second = tuple(after(v, att_far) for v in second)
    second_sib = swap(second)
    kv_late = after(kv_late, att_far)
    att_own = attend(place, own_heads, kv_late)
    b0, b1, b2, b3 = out_blocks(place, att_own, att_far, w_out, [*second, *second_sib])

    proj_c = pick(projection.reshape(8, 2, 256, 1024), c, 1).reshape(2048, 1024)
    sends = lax.optimization_barrier((proj_c[:1024], proj_c[1024:], ends[0]))[:2]
    third = fetch(*(after(v, kv_late, *second) for v in sends))

    parts = [b0, shift(b3, "z", 2), shift(b1, "z", 1), shift(b2, "z", -1)]
    own_layer = make_layer(place, student_in, parts)
    third = jnp.concatenate([after(v, own_layer[0]) for v in third], axis=0)
    third_sib = shift(third, "c", 1)
    teach_far = shift(after(rows_of(teacher_rows, (1 - yl) * 512, 512), third), "yl", 1)
    p_far = [third, third_sib]

    layers, ends = around(*own_layer)
    same = (projection, p_far, teacher_rows, teach_far)
    near = errors(1, place, layers, *same)
    ends = [after(v, near[0]) for v in ends]
    err_b, sq_b, mine, other = errors(1, place, ends, *same, earlier=near)
    theirs = shift(other, "c", 1)
    err_b_sib = shift(err_b, "c", 1)
    err_a, sq_a = errors(0, place, [mine, after(other, err_b)], *same)
    err_a_sib = shift(err_a, "c", 1)

    gb = gradient(False, place, mine, theirs, after(err_b, err_a), err_b_sib)
    ga = gradient(True, place, mine, theirs, after(err_a, gb[0]), err_a_sib)
    ga = [ga[0]] + [shift(ga[k], "x", k) for k in (1, 2, 3)]
    squared = after(sq_a + sq_b, gb[0])
    squared = lax.psum(squared + shift(squared, "yl", 1), "z")
    seq_loss = squared.reshape(1) / (lengths.astype(F32) * DT)
    gb = [after(gb[0], seq_loss), shift_y(gb[1], 2), shift_y(gb[2], 1), shift_y(gb[3], -1)]
    a = partial_sums(sum_x_kernel, place, ga)
    a = [a[0], shift_y(a[1], 2), shift_y(a[2], 1), shift_y(a[3], -1)]
    b = partial_sums(sum_y_kernel, place, gb)
    b = [b[0]] + [shift(b[k], "x", k) for k in (1, 2, 3)]
    return last_sum(a + b), seq_loss


def solution(mesh):
    split = Mesh(mesh.devices.reshape(4, 2, 2, 2, 4), AXES)
    dp, tensor = ("x", "yh", "c"), ("yl", "z")
    placed = (
        P(dp + tensor, None),
        P(),
        P(None, tensor),
        P(None, tensor),
        P(None, tensor),
        P(tensor, None),
        P(None, tensor),
        P(dp, tensor),
        P(dp),
    )
    return jax.shard_map(
        shards, mesh=split, in_specs=placed, out_specs=(P(dp, tensor), P(dp)), check_vma=False
    )
```

```python
import functools
import math

import jax
import jax.numpy as jnp
from jax import lax
from jax.experimental import pallas as pl
from jax.experimental.pallas import tpu as pltpu
from jax.sharding import Mesh, PartitionSpec as P

HEAD_DIM = 128
DT = 8192
EPSILON = 1e-05
ROPE_BASE = 500000.0
NEG_LARGE = -1e30
AXES = ("x", "yh", "c", "yl", "z")
SIZES = {"x": 4, "yh": 2, "c": 2, "yl": 2, "z": 4}
F32 = jnp.float32
BF16 = jnp.bfloat16
PARAMS = pltpu.CompilerParams(vmem_limit_bytes=48 * 2**20)


def shift(value, axis, step):
    count = SIZES[axis]
    return lax.ppermute(value, axis, [(i, (i + step) % count) for i in range(count)])


def shift_y(value, step):
    return lax.ppermute(value, ("yh", "yl"), [(i, (i + step) % 4) for i in range(4)])


def after(value, *others):
    return lax.optimization_barrier((value, *others))[0]


def rows_of(array, start, count):
    return lax.dynamic_slice_in_dim(array, start, count, 0)


def pick(array, at, axis):
    return lax.dynamic_index_in_dim(array, at, axis, keepdims=False)


def dot(left, right):
    return jnp.dot(left, right, preferred_element_type=F32)


def norm_kernel(in_ref, gain_ref, out_ref):
    widened = in_ref[...].astype(F32)
    mean_square = jnp.mean(widened * widened, axis=-1, keepdims=True)
    out_ref[...] = (widened * lax.rsqrt(mean_square + EPSILON) * gain_ref[...]).astype(BF16)


def root_norm(inputs, norm_gain):
    return pl.pallas_call(
        norm_kernel,
        grid=(4,),
        in_specs=[
            pl.BlockSpec((32, 4096), lambda i: (i, 0)),
            pl.BlockSpec((1, 4096), lambda i: (0, 0)),
        ],
        out_specs=pl.BlockSpec((32, 4096), lambda i: (i, 0)),
        out_shape=jax.ShapeDtypeStruct((128, 4096), BF16),
        compiler_params=PARAMS,
    )(inputs, norm_gain.reshape(1, 4096))


def ring_step(block):
    return block ^ (block // 2)


def ring_position(index, z):
    return ((z + ring_step(index // 128)) % 4) * 128 + index % 128


def turned(product, cosine, sine, last):
    def turn(head):
        return head * cosine + pltpu.roll(head, 64, 1) * sine

    left, right = product[:, :128], product[:, 128:]
    right = jnp.where(last, right, turn(right))
    return jnp.concatenate([turn(left), right], axis=1).astype(BF16)


def own_heads_kernel(*refs):
    *x_refs, q_ref, kv_ref, cos_ref, sin_ref, out_ref = refs
    x = jnp.concatenate([ref[...] for ref in x_refs if ref.shape[1] == 4096], axis=0)
    last = pl.program_id(0) == 2

    def finish(w_ref):
        out_ref[...] = turned(dot(x, w_ref[...]), cos_ref[...], sin_ref[...], last)

    pl.when(pl.program_id(0) < 2)(lambda: finish(q_ref))
    pl.when(last)(lambda: finish(kv_ref))


def own_heads_of(pieces, w_query, kv_own, cosine, sine, earlier=None):
    rows, at = sum(v.shape[0] for v in pieces), 0 if earlier is None else 3
    turn = pl.BlockSpec((rows, 128), lambda n: (at, 0))
    kept, alias = [], {}
    if earlier is not None:
        kept, alias = [earlier], {0: 0}
    return pl.pallas_call(
        own_heads_kernel,
        grid=(3,),
        in_specs=[pl.BlockSpec(memory_space=pl.ANY)] * len(kept)
        + [pl.BlockSpec(v.shape, lambda n: (0, 0)) for v in pieces]
        + [
            pl.BlockSpec((4096, 256), lambda n: (0, jnp.minimum(n, 1))),
            pl.BlockSpec((4096, 256), lambda n: (0, 0)),
            turn,
            turn,
        ],
        out_specs=pl.BlockSpec((rows, 256), lambda n: (at, n)),
        out_shape=jax.ShapeDtypeStruct((512, 768), BF16),
        input_output_aliases=alias,
        compiler_params=PARAMS,
    )(*kept, *pieces, w_query, kv_own, cosine, sine)


def placed(refs):
    start = 0
    for ref in refs:
        yield slice(start, start + ref.shape[0]), ref
        start += ref.shape[0]


def far_heads_kernel(at_ref, *refs):
    *pieces, w0, w1, w2, w3, cos_ref, sin_ref, out_ref, x_ref = refs
    core = at_ref[3]

    @pl.when(pl.program_id(0) == 0)
    def _():
        for here, ref in placed(pieces):
            for k in range(4):
                source = ((core + k // 2) % 2) * 2048 + (k % 2) * 1024
                x_ref[here, 1024 * k : 1024 * k + 1024] = ref[
                    :, pl.ds(pl.multiple_of(source, 1024), 1024)
                ]

    product = dot(x_ref[:, :1024], w0[...])
    for k, ref in ((1, w1), (2, w2), (3, w3)):
        product = product + dot(x_ref[:, 1024 * k : 1024 * k + 1024], ref[...])
    out_ref[...] = turned(product, cos_ref[...], sin_ref[...], pl.program_id(0) == 2)


def far_heads_of(place, pieces, quarters, cosine, sine):
    whole = [pl.BlockSpec(v.shape, lambda n, at: (0, 0)) for v in pieces]
    weight = pl.BlockSpec((1024, 256), lambda n, at: (0, n))
    turn = pl.BlockSpec((512, 128), lambda n, at: (0, 0))
    return pl.pallas_call(
        far_heads_kernel,
        grid_spec=pltpu.PrefetchScalarGridSpec(
            num_scalar_prefetch=1,
            grid=(3,),
            in_specs=whole + [weight] * 4 + [turn] * 2,
            out_specs=pl.BlockSpec((512, 256), lambda n, at: (0, n)),
            scratch_shapes=[pltpu.VMEM((512, 4096), BF16)],
        ),
        out_shape=jax.ShapeDtypeStruct((512, 768), BF16),
        compiler_params=PARAMS,
    )(place, *pieces, *quarters, cosine, sine)


def attend_kernel(at_ref, q_ref, own_ref, far_ref, out_ref):
    z, yl, length = at_ref[0], at_ref[1], at_ref[2]
    factor = math.log2(math.e) / math.sqrt(HEAD_DIM)
    q = jnp.concatenate([q_ref[:, 128 * h : 128 * h + 128] for h in range(4)], axis=0)
    shape = (512, 512)
    ring = ring_position(lax.broadcasted_iota(jnp.int32, (1, 512), 1), z)
    q_at = ((z + ring_step(pl.program_id(0))) % 4) * 128 + lax.broadcasted_iota(jnp.int32, (512, 1), 0) % 128
    contract = (((1,), (1,)), ((), ()))

    def scores(kv_ref):
        return factor * lax.dot_general(q, kv_ref[:, :128], contract, preferred_element_type=F32)

    own_ok = (ring <= q_at) & (ring + yl * 512 < length)
    own = jnp.where(jnp.broadcast_to(own_ok, shape), scores(own_ref), NEG_LARGE)
    top = jnp.max(own, axis=-1, keepdims=True)

    def store(total, blended):
        blended = (blended / total).astype(BF16)
        for h in range(4):
            out_ref[:, 128 * h : 128 * h + 128] = blended[128 * h : 128 * h + 128]

    @pl.when(yl == 0)
    def _():
        weights = jnp.exp2(own - top)
        store(
            jnp.sum(weights, axis=-1, keepdims=True), dot(weights.astype(BF16), own_ref[:, 128:])
        )

    @pl.when(yl == 1)
    def _():
        far = jnp.where(jnp.broadcast_to(ring < length, shape), scores(far_ref), NEG_LARGE)
        highest = jnp.maximum(top, jnp.max(far, axis=-1, keepdims=True))
        own_weights = jnp.exp2(own - highest)
        far_weights = jnp.exp2(far - highest)
        total = jnp.sum(own_weights, axis=-1, keepdims=True) + jnp.sum(
            far_weights, axis=-1, keepdims=True
        )
        store(
            total,
            dot(own_weights.astype(BF16), own_ref[:, 128:])
            + dot(far_weights.astype(BF16), far_ref[:, 128:]),
        )


def attend(place, heads, far_kv):
    return pl.pallas_call(
        attend_kernel,
        grid_spec=pltpu.PrefetchScalarGridSpec(
            num_scalar_prefetch=1,
            grid=(4,),
            in_specs=[
                pl.BlockSpec((128, 512), lambda j, at: (j, 0)),
                pl.BlockSpec((512, 256), lambda j, at: (0, 2)),
                pl.BlockSpec((512, 256), lambda j, at: (0, 0)),
            ],
            out_specs=pl.BlockSpec((128, 512), lambda j, at: (j, 0)),
        ),
        out_shape=jax.ShapeDtypeStruct((512, 512), BF16),
        compiler_params=PARAMS,
    )(place, heads, heads, far_kv)


def layer_kernel(at_ref, student_ref, *refs):
    *parts, out_ref = refs
    total = parts[0][...].astype(F32)
    for part in parts[1:]:
        total = total + part[...].astype(F32)
    layer = (student_ref[...].astype(F32) + total).astype(BF16)
    even = [layer[:, 512 * i : 512 * i + 256] for i in range(8)]
    odd = [layer[:, 512 * i + 256 : 512 * i + 512] for i in range(8)]

    @pl.when(at_ref[3] == 0)
    def _():
        out_ref[...] = jnp.concatenate(even + odd, axis=1)

    @pl.when(at_ref[3] == 1)
    def _():
        out_ref[...] = jnp.concatenate(odd + even, axis=1)


def make_layer(place, student_in, parts):
    spec = pl.BlockSpec((32, 4096), lambda i, at: (i, 0))
    return pl.pallas_call(
        layer_kernel,
        grid_spec=pltpu.PrefetchScalarGridSpec(
            num_scalar_prefetch=1, grid=(4,), in_specs=[spec] * 5, out_specs=spec
        ),
        out_shape=jax.ShapeDtypeStruct((128, 4096), BF16),
        compiler_params=PARAMS,
    )(place, student_in, *parts)


def out_kernel(at_ref, own, far, w, w0, w1, w2, w3, *refs):
    *out_refs, x_ref = refs

    @pl.when(pl.program_id(0) == 0)
    def _():
        x_ref[:, :512] = own[...]
        for k in range(2):
            source = ((at_ref[3] + k) % 2) * 256
            x_ref[:, 512 + 256 * k : 768 + 256 * k] = far[:, pl.ds(pl.multiple_of(source, 256), 256)]

    weights = jnp.concatenate([ref[...] for ref in (w, w0, w1, w2, w3)], axis=0)
    total = dot(x_ref[...], weights)
    for j, ref in enumerate(out_refs):
        ref[...] = total[128 * j : 128 * j + 128].astype(BF16)


def out_blocks(place, own, far, w_out, quarters):
    att = pl.BlockSpec((512, 512), lambda n, at: (0, 0))
    quarter = pl.BlockSpec((128, 1024), lambda n, at: (0, n))
    return pl.pallas_call(
        out_kernel,
        grid_spec=pltpu.PrefetchScalarGridSpec(
            num_scalar_prefetch=1,
            grid=(4,),
            in_specs=[att, att, pl.BlockSpec((512, 1024), lambda n, at: (0, n))] + [quarter] * 4,
            out_specs=[quarter] * 4,
            scratch_shapes=[pltpu.VMEM((512, 1024), BF16)],
        ),
        out_shape=[jax.ShapeDtypeStruct((128, 4096), BF16)] * 4,
        compiler_params=PARAMS,
    )(place, own, far, w_out, *quarters)


def error_kernel(first, rows, kept, at_ref, *refs):
    layers = refs[kept:-11] if rows < 512 else refs[:2]
    p_own, f0, f1, t_own, t_far, err_ref, sum_ref = refs[len(layers) + kept :][:7]
    x_ref, n_ref = refs[-2:]
    step = pl.program_id(0)
    z, yl, length, core = at_ref[0], at_ref[1], at_ref[2], at_ref[3]

    @pl.when(step == 0)
    def _():
        if rows == 512:
            x_ref[:, :2048] = layers[0][...]
            x_ref[:, 2048:] = layers[1][...]
        else:
            for here, ref in placed(layers):
                x_ref[here, :] = ref[...]
            refs[-4][...] = x_ref[:, :2048]
            refs[-3][...] = x_ref[:, 2048:]
        for i in range(16):
            block = i // 2 + 8 * ((core + i) % 2)
            n_ref[:, 256 * i : 256 * i + 256] = x_ref[
                :, pl.ds(pl.multiple_of(block * 256, 256), 256)
            ]
        sum_ref[...] = refs[3][...] if kept else jnp.zeros((1, 1), F32)

    index = 128 * first + lax.broadcasted_iota(jnp.int32, (rows, 1), 0)
    pos = yl * 512 + ring_position(index, z)
    live = jnp.broadcast_to(pos < length, (rows, 256))

    def part(columns, predicted, t_ref):
        teacher = [
            t_ref[pl.ds(pl.multiple_of(((z + ring_step(first + j)) % 4) * 128, 128), 128), :]
            for j in range(rows // 128)
        ]
        residue = predicted - jnp.concatenate(teacher, axis=0).astype(F32)
        residue = jnp.where(live, residue, 0.0)
        err_ref[:, columns] = (residue / length.astype(F32)).astype(BF16)
        sum_ref[...] += jnp.sum(residue * residue).reshape(1, 1)

    part(slice(0, 256), dot(n_ref[...], p_own[...]), t_own)
    part(
        slice(256, 512),
        dot(x_ref[:, :2048], f0[...]) + dot(x_ref[:, 2048:], f1[...]),
        t_far,
    )


def errors(half, place, layers, projection, p_far, t_own, t_far, earlier=()):
    rows = 512 if layers[0].shape[0] == 512 else sum(v.shape[0] for v in layers)
    first, kept = (3, 4) if earlier else (0, 0)

    def columns(n, at):
        return (0, 2 * half + n)

    def own_rows(n, at):
        return (at[1], 2 * half + n)

    def constant(n, at):
        return (0, 0)

    anywhere = pl.BlockSpec(memory_space=pl.ANY)
    kept_specs = [anywhere] * 3 + [pl.BlockSpec((1, 1), constant)] if earlier else []
    out_specs = [
        pl.BlockSpec((rows, 512), lambda n, at: (first, n)),
        pl.BlockSpec((1, 1), constant),
    ]
    out_shape = [
        jax.ShapeDtypeStruct((512, 1024), BF16),
        jax.ShapeDtypeStruct((1, 1), F32),
    ]
    if rows < 512:
        out_specs += [pl.BlockSpec((rows, 2048), lambda n, at: (first, 0))] * 2
        out_shape += [jax.ShapeDtypeStruct((512, 2048), BF16)] * 2
    if earlier:
        err, total, left, right = earlier
        earlier = (err, left, right, total)
    return pl.pallas_call(
        functools.partial(error_kernel, first, rows, kept),
        grid_spec=pltpu.PrefetchScalarGridSpec(
            num_scalar_prefetch=1,
            grid=(2,),
            in_specs=kept_specs
            + [pl.BlockSpec(v.shape, constant) for v in layers]
            + [pl.BlockSpec((4096, 256), columns)]
            + [pl.BlockSpec((2048, 256), columns)] * 2
            + [pl.BlockSpec((512, 256), own_rows), pl.BlockSpec((512, 256), columns)],
            out_specs=out_specs,
            scratch_shapes=[pltpu.VMEM((rows, 4096), BF16)] * 2,
        ),
        out_shape=out_shape,
        input_output_aliases={1: 0, 2: 2, 3: 3} if earlier else {},
        compiler_params=PARAMS,
    )(place, *earlier, *layers, projection, *p_far, t_own, t_far)


def split_columns(product):
    own = jnp.concatenate([product[:, :256], product[:, 512:768]], axis=1)
    far = jnp.concatenate([product[:, 256:512], product[:, 768:]], axis=1)
    return own, far


def by_y(at_ref, own, far, store):
    for t in (0, 1):
        this, that = slice(256 * t, 256 * t + 256), slice(256 - 256 * t, 512 - 256 * t)

        @pl.when(at_ref[5] == t)
        def _():
            store(0, own[this])
            store(1, own[that])

        @pl.when(at_ref[6] == t)
        def _():
            store(2, far[this])
            store(3, far[that])


def gradient_kernel(by_x, at_ref, mine, theirs, e_mine, e_theirs, *out_refs):
    contract = (((0,), (0,)), ((), ()))
    product = lax.dot_general(mine[...], e_mine[...], contract, preferred_element_type=F32)
    product = product + lax.dot_general(
        theirs[...], e_theirs[...], contract, preferred_element_type=F32
    )
    product = product.astype(BF16)
    if by_x:
        for k, ref in enumerate(out_refs):

            @pl.when(pl.program_id(0) == k)
            def _():
                ref[...] = product
    else:

        def store(k, value):
            out_refs[k][0] = value

        by_y(at_ref, *split_columns(product), store)


def gradient(by_x, place, mine, theirs, e_mine, e_theirs):
    rows = pl.BlockSpec((512, 512), lambda k, at: (0, (at[4] + k) % 4))
    error = pl.BlockSpec((512, 1024), lambda k, at: (0, 0))
    if by_x:
        out_spec = pl.BlockSpec((512, 1024), lambda k, at: (0, 0))
        shape = (512, 1024)
    else:
        out_spec = pl.BlockSpec((1, 256, 512), lambda k, at: (k, 0, 0))
        shape = (4, 256, 512)
    return pl.pallas_call(
        functools.partial(gradient_kernel, by_x),
        grid_spec=pltpu.PrefetchScalarGridSpec(
            num_scalar_prefetch=1,
            grid=(4,),
            in_specs=[rows, rows, error, error],
            out_specs=[out_spec] * 4,
        ),
        out_shape=[jax.ShapeDtypeStruct(shape, BF16)] * 4,
        compiler_params=PARAMS,
    )(place, mine, theirs, e_mine, e_theirs)


def total_of(refs):
    total = refs[0][...].astype(F32)
    for ref in refs[1:]:
        total = total + ref[...].astype(F32)
    return total


def sum_x_kernel(at_ref, *refs):
    def store(k, value):
        refs[4 + k][...] = value

    by_y(at_ref, *split_columns(total_of(refs[:4]).astype(BF16)), store)


def sum_y_kernel(at_ref, *refs):
    total = total_of(refs[:4]).astype(BF16)
    for k in range(4):
        refs[4 + k][...] = total[k]


def partial_sums(kernel, place, arrays):
    return pl.pallas_call(
        kernel,
        grid_spec=pltpu.PrefetchScalarGridSpec(
            num_scalar_prefetch=1,
            grid=(1,),
            in_specs=[pl.BlockSpec(memory_space=pltpu.VMEM)] * 4,
            out_specs=[pl.BlockSpec(memory_space=pltpu.VMEM)] * 4,
        ),
        out_shape=[jax.ShapeDtypeStruct((256, 512), BF16)] * 4,
        compiler_params=PARAMS,
    )(place, *arrays)


def last_kernel(*refs):
    refs[8][:, :512] = total_of(refs[:4])
    refs[8][:, 512:] = total_of(refs[4:8])


def last_sum(arrays):
    return pl.pallas_call(
        last_kernel,
        out_shape=jax.ShapeDtypeStruct((256, 1024), F32),
        compiler_params=PARAMS,
    )(*arrays)


def fetch(plus, minus):
    return shift_y(plus, 1), shift_y(minus, -1)


def swap(pair):
    return tuple(shift(v, "c", 1) for v in pair)


def shards(
    student_in, norm_gain, w_query, w_key, w_value, w_out, projection, teacher_rows, lengths
):
    x, yh, c, yl, z = (lax.axis_index(a) for a in AXES)
    length = lengths[0]
    to_up = jnp.where(yl == 0, yh, 1 - yh)
    place = jnp.stack([z, yl, length, c, x, yh, to_up])

    def around(own):
        near, back = shift(own, "z", -1), shift(own, "z", 1)
        return [own, near, back], [shift(back[:64], "z", 1), shift(near[64:], "z", -1)]

    kv_own = jnp.concatenate([w_key, w_value], axis=1)

    def quarter(at):
        return jnp.concatenate([rows_of(w, at, 1024) for w in (w_query, w_key, w_value)], axis=1)

    quarters = quarter(c * 2048), quarter(c * 2048 + 1024)
    first = fetch(*quarters)
    pieces, ends = around(root_norm(after(student_in, *quarters), norm_gain))
    first = tuple(after(v, *pieces[1:]) for v in first)
    first_sib = swap(first)

    inverse = ROPE_BASE ** (-2.0 * jnp.arange(HEAD_DIM // 2).astype(F32) / HEAD_DIM)
    pos = yl * 512 + ring_position(jnp.arange(512), z)
    angles = pos.astype(F32)[:, None] * inverse
    cosine, sine = jnp.cos(angles), jnp.sin(angles)
    cosine = jnp.concatenate([cosine, cosine], axis=1)
    sine = jnp.concatenate([-sine, sine], axis=1)

    near_heads = own_heads_of([after(v, *first) for v in pieces], w_query, kv_own, cosine, sine)
    ends = [after(v, near_heads) for v in ends]
    out_part = after(rows_of(w_out, c * 256, 256), *ends)
    second = fetch(out_part[:128], out_part[128:])
    own_heads = own_heads_of(ends, w_query, kv_own, cosine, sine, near_heads)
    kv_early = shift(own_heads[:, 512:], "yl", 1)
    far_weights = [*first, *(after(v, own_heads) for v in first_sib)]
    far_heads = far_heads_of(place, pieces + ends, far_weights, cosine, sine)
    kv_late = shift(far_heads[:, 512:], "yl", 1)
    att_far = attend(place, far_heads, kv_early)
    second = tuple(after(v, att_far) for v in second)
    second_sib = swap(second)
    kv_late = after(kv_late, att_far)
    att_own = attend(place, own_heads, kv_late)
    b0, b1, b2, b3 = out_blocks(place, att_own, att_far, w_out, [*second, *second_sib])

    proj_c = pick(projection.reshape(8, 2, 256, 1024), c, 1).reshape(2048, 1024)
    sends = lax.optimization_barrier((proj_c[:1024], proj_c[1024:], ends[0]))[:2]
    third = fetch(*(after(v, kv_late, *second) for v in sends))

    parts = [b0, shift(b3, "z", 2), shift(b1, "z", 1), shift(b2, "z", -1)]
    third_up, third_down, *parts = lax.optimization_barrier((*third, *parts))
    own_layer = make_layer(place, student_in, parts)
    teach_far = shift(after(rows_of(teacher_rows, (1 - yl) * 512, 512), own_layer), "yl", 1)
    layers, ends = around(own_layer)
    third = jnp.concatenate([third_up, third_down], axis=0)
    p_far = [third, shift(third, "c", 1)]
    same = (projection, p_far, teacher_rows, teach_far)
    near = errors(1, place, layers, *same)
    ends = [after(v, near[0]) for v in ends]
    err_b, sq_b, mine, other = errors(1, place, ends, *same, earlier=near)
    theirs = shift(other, "c", 1)
    err_b_sib = shift(err_b, "c", 1)
    err_a, sq_a = errors(0, place, [mine, after(other, err_b)], *same)
    err_a_sib = shift(err_a, "c", 1)

    gb = gradient(False, place, mine, theirs, after(err_b, err_a), err_b_sib)
    squared = sq_a + sq_b
    squared = squared + shift(squared, "yl", 1)
    ga = gradient(True, place, mine, theirs, after(err_a, gb[0], squared), err_a_sib)
    ga = [ga[0]] + [shift(ga[k], "x", k) for k in (1, 2, 3)]
    squared = lax.psum(squared, "z")
    seq_loss = squared.reshape(1) / (lengths.astype(F32) * DT)
    ga[0] = after(ga[0], seq_loss)
    gb = [gb[0], shift_y(gb[1], 2), shift_y(gb[2], 1), shift_y(gb[3], -1)]
    a = partial_sums(sum_x_kernel, place, ga)
    a = [a[0], shift_y(a[1], 2), shift_y(a[2], 1), shift_y(a[3], -1)]
    b = partial_sums(sum_y_kernel, place, gb)
    b = [b[0]] + [shift(b[k], "x", k) for k in (1, 2, 3)]
    return last_sum(a + b), seq_loss


def solution(mesh):
    split = Mesh(mesh.devices.reshape(4, 2, 2, 2, 4), AXES)
    dp, tensor = ("x", "yh", "c"), ("yl", "z")
    placed = (
        P(dp + tensor, None),
        P(),
        P(None, tensor),
        P(None, tensor),
        P(None, tensor),
        P(tensor, None),
        P(None, tensor),
        P(dp, tensor),
        P(dp),
    )
    return jax.shard_map(
        shards, mesh=split, in_specs=placed, out_specs=(P(dp, tensor), P(dp)), check_vma=False
    )
```

```python
import functools
import math

import jax
import jax.numpy as jnp
from jax import lax
from jax.experimental import pallas as pl
from jax.experimental.pallas import tpu as pltpu
from jax.sharding import Mesh, PartitionSpec as P

HEAD_DIM = 128
DT = 8192
EPSILON = 1e-05
ROPE_BASE = 500000.0
NEG_LARGE = -1e30
AXES = ("x", "yh", "c", "yl", "z")
SIZES = {"x": 4, "yh": 2, "c": 2, "yl": 2, "z": 4}
F32 = jnp.float32
BF16 = jnp.bfloat16
PARAMS = pltpu.CompilerParams(vmem_limit_bytes=48 * 2**20)


def shift(value, axis, step):
    count = SIZES[axis]
    return lax.ppermute(value, axis, [(i, (i + step) % count) for i in range(count)])


def shift_y(value, step):
    return lax.ppermute(value, ("yh", "yl"), [(i, (i + step) % 4) for i in range(4)])


def after(value, *others):
    return lax.optimization_barrier((value, *others))[0]


def rows_of(array, start, count):
    return lax.dynamic_slice_in_dim(array, start, count, 0)


def pick(array, at, axis):
    return lax.dynamic_index_in_dim(array, at, axis, keepdims=False)


def dot(left, right):
    return jnp.dot(left, right, preferred_element_type=F32)


def norm_kernel(in_ref, gain_ref, out_ref):
    widened = in_ref[...].astype(F32)
    mean_square = jnp.mean(widened * widened, axis=-1, keepdims=True)
    out_ref[...] = (widened * lax.rsqrt(mean_square + EPSILON) * gain_ref[...]).astype(BF16)


def root_norm(inputs, norm_gain):
    return pl.pallas_call(
        norm_kernel,
        grid=(4,),
        in_specs=[
            pl.BlockSpec((32, 4096), lambda i: (i, 0)),
            pl.BlockSpec((1, 4096), lambda i: (0, 0)),
        ],
        out_specs=pl.BlockSpec((32, 4096), lambda i: (i, 0)),
        out_shape=jax.ShapeDtypeStruct((128, 4096), BF16),
        compiler_params=PARAMS,
    )(inputs, norm_gain.reshape(1, 4096))


def ring_step(block):
    return block ^ (block // 2)


def ring_position(index, z):
    return ((z + ring_step(index // 128)) % 4) * 128 + index % 128


def turned(product, cosine, sine, last):
    def turn(head):
        return head * cosine + pltpu.roll(head, 64, 1) * sine

    left, right = product[:, :128], product[:, 128:]
    right = jnp.where(last, right, turn(right))
    return jnp.concatenate([turn(left), right], axis=1).astype(BF16)


def own_heads_kernel(*refs):
    *x_refs, q_ref, kv_ref, cos_ref, sin_ref, out_ref = refs
    x = jnp.concatenate([ref[...] for ref in x_refs if ref.shape[1] == 4096], axis=0)
    last = pl.program_id(0) == 2

    def finish(w_ref):
        out_ref[...] = turned(dot(x, w_ref[...]), cos_ref[...], sin_ref[...], last)

    pl.when(pl.program_id(0) < 2)(lambda: finish(q_ref))
    pl.when(last)(lambda: finish(kv_ref))


def own_heads_of(pieces, w_query, kv_own, cosine, sine, earlier=None):
    rows, at = sum(v.shape[0] for v in pieces), 0 if earlier is None else 3
    turn = pl.BlockSpec((rows, 128), lambda n: (at, 0))
    kept, alias = [], {}
    if earlier is not None:
        kept, alias = [earlier], {0: 0}
    return pl.pallas_call(
        own_heads_kernel,
        grid=(3,),
        in_specs=[pl.BlockSpec(memory_space=pl.ANY)] * len(kept)
        + [pl.BlockSpec(v.shape, lambda n: (0, 0)) for v in pieces]
        + [
            pl.BlockSpec((4096, 256), lambda n: (0, jnp.minimum(n, 1))),
            pl.BlockSpec((4096, 256), lambda n: (0, 0)),
            turn,
            turn,
        ],
        out_specs=pl.BlockSpec((rows, 256), lambda n: (at, n)),
        out_shape=jax.ShapeDtypeStruct((512, 768), BF16),
        input_output_aliases=alias,
        compiler_params=PARAMS,
    )(*kept, *pieces, w_query, kv_own, cosine, sine)


def placed(refs):
    start = 0
    for ref in refs:
        yield slice(start, start + ref.shape[0]), ref
        start += ref.shape[0]


def far_heads_kernel(at_ref, *refs):
    *pieces, w0, w1, w2, w3, cos_ref, sin_ref, out_ref, x_ref = refs
    core = at_ref[3]

    @pl.when(pl.program_id(0) == 0)
    def _():
        for here, ref in placed(pieces):
            for k in range(4):
                source = ((core + k // 2) % 2) * 2048 + (k % 2) * 1024
                x_ref[here, 1024 * k : 1024 * k + 1024] = ref[
                    :, pl.ds(pl.multiple_of(source, 1024), 1024)
                ]

    product = dot(x_ref[:, :1024], w0[...])
    for k, ref in ((1, w1), (2, w2), (3, w3)):
        product = product + dot(x_ref[:, 1024 * k : 1024 * k + 1024], ref[...])
    out_ref[...] = turned(product, cos_ref[...], sin_ref[...], pl.program_id(0) == 2)


def far_heads_of(place, pieces, quarters, cosine, sine):
    whole = [pl.BlockSpec(v.shape, lambda n, at: (0, 0)) for v in pieces]
    weight = pl.BlockSpec((1024, 256), lambda n, at: (0, n))
    turn = pl.BlockSpec((512, 128), lambda n, at: (0, 0))
    return pl.pallas_call(
        far_heads_kernel,
        grid_spec=pltpu.PrefetchScalarGridSpec(
            num_scalar_prefetch=1,
            grid=(3,),
            in_specs=whole + [weight] * 4 + [turn] * 2,
            out_specs=pl.BlockSpec((512, 256), lambda n, at: (0, n)),
            scratch_shapes=[pltpu.VMEM((512, 4096), BF16)],
        ),
        out_shape=jax.ShapeDtypeStruct((512, 768), BF16),
        compiler_params=PARAMS,
    )(place, *pieces, *quarters, cosine, sine)


def attend_kernel(at_ref, q_ref, own_ref, far_ref, out_ref):
    z, yl, length = at_ref[0], at_ref[1], at_ref[2]
    factor = math.log2(math.e) / math.sqrt(HEAD_DIM)
    q = jnp.concatenate([q_ref[:, 128 * h : 128 * h + 128] for h in range(4)], axis=0)
    shape = (512, 512)
    ring = ring_position(lax.broadcasted_iota(jnp.int32, (1, 512), 1), z)
    q_at = ((z + ring_step(pl.program_id(0))) % 4) * 128 + lax.broadcasted_iota(jnp.int32, (512, 1), 0) % 128
    contract = (((1,), (1,)), ((), ()))

    def scores(kv_ref):
        return factor * lax.dot_general(q, kv_ref[:, :128], contract, preferred_element_type=F32)

    own_ok = (ring <= q_at) & (ring + yl * 512 < length)
    own = jnp.where(jnp.broadcast_to(own_ok, shape), scores(own_ref), NEG_LARGE)
    top = jnp.max(own, axis=-1, keepdims=True)

    def store(total, blended):
        blended = (blended / total).astype(BF16)
        for h in range(4):
            out_ref[:, 128 * h : 128 * h + 128] = blended[128 * h : 128 * h + 128]

    @pl.when(yl == 0)
    def _():
        weights = jnp.exp2(own - top)
        store(
            jnp.sum(weights, axis=-1, keepdims=True), dot(weights.astype(BF16), own_ref[:, 128:])
        )

    @pl.when(yl == 1)
    def _():
        far = jnp.where(jnp.broadcast_to(ring < length, shape), scores(far_ref), NEG_LARGE)
        highest = jnp.maximum(top, jnp.max(far, axis=-1, keepdims=True))
        own_weights = jnp.exp2(own - highest)
        far_weights = jnp.exp2(far - highest)
        total = jnp.sum(own_weights, axis=-1, keepdims=True) + jnp.sum(
            far_weights, axis=-1, keepdims=True
        )
        store(
            total,
            dot(own_weights.astype(BF16), own_ref[:, 128:])
            + dot(far_weights.astype(BF16), far_ref[:, 128:]),
        )


def attend(place, heads, far_kv):
    return pl.pallas_call(
        attend_kernel,
        grid_spec=pltpu.PrefetchScalarGridSpec(
            num_scalar_prefetch=1,
            grid=(4,),
            in_specs=[
                pl.BlockSpec((128, 512), lambda j, at: (j, 0)),
                pl.BlockSpec((512, 256), lambda j, at: (0, 2)),
                pl.BlockSpec((512, 256), lambda j, at: (0, 0)),
            ],
            out_specs=pl.BlockSpec((128, 512), lambda j, at: (j, 0)),
        ),
        out_shape=jax.ShapeDtypeStruct((512, 512), BF16),
        compiler_params=PARAMS,
    )(place, heads, heads, far_kv)


def layer_kernel(at_ref, student_ref, *refs):
    *parts, out_ref = refs
    total = parts[0][...].astype(F32)
    for part in parts[1:]:
        total = total + part[...].astype(F32)
    layer = (student_ref[...].astype(F32) + total).astype(BF16)
    even = [layer[:, 512 * i : 512 * i + 256] for i in range(8)]
    odd = [layer[:, 512 * i + 256 : 512 * i + 512] for i in range(8)]

    @pl.when(at_ref[3] == 0)
    def _():
        out_ref[...] = jnp.concatenate(even + odd, axis=1)

    @pl.when(at_ref[3] == 1)
    def _():
        out_ref[...] = jnp.concatenate(odd + even, axis=1)


def make_layer(place, student_in, parts):
    spec = pl.BlockSpec((32, 4096), lambda i, at: (i, 0))
    return pl.pallas_call(
        layer_kernel,
        grid_spec=pltpu.PrefetchScalarGridSpec(
            num_scalar_prefetch=1, grid=(4,), in_specs=[spec] * 5, out_specs=spec
        ),
        out_shape=jax.ShapeDtypeStruct((128, 4096), BF16),
        compiler_params=PARAMS,
    )(place, student_in, *parts)


def out_kernel(own, far, w_own, w_far, *refs):
    *out_refs, x_ref = refs

    @pl.when(pl.program_id(0) == 0)
    def _():
        x_ref[:, :512] = own[...]
        x_ref[:, 512:] = far[...]

    total = dot(x_ref[...], jnp.concatenate([w_own[...], w_far[...]], axis=0))
    for j, ref in enumerate(out_refs):
        ref[...] = total[128 * j : 128 * j + 128].astype(BF16)


def out_blocks(own, far, w_own, w_far):
    att = pl.BlockSpec((512, 512), lambda n: (0, 0))
    weight = pl.BlockSpec((512, 1024), lambda n: (0, n))
    return pl.pallas_call(
        out_kernel,
        grid=(4,),
        in_specs=[att, att, weight, weight],
        out_specs=[pl.BlockSpec((128, 1024), lambda n: (0, n))] * 4,
        out_shape=[jax.ShapeDtypeStruct((128, 4096), BF16)] * 4,
        scratch_shapes=[pltpu.VMEM((512, 1024), BF16)],
        compiler_params=PARAMS,
    )(own, far, w_own, w_far)


def error_kernel(first, rows, kept, at_ref, *refs):
    layers = refs[kept:-11] if rows < 512 else refs[:2]
    p_own, f0, f1, t_own, t_far, err_ref, sum_ref = refs[len(layers) + kept :][:7]
    x_ref, n_ref = refs[-2:]
    step = pl.program_id(0)
    z, yl, length, core = at_ref[0], at_ref[1], at_ref[2], at_ref[3]

    @pl.when(step == 0)
    def _():
        if rows == 512:
            x_ref[:, :2048] = layers[0][...]
            x_ref[:, 2048:] = layers[1][...]
        else:
            for here, ref in placed(layers):
                x_ref[here, :] = ref[...]
            refs[-4][...] = x_ref[:, :2048]
            refs[-3][...] = x_ref[:, 2048:]
        for i in range(16):
            block = i // 2 + 8 * ((core + i) % 2)
            n_ref[:, 256 * i : 256 * i + 256] = x_ref[
                :, pl.ds(pl.multiple_of(block * 256, 256), 256)
            ]
        sum_ref[...] = refs[3][...] if kept else jnp.zeros((1, 1), F32)

    index = 128 * first + lax.broadcasted_iota(jnp.int32, (rows, 1), 0)
    pos = yl * 512 + ring_position(index, z)
    live = jnp.broadcast_to(pos < length, (rows, 256))

    def part(columns, predicted, t_ref):
        teacher = [
            t_ref[pl.ds(pl.multiple_of(((z + ring_step(first + j)) % 4) * 128, 128), 128), :]
            for j in range(rows // 128)
        ]
        residue = predicted - jnp.concatenate(teacher, axis=0).astype(F32)
        residue = jnp.where(live, residue, 0.0)
        err_ref[:, columns] = (residue / length.astype(F32)).astype(BF16)
        sum_ref[...] += jnp.sum(residue * residue).reshape(1, 1)

    part(slice(0, 256), dot(n_ref[...], p_own[...]), t_own)
    part(
        slice(256, 512),
        dot(x_ref[:, :2048], f0[...]) + dot(x_ref[:, 2048:], f1[...]),
        t_far,
    )


def errors(half, place, layers, projection, p_far, t_own, t_far, earlier=()):
    rows = 512 if layers[0].shape[0] == 512 else sum(v.shape[0] for v in layers)
    first, kept = (3, 4) if earlier else (0, 0)

    def columns(n, at):
        return (0, 2 * half + n)

    def own_rows(n, at):
        return (at[1], 2 * half + n)

    def constant(n, at):
        return (0, 0)

    anywhere = pl.BlockSpec(memory_space=pl.ANY)
    kept_specs = [anywhere] * 3 + [pl.BlockSpec((1, 1), constant)] if earlier else []
    out_specs = [
        pl.BlockSpec((rows, 512), lambda n, at: (first, n)),
        pl.BlockSpec((1, 1), constant),
    ]
    out_shape = [
        jax.ShapeDtypeStruct((512, 1024), BF16),
        jax.ShapeDtypeStruct((1, 1), F32),
    ]
    if rows < 512:
        out_specs += [pl.BlockSpec((rows, 2048), lambda n, at: (first, 0))] * 2
        out_shape += [jax.ShapeDtypeStruct((512, 2048), BF16)] * 2
    if earlier:
        err, total, left, right = earlier
        earlier = (err, left, right, total)
    return pl.pallas_call(
        functools.partial(error_kernel, first, rows, kept),
        grid_spec=pltpu.PrefetchScalarGridSpec(
            num_scalar_prefetch=1,
            grid=(2,),
            in_specs=kept_specs
            + [pl.BlockSpec(v.shape, constant) for v in layers]
            + [pl.BlockSpec((4096, 256), columns)]
            + [pl.BlockSpec((2048, 256), columns)] * 2
            + [pl.BlockSpec((512, 256), own_rows), pl.BlockSpec((512, 256), columns)],
            out_specs=out_specs,
            scratch_shapes=[pltpu.VMEM((rows, 4096), BF16)] * 2,
        ),
        out_shape=out_shape,
        input_output_aliases={1: 0, 2: 2, 3: 3} if earlier else {},
        compiler_params=PARAMS,
    )(place, *earlier, *layers, projection, *p_far, t_own, t_far)


def split_columns(product):
    own = jnp.concatenate([product[:, :256], product[:, 512:768]], axis=1)
    far = jnp.concatenate([product[:, 256:512], product[:, 768:]], axis=1)
    return own, far


def by_y(at_ref, own, far, store):
    for t in (0, 1):
        this, that = slice(256 * t, 256 * t + 256), slice(256 - 256 * t, 512 - 256 * t)

        @pl.when(at_ref[5] == t)
        def _():
            store(0, own[this])
            store(1, own[that])

        @pl.when(at_ref[6] == t)
        def _():
            store(2, far[this])
            store(3, far[that])


def gradient_kernel(by_x, at_ref, mine, theirs, e_mine, e_theirs, *out_refs):
    contract = (((0,), (0,)), ((), ()))
    product = lax.dot_general(mine[...], e_mine[...], contract, preferred_element_type=F32)
    product = product + lax.dot_general(
        theirs[...], e_theirs[...], contract, preferred_element_type=F32
    )
    product = product.astype(BF16)
    if by_x:
        for k, ref in enumerate(out_refs):

            @pl.when(pl.program_id(0) == k)
            def _():
                ref[...] = product
    else:

        def store(k, value):
            out_refs[k][0] = value

        by_y(at_ref, *split_columns(product), store)


def gradient(by_x, place, mine, theirs, e_mine, e_theirs):
    rows = pl.BlockSpec((512, 512), lambda k, at: (0, (at[4] + k) % 4))
    error = pl.BlockSpec((512, 1024), lambda k, at: (0, 0))
    if by_x:
        out_spec = pl.BlockSpec((512, 1024), lambda k, at: (0, 0))
        shape = (512, 1024)
    else:
        out_spec = pl.BlockSpec((1, 256, 512), lambda k, at: (k, 0, 0))
        shape = (4, 256, 512)
    return pl.pallas_call(
        functools.partial(gradient_kernel, by_x),
        grid_spec=pltpu.PrefetchScalarGridSpec(
            num_scalar_prefetch=1,
            grid=(4,),
            in_specs=[rows, rows, error, error],
            out_specs=[out_spec] * 4,
        ),
        out_shape=[jax.ShapeDtypeStruct(shape, BF16)] * 4,
        compiler_params=PARAMS,
    )(place, mine, theirs, e_mine, e_theirs)


def total_of(refs):
    total = refs[0][...].astype(F32)
    for ref in refs[1:]:
        total = total + ref[...].astype(F32)
    return total


def sum_x_kernel(at_ref, *refs):
    def store(k, value):
        refs[4 + k][...] = value

    by_y(at_ref, *split_columns(total_of(refs[:4]).astype(BF16)), store)


def sum_y_kernel(at_ref, *refs):
    total = total_of(refs[:4]).astype(BF16)
    for k in range(4):
        refs[4 + k][...] = total[k]


def partial_sums(kernel, place, arrays):
    return pl.pallas_call(
        kernel,
        grid_spec=pltpu.PrefetchScalarGridSpec(
            num_scalar_prefetch=1,
            grid=(1,),
            in_specs=[pl.BlockSpec(memory_space=pltpu.VMEM)] * 4,
            out_specs=[pl.BlockSpec(memory_space=pltpu.VMEM)] * 4,
        ),
        out_shape=[jax.ShapeDtypeStruct((256, 512), BF16)] * 4,
        compiler_params=PARAMS,
    )(place, *arrays)


def last_kernel(*refs):
    refs[8][:, :512] = total_of(refs[:4])
    refs[8][:, 512:] = total_of(refs[4:8])


def last_sum(arrays):
    return pl.pallas_call(
        last_kernel,
        out_shape=jax.ShapeDtypeStruct((256, 1024), F32),
        compiler_params=PARAMS,
    )(*arrays)


def fetch(plus, minus):
    return shift_y(plus, 1), shift_y(minus, -1)


def swap(pair):
    return tuple(shift(v, "c", 1) for v in pair)


def shards(
    student_in, norm_gain, w_query, w_key, w_value, w_out, projection, teacher_rows, lengths
):
    x, yh, c, yl, z = (lax.axis_index(a) for a in AXES)
    length = lengths[0]
    to_up = jnp.where(yl == 0, yh, 1 - yh)
    place = jnp.stack([z, yl, length, c, x, yh, to_up])

    def around(own):
        near, back = shift(own, "z", -1), shift(own, "z", 1)
        return [own, near, back], [shift(back[:64], "z", 1), shift(near[64:], "z", -1)]

    kv_own = jnp.concatenate([w_key, w_value], axis=1)

    def quarter(at):
        return jnp.concatenate([rows_of(w, at, 1024) for w in (w_query, w_key, w_value)], axis=1)

    out_part = shift(rows_of(w_out, (2 * x + c) * 64, 64), "yl", 1)
    out_far = lax.all_gather(out_part, ("x", "c"), axis=0, tiled=True)
    quarters = quarter(c * 2048), quarter(c * 2048 + 1024)
    first = fetch(*quarters)
    inverse = ROPE_BASE ** (-2.0 * jnp.arange(HEAD_DIM // 2).astype(F32) / HEAD_DIM)
    pos = yl * 512 + ring_position(jnp.arange(512), z)
    angles = pos.astype(F32)[:, None] * inverse
    cosine, sine = jnp.cos(angles), jnp.sin(angles)
    cosine = jnp.concatenate([cosine, cosine], axis=1)
    sine = jnp.concatenate([-sine, sine], axis=1)
    pieces, ends = around(root_norm(after(student_in, *quarters), norm_gain))
    pieces = list(lax.optimization_barrier((*pieces, cosine, sine, kv_own))[:3])
    near_heads = own_heads_of(pieces, w_query, kv_own, cosine, sine)
    first = tuple(after(v, *ends, near_heads, out_part) for v in first)
    first_sib = swap(first)
    ends = [after(v, near_heads) for v in ends]
    own_heads = own_heads_of(ends, w_query, kv_own, cosine, sine, near_heads)
    kv_early = shift(own_heads[:, 512:], "yl", 1)
    far_weights = [*first, *(after(v, own_heads) for v in first_sib)]
    far_heads = far_heads_of(place, pieces + ends, far_weights, cosine, sine)
    kv_late = shift(far_heads[:, 512:], "yl", 1)
    att_far = attend(place, far_heads, kv_early)
    kv_late = after(kv_late, att_far)
    att_own = attend(place, own_heads, kv_late)
    b0, b1, b2, b3 = out_blocks(att_own, att_far, w_out, out_far)

    proj_c = pick(projection.reshape(8, 2, 256, 1024), c, 1).reshape(2048, 1024)
    sends = lax.optimization_barrier((proj_c[:1024], proj_c[1024:], ends[0]))[:2]
    third = fetch(*(after(v, kv_late) for v in sends))

    parts = [b0, shift(b3, "z", 2), shift(b1, "z", 1), shift(b2, "z", -1)]
    third_up, third_down, *parts = lax.optimization_barrier((*third, *parts))
    own_layer = make_layer(place, student_in, parts)
    teach_far = shift(after(rows_of(teacher_rows, (1 - yl) * 512, 512), own_layer), "yl", 1)
    layers, ends = around(own_layer)
    third = jnp.concatenate([third_up, third_down], axis=0)
    p_far = [third, shift(third, "c", 1)]
    same = (projection, p_far, teacher_rows, teach_far)
    near = errors(1, place, layers, *same)
    ends = [after(v, near[0]) for v in ends]
    err_b, sq_b, mine, other = errors(1, place, ends, *same, earlier=near)
    theirs = shift(other, "c", 1)
    err_b_sib = shift(err_b, "c", 1)
    err_a, sq_a = errors(0, place, [mine, after(other, err_b)], *same)
    err_a_sib = shift(err_a, "c", 1)

    gb = gradient(False, place, mine, theirs, after(err_b, err_a), err_b_sib)
    squared = sq_a + sq_b
    squared = squared + shift(squared, "yl", 1)
    ga = gradient(True, place, mine, theirs, after(err_a, gb[0], squared), err_a_sib)
    ga = [ga[0]] + [shift(ga[k], "x", k) for k in (1, 2, 3)]
    squared = lax.psum(squared, "z")
    seq_loss = squared.reshape(1) / (lengths.astype(F32) * DT)
    ga[0] = after(ga[0], seq_loss)
    gb = [gb[0], shift_y(gb[1], 2), shift_y(gb[2], 1), shift_y(gb[3], -1)]
    a = partial_sums(sum_x_kernel, place, ga)
    a = [a[0], shift_y(a[1], 2), shift_y(a[2], 1), shift_y(a[3], -1)]
    b = partial_sums(sum_y_kernel, place, gb)
    b = [b[0]] + [shift(b[k], "x", k) for k in (1, 2, 3)]
    return last_sum(a + b), seq_loss


def solution(mesh):
    split = Mesh(mesh.devices.reshape(4, 2, 2, 2, 4), AXES)
    dp, tensor = ("x", "yh", "c"), ("yl", "z")
    placed = (
        P(dp + tensor, None),
        P(),
        P(None, tensor),
        P(None, tensor),
        P(None, tensor),
        P(tensor, None),
        P(None, tensor),
        P(dp, tensor),
        P(dp),
    )
    return jax.shard_map(
        shards, mesh=split, in_specs=placed, out_specs=(P(dp, tensor), P(dp)), check_vma=False
    )
```

```python
import functools
import math

import jax
import jax.numpy as jnp
from jax import lax
from jax.experimental import pallas as pl
from jax.experimental.pallas import tpu as pltpu
from jax.sharding import Mesh, PartitionSpec as P

HEAD_DIM = 128
DT = 8192
EPSILON = 1e-05
ROPE_BASE = 500000.0
NEG_LARGE = -1e30
AXES = ("x", "yh", "c", "yl", "z")
SIZES = {"x": 4, "yh": 2, "c": 2, "yl": 2, "z": 4}
F32 = jnp.float32
BF16 = jnp.bfloat16
PARAMS = pltpu.CompilerParams(vmem_limit_bytes=48 * 2**20)


def shift(value, axis, step):
    count = SIZES[axis]
    return lax.ppermute(value, axis, [(i, (i + step) % count) for i in range(count)])


def shift_y(value, step):
    return lax.ppermute(value, ("yh", "yl"), [(i, (i + step) % 4) for i in range(4)])


def after(value, *others):
    return lax.optimization_barrier((value, *others))[0]


def rows_of(array, start, count):
    return lax.dynamic_slice_in_dim(array, start, count, 0)


def pick(array, at, axis):
    return lax.dynamic_index_in_dim(array, at, axis, keepdims=False)


def dot(left, right):
    return jnp.dot(left, right, preferred_element_type=F32)


def norm_kernel(in_ref, gain_ref, out_ref):
    widened = in_ref[...].astype(F32)
    mean_square = jnp.mean(widened * widened, axis=-1, keepdims=True)
    out_ref[...] = (widened * lax.rsqrt(mean_square + EPSILON) * gain_ref[...]).astype(BF16)


def root_norm(inputs, norm_gain):
    return pl.pallas_call(
        norm_kernel,
        grid=(4,),
        in_specs=[
            pl.BlockSpec((32, 4096), lambda i: (i, 0)),
            pl.BlockSpec((1, 4096), lambda i: (0, 0)),
        ],
        out_specs=pl.BlockSpec((32, 4096), lambda i: (i, 0)),
        out_shape=jax.ShapeDtypeStruct((128, 4096), BF16),
        compiler_params=PARAMS,
    )(inputs, norm_gain.reshape(1, 4096))


def ring_step(block):
    return block ^ (block // 2)


def ring_position(index, z):
    return ((z + ring_step(index // 128)) % 4) * 128 + index % 128


def turned(product, cosine, sine, last):
    def turn(head):
        return head * cosine + pltpu.roll(head, 64, 1) * sine

    left, right = product[:, :128], product[:, 128:]
    right = jnp.where(last, right, turn(right))
    return jnp.concatenate([turn(left), right], axis=1).astype(BF16)


def own_heads_kernel(*refs):
    *x_refs, q_ref, kv_ref, cos_ref, sin_ref, out_ref = refs
    x = jnp.concatenate([ref[...] for ref in x_refs if ref.shape[1] == 4096], axis=0)
    last = pl.program_id(0) == 2

    def finish(w_ref):
        out_ref[...] = turned(dot(x, w_ref[...]), cos_ref[...], sin_ref[...], last)

    pl.when(pl.program_id(0) < 2)(lambda: finish(q_ref))
    pl.when(last)(lambda: finish(kv_ref))


def own_heads_of(pieces, w_query, kv_own, cosine, sine, earlier=None):
    rows, at = sum(v.shape[0] for v in pieces), 0 if earlier is None else 3
    turn = pl.BlockSpec((rows, 128), lambda n: (at, 0))
    kept, alias = [], {}
    if earlier is not None:
        kept, alias = [earlier], {0: 0}
    return pl.pallas_call(
        own_heads_kernel,
        grid=(3,),
        in_specs=[pl.BlockSpec(memory_space=pl.ANY)] * len(kept)
        + [pl.BlockSpec(v.shape, lambda n: (0, 0)) for v in pieces]
        + [
            pl.BlockSpec((4096, 256), lambda n: (0, jnp.minimum(n, 1))),
            pl.BlockSpec((4096, 256), lambda n: (0, 0)),
            turn,
            turn,
        ],
        out_specs=pl.BlockSpec((rows, 256), lambda n: (at, n)),
        out_shape=jax.ShapeDtypeStruct((512, 768), BF16),
        input_output_aliases=alias,
        compiler_params=PARAMS,
    )(*kept, *pieces, w_query, kv_own, cosine, sine)


def placed(refs):
    start = 0
    for ref in refs:
        yield slice(start, start + ref.shape[0]), ref
        start += ref.shape[0]


def far_heads_kernel(at_ref, *refs):
    *pieces, w0, w1, w2, w3, cos_ref, sin_ref, out_ref, x_ref = refs
    core = at_ref[3]

    @pl.when(pl.program_id(0) == 0)
    def _():
        for here, ref in placed(pieces):
            for k in range(4):
                source = ((core + k // 2) % 2) * 2048 + (k % 2) * 1024
                x_ref[here, 1024 * k : 1024 * k + 1024] = ref[
                    :, pl.ds(pl.multiple_of(source, 1024), 1024)
                ]

    product = dot(x_ref[:, :1024], w0[...])
    for k, ref in ((1, w1), (2, w2), (3, w3)):
        product = product + dot(x_ref[:, 1024 * k : 1024 * k + 1024], ref[...])
    out_ref[...] = turned(product, cos_ref[...], sin_ref[...], pl.program_id(0) == 2)


def far_heads_of(place, pieces, quarters, cosine, sine):
    whole = [pl.BlockSpec(v.shape, lambda n, at: (0, 0)) for v in pieces]
    weight = pl.BlockSpec((1024, 256), lambda n, at: (0, n))
    turn = pl.BlockSpec((512, 128), lambda n, at: (0, 0))
    return pl.pallas_call(
        far_heads_kernel,
        grid_spec=pltpu.PrefetchScalarGridSpec(
            num_scalar_prefetch=1,
            grid=(3,),
            in_specs=whole + [weight] * 4 + [turn] * 2,
            out_specs=pl.BlockSpec((512, 256), lambda n, at: (0, n)),
            scratch_shapes=[pltpu.VMEM((512, 4096), BF16)],
        ),
        out_shape=jax.ShapeDtypeStruct((512, 768), BF16),
        compiler_params=PARAMS,
    )(place, *pieces, *quarters, cosine, sine)


def attend_kernel(at_ref, q_ref, own_ref, far_ref, out_ref):
    z, yl, length = at_ref[0], at_ref[1], at_ref[2]
    factor = math.log2(math.e) / math.sqrt(HEAD_DIM)
    q = jnp.concatenate([q_ref[:, 128 * h : 128 * h + 128] for h in range(4)], axis=0)
    shape = (512, 512)
    ring = ring_position(lax.broadcasted_iota(jnp.int32, (1, 512), 1), z)
    q_at = ((z + ring_step(pl.program_id(0))) % 4) * 128 + lax.broadcasted_iota(jnp.int32, (512, 1), 0) % 128
    contract = (((1,), (1,)), ((), ()))

    def scores(kv_ref):
        return factor * lax.dot_general(q, kv_ref[:, :128], contract, preferred_element_type=F32)

    own_ok = (ring <= q_at) & (ring + yl * 512 < length)
    own = jnp.where(jnp.broadcast_to(own_ok, shape), scores(own_ref), NEG_LARGE)
    top = jnp.max(own, axis=-1, keepdims=True)

    def store(total, blended):
        blended = (blended / total).astype(BF16)
        for h in range(4):
            out_ref[:, 128 * h : 128 * h + 128] = blended[128 * h : 128 * h + 128]

    @pl.when(yl == 0)
    def _():
        weights = jnp.exp2(own - top)
        store(
            jnp.sum(weights, axis=-1, keepdims=True), dot(weights.astype(BF16), own_ref[:, 128:])
        )

    @pl.when(yl == 1)
    def _():
        far = jnp.where(jnp.broadcast_to(ring < length, shape), scores(far_ref), NEG_LARGE)
        highest = jnp.maximum(top, jnp.max(far, axis=-1, keepdims=True))
        own_weights = jnp.exp2(own - highest)
        far_weights = jnp.exp2(far - highest)
        total = jnp.sum(own_weights, axis=-1, keepdims=True) + jnp.sum(
            far_weights, axis=-1, keepdims=True
        )
        store(
            total,
            dot(own_weights.astype(BF16), own_ref[:, 128:])
            + dot(far_weights.astype(BF16), far_ref[:, 128:]),
        )


def attend(place, heads, far_kv):
    return pl.pallas_call(
        attend_kernel,
        grid_spec=pltpu.PrefetchScalarGridSpec(
            num_scalar_prefetch=1,
            grid=(4,),
            in_specs=[
                pl.BlockSpec((128, 512), lambda j, at: (j, 0)),
                pl.BlockSpec((512, 256), lambda j, at: (0, 2)),
                pl.BlockSpec((512, 256), lambda j, at: (0, 0)),
            ],
            out_specs=pl.BlockSpec((128, 512), lambda j, at: (j, 0)),
        ),
        out_shape=jax.ShapeDtypeStruct((512, 512), BF16),
        compiler_params=PARAMS,
    )(place, heads, heads, far_kv)


def layer_kernel(at_ref, student_ref, *refs):
    *parts, out_ref = refs
    total = parts[0][...].astype(F32)
    for part in parts[1:]:
        total = total + part[...].astype(F32)
    layer = (student_ref[...].astype(F32) + total).astype(BF16)
    even = [layer[:, 512 * i : 512 * i + 256] for i in range(8)]
    odd = [layer[:, 512 * i + 256 : 512 * i + 512] for i in range(8)]

    @pl.when(at_ref[3] == 0)
    def _():
        out_ref[...] = jnp.concatenate(even + odd, axis=1)

    @pl.when(at_ref[3] == 1)
    def _():
        out_ref[...] = jnp.concatenate(odd + even, axis=1)


def make_layer(place, student_in, parts):
    spec = pl.BlockSpec((32, 4096), lambda i, at: (i, 0))
    return pl.pallas_call(
        layer_kernel,
        grid_spec=pltpu.PrefetchScalarGridSpec(
            num_scalar_prefetch=1, grid=(4,), in_specs=[spec] * 5, out_specs=spec
        ),
        out_shape=jax.ShapeDtypeStruct((128, 4096), BF16),
        compiler_params=PARAMS,
    )(place, student_in, *parts)


def out_kernel(at_ref, own, far, w, w0, w1, w2, w3, *refs):
    *out_refs, x_ref = refs

    @pl.when(pl.program_id(0) == 0)
    def _():
        x_ref[:, :512] = own[...]
        for k in range(2):
            source = ((at_ref[3] + k) % 2) * 256
            x_ref[:, 512 + 256 * k : 768 + 256 * k] = far[:, pl.ds(pl.multiple_of(source, 256), 256)]

    weights = jnp.concatenate([ref[...] for ref in (w, w0, w1, w2, w3)], axis=0)
    total = dot(x_ref[...], weights)
    for j, ref in enumerate(out_refs):
        ref[...] = total[128 * j : 128 * j + 128].astype(BF16)


def out_blocks(place, own, far, w_out, quarters):
    att = pl.BlockSpec((512, 512), lambda n, at: (0, 0))
    quarter = pl.BlockSpec((128, 1024), lambda n, at: (0, n))
    return pl.pallas_call(
        out_kernel,
        grid_spec=pltpu.PrefetchScalarGridSpec(
            num_scalar_prefetch=1,
            grid=(4,),
            in_specs=[att, att, pl.BlockSpec((512, 1024), lambda n, at: (0, n))] + [quarter] * 4,
            out_specs=[quarter] * 4,
            scratch_shapes=[pltpu.VMEM((512, 1024), BF16)],
        ),
        out_shape=[jax.ShapeDtypeStruct((128, 4096), BF16)] * 4,
        compiler_params=PARAMS,
    )(place, own, far, w_out, *quarters)


def error_kernel(first, rows, kept, at_ref, *refs):
    layers = refs[kept:-13] if rows < 512 else refs[:2]
    p_own, f0, f1, f2, f3, t_own, t_far, err_ref, sum_ref = refs[len(layers) + kept :][:9]
    x_ref, n_ref = refs[-2:]
    step = pl.program_id(0)
    z, yl, length, core = at_ref[0], at_ref[1], at_ref[2], at_ref[3]

    @pl.when(step == 0)
    def _():
        if rows == 512:
            x_ref[:, :2048] = layers[0][...]
            x_ref[:, 2048:] = layers[1][...]
        else:
            for here, ref in placed(layers):
                x_ref[here, :] = ref[...]
            refs[-4][...] = x_ref[:, :2048]
            refs[-3][...] = x_ref[:, 2048:]
        for i in range(16):
            block = i // 2 + 8 * ((core + i) % 2)
            n_ref[:, 256 * i : 256 * i + 256] = x_ref[
                :, pl.ds(pl.multiple_of(block * 256, 256), 256)
            ]
        sum_ref[...] = refs[3][...] if kept else jnp.zeros((1, 1), F32)

    index = 128 * first + lax.broadcasted_iota(jnp.int32, (rows, 1), 0)
    pos = yl * 512 + ring_position(index, z)
    live = jnp.broadcast_to(pos < length, (rows, 256))

    def part(columns, predicted, t_ref):
        teacher = [
            t_ref[pl.ds(pl.multiple_of(((z + ring_step(first + j)) % 4) * 128, 128), 128), :]
            for j in range(rows // 128)
        ]
        residue = predicted - jnp.concatenate(teacher, axis=0).astype(F32)
        residue = jnp.where(live, residue, 0.0)
        err_ref[:, columns] = (residue / length.astype(F32)).astype(BF16)
        sum_ref[...] += jnp.sum(residue * residue).reshape(1, 1)

    part(slice(0, 256), dot(n_ref[...], p_own[...]), t_own)
    predicted = dot(x_ref[:, :1024], f0[...])
    for k, ref in ((1, f1), (2, f2), (3, f3)):
        predicted = predicted + dot(x_ref[:, 1024 * k : 1024 * k + 1024], ref[...])
    part(slice(256, 512), predicted, t_far)


def errors(half, place, layers, projection, p_far, t_own, t_far, earlier=()):
    rows = 512 if layers[0].shape[0] == 512 else sum(v.shape[0] for v in layers)
    first, kept = (3, 4) if earlier else (0, 0)

    def columns(n, at):
        return (0, 2 * half + n)

    def own_rows(n, at):
        return (at[1], 2 * half + n)

    def constant(n, at):
        return (0, 0)

    anywhere = pl.BlockSpec(memory_space=pl.ANY)
    kept_specs = [anywhere] * 3 + [pl.BlockSpec((1, 1), constant)] if earlier else []
    out_specs = [
        pl.BlockSpec((rows, 512), lambda n, at: (first, n)),
        pl.BlockSpec((1, 1), constant),
    ]
    out_shape = [
        jax.ShapeDtypeStruct((512, 1024), BF16),
        jax.ShapeDtypeStruct((1, 1), F32),
    ]
    if rows < 512:
        out_specs += [pl.BlockSpec((rows, 2048), lambda n, at: (first, 0))] * 2
        out_shape += [jax.ShapeDtypeStruct((512, 2048), BF16)] * 2
    if earlier:
        err, total, left, right = earlier
        earlier = (err, left, right, total)
    return pl.pallas_call(
        functools.partial(error_kernel, first, rows, kept),
        grid_spec=pltpu.PrefetchScalarGridSpec(
            num_scalar_prefetch=1,
            grid=(2,),
            in_specs=kept_specs
            + [pl.BlockSpec(v.shape, constant) for v in layers]
            + [pl.BlockSpec((4096, 256), columns)]
            + [pl.BlockSpec((1024, 256), columns)] * 4
            + [pl.BlockSpec((512, 256), own_rows), pl.BlockSpec((512, 256), columns)],
            out_specs=out_specs,
            scratch_shapes=[pltpu.VMEM((rows, 4096), BF16)] * 2,
        ),
        out_shape=out_shape,
        input_output_aliases={1: 0, 2: 2, 3: 3} if earlier else {},
        compiler_params=PARAMS,
    )(place, *earlier, *layers, projection, *p_far, t_own, t_far)


def split_columns(product):
    own = jnp.concatenate([product[:, :256], product[:, 512:768]], axis=1)
    far = jnp.concatenate([product[:, 256:512], product[:, 768:]], axis=1)
    return own, far


def by_y(at_ref, own, far, store):
    for t in (0, 1):
        this, that = slice(256 * t, 256 * t + 256), slice(256 - 256 * t, 512 - 256 * t)

        @pl.when(at_ref[5] == t)
        def _():
            store(0, own[this])
            store(1, own[that])

        @pl.when(at_ref[6] == t)
        def _():
            store(2, far[this])
            store(3, far[that])


def gradient_kernel(by_x, at_ref, mine, theirs, e_mine, e_theirs, *out_refs):
    contract = (((0,), (0,)), ((), ()))
    product = lax.dot_general(mine[...], e_mine[...], contract, preferred_element_type=F32)
    product = product + lax.dot_general(
        theirs[...], e_theirs[...], contract, preferred_element_type=F32
    )
    product = product.astype(BF16)
    if by_x:
        for k, ref in enumerate(out_refs):

            @pl.when(pl.program_id(0) == k)
            def _():
                ref[...] = product
    else:

        def store(k, value):
            out_refs[k][0] = value

        by_y(at_ref, *split_columns(product), store)


def gradient(by_x, place, mine, theirs, e_mine, e_theirs):
    rows = pl.BlockSpec((512, 512), lambda k, at: (0, (at[4] + k) % 4))
    error = pl.BlockSpec((512, 1024), lambda k, at: (0, 0))
    if by_x:
        out_spec = pl.BlockSpec((512, 1024), lambda k, at: (0, 0))
        shape = (512, 1024)
    else:
        out_spec = pl.BlockSpec((1, 256, 512), lambda k, at: (k, 0, 0))
        shape = (4, 256, 512)
    return pl.pallas_call(
        functools.partial(gradient_kernel, by_x),
        grid_spec=pltpu.PrefetchScalarGridSpec(
            num_scalar_prefetch=1,
            grid=(4,),
            in_specs=[rows, rows, error, error],
            out_specs=[out_spec] * 4,
        ),
        out_shape=[jax.ShapeDtypeStruct(shape, BF16)] * 4,
        compiler_params=PARAMS,
    )(place, mine, theirs, e_mine, e_theirs)


def total_of(refs):
    total = refs[0][...].astype(F32)
    for ref in refs[1:]:
        total = total + ref[...].astype(F32)
    return total


def sum_x_kernel(at_ref, *refs):
    def store(k, value):
        refs[4 + k][...] = value

    by_y(at_ref, *split_columns(total_of(refs[:4]).astype(BF16)), store)


def sum_y_kernel(at_ref, *refs):
    total = total_of(refs[:4]).astype(BF16)
    for k in range(4):
        refs[4 + k][...] = total[k]


def partial_sums(kernel, place, arrays):
    return pl.pallas_call(
        kernel,
        grid_spec=pltpu.PrefetchScalarGridSpec(
            num_scalar_prefetch=1,
            grid=(1,),
            in_specs=[pl.BlockSpec(memory_space=pltpu.VMEM)] * 4,
            out_specs=[pl.BlockSpec(memory_space=pltpu.VMEM)] * 4,
        ),
        out_shape=[jax.ShapeDtypeStruct((256, 512), BF16)] * 4,
        compiler_params=PARAMS,
    )(place, *arrays)


def last_kernel(*refs):
    refs[8][:, :512] = total_of(refs[:4])
    refs[8][:, 512:] = total_of(refs[4:8])


def last_sum(arrays):
    return pl.pallas_call(
        last_kernel,
        out_shape=jax.ShapeDtypeStruct((256, 1024), F32),
        compiler_params=PARAMS,
    )(*arrays)


def fetch(plus, minus):
    return shift_y(plus, 1), shift_y(minus, -1)


def swap(pair):
    return tuple(shift(v, "c", 1) for v in pair)


def shards(
    student_in, norm_gain, w_query, w_key, w_value, w_out, projection, teacher_rows, lengths
):
    x, yh, c, yl, z = (lax.axis_index(a) for a in AXES)
    length = lengths[0]
    to_up = jnp.where(yl == 0, yh, 1 - yh)
    place = jnp.stack([z, yl, length, c, x, yh, to_up])

    def around(own):
        near, back = shift(own, "z", -1), shift(own, "z", 1)
        return [own, near, back], [shift(back[:64], "z", 1), shift(near[64:], "z", -1)]

    kv_own = jnp.concatenate([w_key, w_value], axis=1)

    def quarter(at):
        return jnp.concatenate([rows_of(w, at, 1024) for w in (w_query, w_key, w_value)], axis=1)

    quarters = quarter(c * 2048), quarter(c * 2048 + 1024)
    first = fetch(*quarters)
    inverse = ROPE_BASE ** (-2.0 * jnp.arange(HEAD_DIM // 2).astype(F32) / HEAD_DIM)
    pos = yl * 512 + ring_position(jnp.arange(512), z)
    angles = pos.astype(F32)[:, None] * inverse
    cosine, sine = jnp.cos(angles), jnp.sin(angles)
    cosine = jnp.concatenate([cosine, cosine], axis=1)
    sine = jnp.concatenate([-sine, sine], axis=1)
    pieces, ends = around(root_norm(after(student_in, *quarters), norm_gain))
    pieces = list(lax.optimization_barrier((*pieces, cosine, sine, kv_own))[:3])
    near_heads = own_heads_of(pieces, w_query, kv_own, cosine, sine)
    first = tuple(after(v, *ends, near_heads) for v in first)
    first_sib = swap(first)
    out_part = after(rows_of(w_out, c * 256, 256), *first)
    second = fetch(out_part[:128], out_part[128:])
    ends = [after(v, near_heads) for v in ends]
    own_heads = own_heads_of(ends, w_query, kv_own, cosine, sine, near_heads)
    kv_early = shift(own_heads[:, 512:], "yl", 1)
    far_weights = [*first, *(after(v, own_heads) for v in first_sib)]
    far_heads = far_heads_of(place, pieces + ends, far_weights, cosine, sine)
    kv_late = shift(far_heads[:, 512:], "yl", 1)
    att_far = attend(place, far_heads, kv_early)
    second = tuple(after(v, far_heads) for v in second)
    second_sib = swap(second)
    kv_late = after(kv_late, att_far)
    att_own = attend(place, own_heads, kv_late)
    b0, b1, b2, b3 = out_blocks(place, att_own, att_far, w_out, [*second, *second_sib])

    proj_c = pick(projection.reshape(8, 2, 256, 1024), c, 1).reshape(2048, 1024)
    sends = lax.optimization_barrier((proj_c[:1024], proj_c[1024:], ends[0]))[:2]
    third = fetch(*(after(v, kv_late, *second) for v in sends))

    parts = [b0, shift(b3, "z", 2), shift(b1, "z", 1), shift(b2, "z", -1)]
    third_up, third_down, *parts = lax.optimization_barrier((*third, *parts))
    own_layer = make_layer(place, student_in, parts)
    teach_far = shift(after(rows_of(teacher_rows, (1 - yl) * 512, 512), own_layer), "yl", 1)
    layers, ends = around(own_layer)
    p_far = [third_up, third_down, shift(third_up, "c", 1), shift(third_down, "c", 1)]
    same = (projection, p_far, teacher_rows, teach_far)
    near = errors(1, place, layers, *same)
    ends = [after(v, near[0]) for v in ends]
    err_b, sq_b, mine, other = errors(1, place, ends, *same, earlier=near)
    theirs = shift(other, "c", 1)
    err_b_sib = shift(err_b, "c", 1)
    err_a, sq_a = errors(0, place, [mine, after(other, err_b)], *same)
    err_a_sib = shift(err_a, "c", 1)

    gb = gradient(False, place, mine, theirs, after(err_b, err_a), err_b_sib)
    squared = after(sq_a + sq_b, gb[0])
    squared = squared + shift(squared, "z", 1)
    ga = gradient(True, place, mine, theirs, after(err_a, gb[0], squared), err_a_sib)
    ga = [ga[0]] + [shift(ga[k], "x", k) for k in (1, 2, 3)]
    squared = squared + shift(squared, "z", 2)
    squared = squared + shift(squared, "yl", 1)
    seq_loss = squared.reshape(1) / (lengths.astype(F32) * DT)
    ga[0] = after(ga[0], seq_loss)
    gb = [gb[0], shift_y(gb[1], 2), shift_y(gb[2], 1), shift_y(gb[3], -1)]
    a = partial_sums(sum_x_kernel, place, ga)
    a = [a[0], shift_y(a[1], 2), shift_y(a[2], 1), shift_y(a[3], -1)]
    b = partial_sums(sum_y_kernel, place, gb)
    b = [b[0]] + [shift(b[k], "x", k) for k in (1, 2, 3)]
    return last_sum(a + b), seq_loss


def solution(mesh):
    split = Mesh(mesh.devices.reshape(4, 2, 2, 2, 4), AXES)
    dp, tensor = ("x", "yh", "c"), ("yl", "z")
    placed = (
        P(dp + tensor, None),
        P(),
        P(None, tensor),
        P(None, tensor),
        P(None, tensor),
        P(tensor, None),
        P(None, tensor),
        P(dp, tensor),
        P(dp),
    )
    return jax.shard_map(
        shards, mesh=split, in_specs=placed, out_specs=(P(dp, tensor), P(dp)), check_vma=False
    )
```

```python
import functools
import math

import jax
import jax.numpy as jnp
from jax import lax
from jax.experimental import pallas as pl
from jax.experimental.pallas import tpu as pltpu
from jax.sharding import Mesh, PartitionSpec as P

HEAD_DIM = 128
DT = 8192
EPSILON = 1e-05
ROPE_BASE = 500000.0
NEG_LARGE = -1e30
AXES = ("x", "yh", "c", "yl", "z")
SIZES = {"x": 4, "yh": 2, "c": 2, "yl": 2, "z": 4}
F32 = jnp.float32
BF16 = jnp.bfloat16
PARAMS = pltpu.CompilerParams(vmem_limit_bytes=48 * 2**20)


def shift(value, axis, step):
    count = SIZES[axis]
    return lax.ppermute(value, axis, [(i, (i + step) % count) for i in range(count)])


def shift_y(value, step):
    return lax.ppermute(value, ("yh", "yl"), [(i, (i + step) % 4) for i in range(4)])


def cross_y(value):
    return lax.ppermute(value, ("yh", "yl"), [(0, 3), (3, 0), (1, 2), (2, 1)])


def after(value, *others):
    return lax.optimization_barrier((value, *others))[0]


def rows_of(array, start, count):
    return lax.dynamic_slice_in_dim(array, start, count, 0)


def pick(array, at, axis):
    return lax.dynamic_index_in_dim(array, at, axis, keepdims=False)


def dot(left, right):
    return jnp.dot(left, right, preferred_element_type=F32)


def norm_kernel(in_ref, gain_ref, out_ref):
    widened = in_ref[...].astype(F32)
    mean_square = jnp.mean(widened * widened, axis=-1, keepdims=True)
    out_ref[...] = (widened * lax.rsqrt(mean_square + EPSILON) * gain_ref[...]).astype(BF16)


def root_norm(inputs, norm_gain):
    return pl.pallas_call(
        norm_kernel,
        grid=(4,),
        in_specs=[
            pl.BlockSpec((32, 4096), lambda i: (i, 0)),
            pl.BlockSpec((1, 4096), lambda i: (0, 0)),
        ],
        out_specs=pl.BlockSpec((32, 4096), lambda i: (i, 0)),
        out_shape=jax.ShapeDtypeStruct((128, 4096), BF16),
        compiler_params=PARAMS,
    )(inputs, norm_gain.reshape(1, 4096))


def ring_step(block):
    return block ^ (block // 2)


def ring_position(index, z):
    return ((z + ring_step(index // 128)) % 4) * 128 + index % 128


def turned(product, cosine, sine, last):
    def turn(head):
        return head * cosine + pltpu.roll(head, 64, 1) * sine

    left, right = product[:, :128], product[:, 128:]
    right = jnp.where(last, right, turn(right))
    return jnp.concatenate([turn(left), right], axis=1).astype(BF16)


def own_heads_kernel(*refs):
    *x_refs, q_ref, kv_ref, cos_ref, sin_ref, out_ref = refs
    x = jnp.concatenate([ref[...] for ref in x_refs if ref.shape[1] == 4096], axis=0)
    last = pl.program_id(0) == 2

    def finish(w_ref):
        out_ref[...] = turned(dot(x, w_ref[...]), cos_ref[...], sin_ref[...], last)

    pl.when(pl.program_id(0) < 2)(lambda: finish(q_ref))
    pl.when(last)(lambda: finish(kv_ref))


def own_heads_of(pieces, w_query, kv_own, cosine, sine, earlier=None):
    rows, at = sum(v.shape[0] for v in pieces), 0 if earlier is None else 3
    turn = pl.BlockSpec((rows, 128), lambda n: (at, 0))
    kept, alias = [], {}
    if earlier is not None:
        kept, alias = [earlier], {0: 0}
    return pl.pallas_call(
        own_heads_kernel,
        grid=(3,),
        in_specs=[pl.BlockSpec(memory_space=pl.ANY)] * len(kept)
        + [pl.BlockSpec(v.shape, lambda n: (0, 0)) for v in pieces]
        + [
            pl.BlockSpec((4096, 256), lambda n: (0, jnp.minimum(n, 1))),
            pl.BlockSpec((4096, 256), lambda n: (0, 0)),
            turn,
            turn,
        ],
        out_specs=pl.BlockSpec((rows, 256), lambda n: (at, n)),
        out_shape=jax.ShapeDtypeStruct((512, 768), BF16),
        input_output_aliases=alias,
        compiler_params=PARAMS,
    )(*kept, *pieces, w_query, kv_own, cosine, sine)


def placed(refs):
    start = 0
    for ref in refs:
        yield slice(start, start + ref.shape[0]), ref
        start += ref.shape[0]


def far_heads_kernel(at_ref, *refs):
    *pieces, w0, w1, w2, w3, cos_ref, sin_ref, out_ref, x_ref = refs
    core = at_ref[3]

    @pl.when(pl.program_id(0) == 0)
    def _():
        for here, ref in placed(pieces):
            for k in range(4):
                source = ((core + k // 2) % 2) * 2048 + (k % 2) * 1024
                x_ref[here, 1024 * k : 1024 * k + 1024] = ref[
                    :, pl.ds(pl.multiple_of(source, 1024), 1024)
                ]

    product = dot(x_ref[:, :1024], w0[...])
    for k, ref in ((1, w1), (2, w2), (3, w3)):
        product = product + dot(x_ref[:, 1024 * k : 1024 * k + 1024], ref[...])
    out_ref[...] = turned(product, cos_ref[...], sin_ref[...], pl.program_id(0) == 2)


def far_heads_of(place, pieces, quarters, cosine, sine):
    whole = [pl.BlockSpec(v.shape, lambda n, at: (0, 0)) for v in pieces]
    weight = pl.BlockSpec((1024, 256), lambda n, at: (0, n))
    turn = pl.BlockSpec((512, 128), lambda n, at: (0, 0))
    return pl.pallas_call(
        far_heads_kernel,
        grid_spec=pltpu.PrefetchScalarGridSpec(
            num_scalar_prefetch=1,
            grid=(3,),
            in_specs=whole + [weight] * 4 + [turn] * 2,
            out_specs=pl.BlockSpec((512, 256), lambda n, at: (0, n)),
            scratch_shapes=[pltpu.VMEM((512, 4096), BF16)],
        ),
        out_shape=jax.ShapeDtypeStruct((512, 768), BF16),
        compiler_params=PARAMS,
    )(place, *pieces, *quarters, cosine, sine)


def attend_kernel(at_ref, q_ref, own_ref, far_ref, out_ref):
    z, yl, length = at_ref[0], at_ref[1], at_ref[2]
    factor = math.log2(math.e) / math.sqrt(HEAD_DIM)
    q = jnp.concatenate([q_ref[:, 128 * h : 128 * h + 128] for h in range(4)], axis=0)
    shape = (512, 512)
    ring = ring_position(lax.broadcasted_iota(jnp.int32, (1, 512), 1), z)
    q_at = ((z + ring_step(pl.program_id(0))) % 4) * 128
    q_at = q_at + lax.broadcasted_iota(jnp.int32, (128, 1), 0)
    contract = (((1,), (1,)), ((), ()))

    def scores(kv_ref):
        return factor * lax.dot_general(q, kv_ref[:, :128], contract, preferred_element_type=F32)

    own_ok = (ring <= q_at) & (ring + yl * 512 < length)
    bias = jnp.where(jnp.broadcast_to(own_ok, (128, 512)), 0.0, NEG_LARGE)
    own = (scores(own_ref).reshape(4, 128, 512) + bias[None]).reshape(shape)
    top = jnp.max(own, axis=-1, keepdims=True)

    def store(total, blended):
        blended = (blended / total).astype(BF16)
        for h in range(4):
            out_ref[:, 128 * h : 128 * h + 128] = blended[128 * h : 128 * h + 128]

    @pl.when(yl == 0)
    def _():
        weights = jnp.exp2(own - top)
        store(
            jnp.sum(weights, axis=-1, keepdims=True), dot(weights.astype(BF16), own_ref[:, 128:])
        )

    @pl.when(yl == 1)
    def _():
        far = scores(far_ref) + jnp.where(ring < length, 0.0, NEG_LARGE)
        highest = jnp.maximum(top, jnp.max(far, axis=-1, keepdims=True))
        own_weights = jnp.exp2(own - highest)
        far_weights = jnp.exp2(far - highest)
        total = jnp.sum(own_weights, axis=-1, keepdims=True) + jnp.sum(
            far_weights, axis=-1, keepdims=True
        )
        store(
            total,
            dot(own_weights.astype(BF16), own_ref[:, 128:])
            + dot(far_weights.astype(BF16), far_ref[:, 128:]),
        )


def attend(place, heads, far_kv):
    return pl.pallas_call(
        attend_kernel,
        grid_spec=pltpu.PrefetchScalarGridSpec(
            num_scalar_prefetch=1,
            grid=(4,),
            in_specs=[
                pl.BlockSpec((128, 512), lambda j, at: (j, 0)),
                pl.BlockSpec((512, 256), lambda j, at: (0, 2)),
                pl.BlockSpec((512, 256), lambda j, at: (0, 0)),
            ],
            out_specs=pl.BlockSpec((128, 512), lambda j, at: (j, 0)),
        ),
        out_shape=jax.ShapeDtypeStruct((512, 512), BF16),
        compiler_params=PARAMS,
    )(place, heads, heads, far_kv)


def layer_kernel(at_ref, student_ref, *refs):
    *parts, out_ref = refs
    total = parts[0][...].astype(F32)
    for part in parts[1:]:
        total = total + part[...].astype(F32)
    layer = (student_ref[...].astype(F32) + total).astype(BF16)
    even = [layer[:, 512 * i : 512 * i + 256] for i in range(8)]
    odd = [layer[:, 512 * i + 256 : 512 * i + 512] for i in range(8)]

    @pl.when(at_ref[3] == 0)
    def _():
        out_ref[...] = jnp.concatenate(even + odd, axis=1)

    @pl.when(at_ref[3] == 1)
    def _():
        out_ref[...] = jnp.concatenate(odd + even, axis=1)


def make_layer(place, student_in, parts):
    spec = pl.BlockSpec((32, 4096), lambda i, at: (i, 0))
    return pl.pallas_call(
        layer_kernel,
        grid_spec=pltpu.PrefetchScalarGridSpec(
            num_scalar_prefetch=1, grid=(4,), in_specs=[spec] * 5, out_specs=spec
        ),
        out_shape=jax.ShapeDtypeStruct((128, 4096), BF16),
        compiler_params=PARAMS,
    )(place, student_in, *parts)


def out_kernel(at_ref, own, far, w, w0, w1, w2, w3, *refs):
    *out_refs, x_ref = refs

    @pl.when(pl.program_id(0) == 0)
    def _():
        x_ref[:, :512] = own[...]
        for k in range(2):
            source = ((at_ref[3] + k) % 2) * 256
            x_ref[:, 512 + 256 * k : 768 + 256 * k] = far[:, pl.ds(pl.multiple_of(source, 256), 256)]

    weights = jnp.concatenate([ref[...] for ref in (w, w0, w1, w2, w3)], axis=0)
    total = dot(x_ref[...], weights)
    for j, ref in enumerate(out_refs):
        ref[...] = total[128 * j : 128 * j + 128].astype(BF16)


def out_blocks(place, own, far, w_out, quarters):
    att = pl.BlockSpec((512, 512), lambda n, at: (0, 0))
    quarter = pl.BlockSpec((128, 1024), lambda n, at: (0, n))
    fetched = [pl.BlockSpec((v.shape[0], 1024), lambda n, at: (0, n)) for v in quarters]
    return pl.pallas_call(
        out_kernel,
        grid_spec=pltpu.PrefetchScalarGridSpec(
            num_scalar_prefetch=1,
            grid=(4,),
            in_specs=[att, att, pl.BlockSpec((512, 1024), lambda n, at: (0, n))] + fetched,
            out_specs=[quarter] * 4,
            scratch_shapes=[pltpu.VMEM((512, 1024), BF16)],
        ),
        out_shape=[jax.ShapeDtypeStruct((128, 4096), BF16)] * 4,
        compiler_params=PARAMS,
    )(place, own, far, w_out, *quarters)


def error_kernel(first, rows, kept, at_ref, *refs):
    layers = refs[kept:-13] if rows < 512 else refs[:2]
    p_own, f0, f1, f2, f3, t_own, t_far, err_ref, sum_ref = refs[len(layers) + kept :][:9]
    x_ref, n_ref = refs[-2:]
    step = pl.program_id(0)
    z, yl, length, core = at_ref[0], at_ref[1], at_ref[2], at_ref[3]

    @pl.when(step == 0)
    def _():
        if rows == 512:
            x_ref[:, :2048] = layers[0][...]
            x_ref[:, 2048:] = layers[1][...]
        else:
            for here, ref in placed(layers):
                x_ref[here, :] = ref[...]
            refs[-4][...] = x_ref[:, :2048]
            refs[-3][...] = x_ref[:, 2048:]
        for i in range(16):
            block = i // 2 + 8 * ((core + i) % 2)
            n_ref[:, 256 * i : 256 * i + 256] = x_ref[
                :, pl.ds(pl.multiple_of(block * 256, 256), 256)
            ]
        sum_ref[...] = refs[3][...] if kept else jnp.zeros((1, 1), F32)

    index = 128 * first + lax.broadcasted_iota(jnp.int32, (rows, 1), 0)
    pos = yl * 512 + ring_position(index, z)
    live = jnp.broadcast_to(pos < length, (rows, 256))

    def part(columns, predicted, t_ref):
        teacher = [
            t_ref[pl.ds(pl.multiple_of(((z + ring_step(first + j)) % 4) * 128, 128), 128), :]
            for j in range(rows // 128)
        ]
        residue = predicted - jnp.concatenate(teacher, axis=0).astype(F32)
        residue = jnp.where(live, residue, 0.0)
        err_ref[:, columns] = (residue / length.astype(F32)).astype(BF16)
        sum_ref[...] += jnp.sum(residue * residue).reshape(1, 1)

    part(slice(0, 256), dot(n_ref[...], p_own[...]), t_own)
    predicted = dot(x_ref[:, :1024], f0[...])
    for k, ref in ((1, f1), (2, f2), (3, f3)):
        predicted = predicted + dot(x_ref[:, 1024 * k : 1024 * k + 1024], ref[...])
    part(slice(256, 512), predicted, t_far)


def errors(half, place, layers, projection, p_far, t_own, t_far, earlier=()):
    rows = 512 if layers[0].shape[0] == 512 else sum(v.shape[0] for v in layers)
    first, kept = (3, 4) if earlier else (0, 0)

    def columns(n, at):
        return (0, 2 * half + n)

    def own_rows(n, at):
        return (at[1], 2 * half + n)

    def constant(n, at):
        return (0, 0)

    anywhere = pl.BlockSpec(memory_space=pl.ANY)
    kept_specs = [anywhere] * 3 + [pl.BlockSpec((1, 1), constant)] if earlier else []
    out_specs = [
        pl.BlockSpec((rows, 512), lambda n, at: (first, n)),
        pl.BlockSpec((1, 1), constant),
    ]
    out_shape = [
        jax.ShapeDtypeStruct((512, 1024), BF16),
        jax.ShapeDtypeStruct((1, 1), F32),
    ]
    if rows < 512:
        out_specs += [pl.BlockSpec((rows, 2048), lambda n, at: (first, 0))] * 2
        out_shape += [jax.ShapeDtypeStruct((512, 2048), BF16)] * 2
    if earlier:
        err, total, left, right = earlier
        earlier = (err, left, right, total)
    return pl.pallas_call(
        functools.partial(error_kernel, first, rows, kept),
        grid_spec=pltpu.PrefetchScalarGridSpec(
            num_scalar_prefetch=1,
            grid=(2,),
            in_specs=kept_specs
            + [pl.BlockSpec(v.shape, constant) for v in layers]
            + [pl.BlockSpec((4096, 256), columns)]
            + [pl.BlockSpec((1024, 256), columns)] * 4
            + [pl.BlockSpec((512, 256), own_rows), pl.BlockSpec((512, 256), columns)],
            out_specs=out_specs,
            scratch_shapes=[pltpu.VMEM((rows, 4096), BF16)] * 2,
        ),
        out_shape=out_shape,
        input_output_aliases={1: 0, 2: 2, 3: 3} if earlier else {},
        compiler_params=PARAMS,
    )(place, *earlier, *layers, projection, *p_far, t_own, t_far)


def split_columns(product):
    own = jnp.concatenate([product[:, :256], product[:, 512:768]], axis=1)
    far = jnp.concatenate([product[:, 256:512], product[:, 768:]], axis=1)
    return own, far


def by_y(at_ref, own, far, store):
    for t in (0, 1):
        this, that = slice(256 * t, 256 * t + 256), slice(256 - 256 * t, 512 - 256 * t)

        @pl.when(at_ref[5] == t)
        def _():
            store(0, own[this])
            store(1, own[that])

        @pl.when(at_ref[6] == t)
        def _():
            store(2, far[this])
            store(3, far[that])


def gradient_kernel(by_x, at_ref, mine, theirs, e_mine, e_theirs, *out_refs):
    contract = (((0,), (0,)), ((), ()))
    product = lax.dot_general(mine[...], e_mine[...], contract, preferred_element_type=F32)
    product = product + lax.dot_general(
        theirs[...], e_theirs[...], contract, preferred_element_type=F32
    )
    product = product.astype(BF16)
    if by_x:
        for k, ref in enumerate(out_refs):

            @pl.when(pl.program_id(0) == k)
            def _():
                ref[...] = product
    else:

        def store(k, value):
            out_refs[k][0] = value

        by_y(at_ref, *split_columns(product), store)


def gradient(by_x, place, mine, theirs, e_mine, e_theirs):
    rows = pl.BlockSpec((512, 512), lambda k, at: (0, (at[4] + k) % 4))
    error = pl.BlockSpec((512, 1024), lambda k, at: (0, 0))
    if by_x:
        out_spec = pl.BlockSpec((512, 1024), lambda k, at: (0, 0))
        shape = (512, 1024)
    else:
        out_spec = pl.BlockSpec((1, 256, 512), lambda k, at: (k, 0, 0))
        shape = (4, 256, 512)
    return pl.pallas_call(
        functools.partial(gradient_kernel, by_x),
        grid_spec=pltpu.PrefetchScalarGridSpec(
            num_scalar_prefetch=1,
            grid=(4,),
            in_specs=[rows, rows, error, error],
            out_specs=[out_spec] * 4,
        ),
        out_shape=[jax.ShapeDtypeStruct(shape, BF16)] * 4,
        compiler_params=PARAMS,
    )(place, mine, theirs, e_mine, e_theirs)


def total_of(refs):
    total = refs[0][...].astype(F32)
    for ref in refs[1:]:
        total = total + ref[...].astype(F32)
    return total


def sum_x_kernel(at_ref, *refs):
    def store(k, value):
        refs[4 + k][...] = value

    by_y(at_ref, *split_columns(total_of(refs[:4]).astype(BF16)), store)


def sum_y_kernel(at_ref, *refs):
    total = total_of(refs[:4]).astype(BF16)
    for k in range(4):
        refs[4 + k][...] = total[k]


def partial_sums(kernel, place, arrays):
    return pl.pallas_call(
        kernel,
        grid_spec=pltpu.PrefetchScalarGridSpec(
            num_scalar_prefetch=1,
            grid=(1,),
            in_specs=[pl.BlockSpec(memory_space=pltpu.VMEM)] * 4,
            out_specs=[pl.BlockSpec(memory_space=pltpu.VMEM)] * 4,
        ),
        out_shape=[jax.ShapeDtypeStruct((256, 512), BF16)] * 4,
        compiler_params=PARAMS,
    )(place, *arrays)


def last_kernel(*refs):
    refs[8][:, :512] = total_of(refs[:4])
    refs[8][:, 512:] = total_of(refs[4:8])


def last_sum(arrays):
    return pl.pallas_call(
        last_kernel,
        out_shape=jax.ShapeDtypeStruct((256, 1024), F32),
        compiler_params=PARAMS,
    )(*arrays)


def fetch(plus, minus):
    return shift_y(plus, 1), shift_y(minus, -1)


def swap(pair):
    return tuple(shift(v, "c", 1) for v in pair)


def shards(
    student_in, norm_gain, w_query, w_key, w_value, w_out, projection, teacher_rows, lengths
):
    x, yh, c, yl, z = (lax.axis_index(a) for a in AXES)
    length = lengths[0]
    to_up = jnp.where(yl == 0, yh, 1 - yh)
    place = jnp.stack([z, yl, length, c, x, yh, to_up])

    def around(own):
        near, back = shift(own, "z", -1), shift(own, "z", 1)
        return [own, near, back], [shift(back[:64], "z", 1), shift(near[64:], "z", -1)]

    kv_own = jnp.concatenate([w_key, w_value], axis=1)

    def quarter(at):
        return jnp.concatenate([rows_of(w, at, 1024) for w in (w_query, w_key, w_value)], axis=1)

    quarters = quarter(c * 2048), quarter(c * 2048 + 1024)
    first = fetch(*quarters)
    inverse = ROPE_BASE ** (-2.0 * jnp.arange(HEAD_DIM // 2).astype(F32) / HEAD_DIM)
    pos = yl * 512 + ring_position(jnp.arange(512), z)
    angles = pos.astype(F32)[:, None] * inverse
    cosine, sine = jnp.cos(angles), jnp.sin(angles)
    cosine = jnp.concatenate([cosine, cosine], axis=1)
    sine = jnp.concatenate([-sine, sine], axis=1)
    pieces, ends = around(root_norm(after(student_in, *quarters), norm_gain))
    pieces = list(lax.optimization_barrier((*pieces, cosine, sine, kv_own))[:3])
    near_heads = own_heads_of(pieces, w_query, kv_own, cosine, sine)
    first = tuple(after(v, *ends, near_heads) for v in first)
    first_sib = swap(first)
    out_part = after(rows_of(w_out, c * 256, 256), *first)
    second = shift(out_part[:96], "yl", 1), cross_y(out_part[96:])
    ends = [after(v, near_heads) for v in ends]
    own_heads = own_heads_of(ends, w_query, kv_own, cosine, sine, near_heads)
    kv_early = shift(own_heads[:, 512:], "yl", 1)
    far_weights = [*first, *(after(v, own_heads) for v in first_sib)]
    far_heads = far_heads_of(place, pieces + ends, far_weights, cosine, sine)
    kv_late = shift(far_heads[:, 512:], "yl", 1)
    att_far = attend(place, far_heads, kv_early)
    second = tuple(after(v, far_heads) for v in second)
    second_sib = swap(second)
    kv_late = after(kv_late, att_far)
    att_own = attend(place, own_heads, kv_late)
    b0, b1, b2, b3 = out_blocks(place, att_own, att_far, w_out, [*second, *second_sib])

    proj_c = pick(projection.reshape(8, 2, 256, 1024), c, 1).reshape(2048, 1024)
    sends = lax.optimization_barrier((proj_c[:1024], proj_c[1024:], ends[0]))[:2]
    third = fetch(*(after(v, kv_late, *second) for v in sends))

    parts = [b0, shift(b3, "z", 2), shift(b1, "z", 1), shift(b2, "z", -1)]
    third_up, third_down, *parts = lax.optimization_barrier((*third, *parts))
    own_layer = make_layer(place, student_in, parts)
    teach_far = shift(after(rows_of(teacher_rows, (1 - yl) * 512, 512), own_layer), "yl", 1)
    layers, ends = around(own_layer)
    p_far = [third_up, third_down, shift(third_up, "c", 1), shift(third_down, "c", 1)]
    same = (projection, p_far, teacher_rows, teach_far)
    near = errors(1, place, layers, *same)
    ends = [after(v, near[0]) for v in ends]
    err_b, sq_b, mine, other = errors(1, place, ends, *same, earlier=near)
    theirs = shift(other, "c", 1)
    err_b_sib = shift(err_b, "c", 1)
    err_a, sq_a = errors(0, place, [mine, after(other, err_b)], *same)
    err_a_sib = shift(err_a, "c", 1)

    gb = gradient(False, place, mine, theirs, after(err_b, err_a), err_b_sib)
    squared = after(sq_a + sq_b, gb[0])
    squared = squared + shift(squared, "z", 1)
    ga = gradient(True, place, mine, theirs, after(err_a, gb[0], squared), err_a_sib)
    ga = [ga[0]] + [shift(ga[k], "x", k) for k in (1, 2, 3)]
    squared = squared + shift(squared, "z", 2)
    squared = squared + shift(squared, "yl", 1)
    seq_loss = squared.reshape(1) / (lengths.astype(F32) * DT)
    ga[0] = after(ga[0], seq_loss)
    gb = [gb[0], shift_y(gb[1], 2), shift_y(gb[2], 1), shift_y(gb[3], -1)]
    a = partial_sums(sum_x_kernel, place, ga)
    a = [a[0], shift_y(a[1], 2), shift_y(a[2], 1), shift_y(a[3], -1)]
    b = partial_sums(sum_y_kernel, place, gb)
    b = [b[0]] + [shift(b[k], "x", k) for k in (1, 2, 3)]
    return last_sum(a + b), seq_loss


def solution(mesh):
    split = Mesh(mesh.devices.reshape(4, 2, 2, 2, 4), AXES)
    dp, tensor = ("x", "yh", "c"), ("yl", "z")
    placed = (
        P(dp + tensor, None),
        P(),
        P(None, tensor),
        P(None, tensor),
        P(None, tensor),
        P(tensor, None),
        P(None, tensor),
        P(dp, tensor),
        P(dp),
    )
    return jax.shard_map(
        shards, mesh=split, in_specs=placed, out_specs=(P(dp, tensor), P(dp)), check_vma=False
    )
```

```python
import functools
import math

import jax
import jax.numpy as jnp
from jax import lax
from jax.experimental import pallas as pl
from jax.experimental.pallas import tpu as pltpu
from jax.sharding import Mesh, PartitionSpec as P

HEAD_DIM = 128
DT = 8192
EPSILON = 1e-05
ROPE_BASE = 500000.0
NEG_LARGE = -1e30
AXES = ("x", "yh", "c", "yl", "z")
SIZES = {"x": 4, "yh": 2, "c": 2, "yl": 2, "z": 4}
F32 = jnp.float32
BF16 = jnp.bfloat16
PARAMS = pltpu.CompilerParams(vmem_limit_bytes=48 * 2**20)


def shift(value, axis, step):
    count = SIZES[axis]
    return lax.ppermute(value, axis, [(i, (i + step) % count) for i in range(count)])


def shift_y(value, step):
    return lax.ppermute(value, ("yh", "yl"), [(i, (i + step) % 4) for i in range(4)])


def cross_y(value):
    return lax.ppermute(value, ("yh", "yl"), [(0, 3), (3, 0), (1, 2), (2, 1)])


def after(value, *others):
    return lax.optimization_barrier((value, *others))[0]


def rows_of(array, start, count):
    return lax.dynamic_slice_in_dim(array, start, count, 0)


def pick(array, at, axis):
    return lax.dynamic_index_in_dim(array, at, axis, keepdims=False)


def dot(left, right):
    return jnp.dot(left, right, preferred_element_type=F32)


def norm_kernel(in_ref, gain_ref, out_ref):
    widened = in_ref[...].astype(F32)
    mean_square = jnp.mean(widened * widened, axis=-1, keepdims=True)
    out_ref[...] = (widened * lax.rsqrt(mean_square + EPSILON) * gain_ref[...]).astype(BF16)


def root_norm(inputs, norm_gain):
    return pl.pallas_call(
        norm_kernel,
        grid=(4,),
        in_specs=[
            pl.BlockSpec((32, 4096), lambda i: (i, 0)),
            pl.BlockSpec((1, 4096), lambda i: (0, 0)),
        ],
        out_specs=pl.BlockSpec((32, 4096), lambda i: (i, 0)),
        out_shape=jax.ShapeDtypeStruct((128, 4096), BF16),
        compiler_params=PARAMS,
    )(inputs, norm_gain.reshape(1, 4096))


def ring_step(block):
    return block ^ (block // 2)


def ring_position(index, z):
    return ((z + ring_step(index // 128)) % 4) * 128 + index % 128


def turned(product, cosine, sine, last):
    def turn(head):
        return head * cosine + pltpu.roll(head, 64, 1) * sine

    left, right = product[:, :128], product[:, 128:]
    right = jnp.where(last, right, turn(right))
    return jnp.concatenate([turn(left), right], axis=1).astype(BF16)


def own_heads_kernel(*refs):
    *x_refs, q_ref, kv_ref, cos_ref, sin_ref, out_ref = refs
    x = jnp.concatenate([ref[...] for ref in x_refs if ref.shape[1] == 4096], axis=0)
    last = pl.program_id(0) == 2

    def finish(w_ref):
        out_ref[...] = turned(dot(x, w_ref[...]), cos_ref[...], sin_ref[...], last)

    pl.when(pl.program_id(0) < 2)(lambda: finish(q_ref))
    pl.when(last)(lambda: finish(kv_ref))


def own_heads_of(pieces, w_query, kv_own, cosine, sine, earlier=None):
    rows, at = sum(v.shape[0] for v in pieces), 0 if earlier is None else 3
    turn = pl.BlockSpec((rows, 128), lambda n: (at, 0))
    kept, alias = [], {}
    if earlier is not None:
        kept, alias = [earlier], {0: 0}
    return pl.pallas_call(
        own_heads_kernel,
        grid=(3,),
        in_specs=[pl.BlockSpec(memory_space=pl.ANY)] * len(kept)
        + [pl.BlockSpec(v.shape, lambda n: (0, 0)) for v in pieces]
        + [
            pl.BlockSpec((4096, 256), lambda n: (0, jnp.minimum(n, 1))),
            pl.BlockSpec((4096, 256), lambda n: (0, 0)),
            turn,
            turn,
        ],
        out_specs=pl.BlockSpec((rows, 256), lambda n: (at, n)),
        out_shape=jax.ShapeDtypeStruct((512, 768), BF16),
        input_output_aliases=alias,
        compiler_params=PARAMS,
    )(*kept, *pieces, w_query, kv_own, cosine, sine)


def placed(refs):
    start = 0
    for ref in refs:
        yield slice(start, start + ref.shape[0]), ref
        start += ref.shape[0]


def far_heads_kernel(at_ref, *refs):
    *pieces, w0, w1, w2, w3, cos_ref, sin_ref, out_ref, x_ref = refs
    core = at_ref[3]

    @pl.when(pl.program_id(0) == 0)
    def _():
        for here, ref in placed(pieces):
            for k in range(4):
                source = ((core + k // 2) % 2) * 2048 + (k % 2) * 1024
                x_ref[here, 1024 * k : 1024 * k + 1024] = ref[
                    :, pl.ds(pl.multiple_of(source, 1024), 1024)
                ]

    product = dot(x_ref[:, :1024], w0[...])
    for k, ref in ((1, w1), (2, w2), (3, w3)):
        product = product + dot(x_ref[:, 1024 * k : 1024 * k + 1024], ref[...])
    out_ref[...] = turned(product, cos_ref[...], sin_ref[...], pl.program_id(0) == 2)


def far_heads_of(place, pieces, quarters, cosine, sine):
    whole = [pl.BlockSpec(v.shape, lambda n, at: (0, 0)) for v in pieces]
    weight = pl.BlockSpec((1024, 256), lambda n, at: (0, n))
    turn = pl.BlockSpec((512, 128), lambda n, at: (0, 0))
    return pl.pallas_call(
        far_heads_kernel,
        grid_spec=pltpu.PrefetchScalarGridSpec(
            num_scalar_prefetch=1,
            grid=(3,),
            in_specs=whole + [weight] * 4 + [turn] * 2,
            out_specs=pl.BlockSpec((512, 256), lambda n, at: (0, n)),
            scratch_shapes=[pltpu.VMEM((512, 4096), BF16)],
        ),
        out_shape=jax.ShapeDtypeStruct((512, 768), BF16),
        compiler_params=PARAMS,
    )(place, *pieces, *quarters, cosine, sine)


def attend_kernel(at_ref, q_ref, own_ref, far_ref, out_ref):
    z, yl, length = at_ref[0], at_ref[1], at_ref[2]
    factor = math.log2(math.e) / math.sqrt(HEAD_DIM)
    q = jnp.concatenate([q_ref[:, 128 * h : 128 * h + 128] for h in range(4)], axis=0)
    shape = (512, 512)
    ring = ring_position(lax.broadcasted_iota(jnp.int32, (1, 512), 1), z)
    q_at = ((z + ring_step(pl.program_id(0))) % 4) * 128
    q_at = q_at + lax.broadcasted_iota(jnp.int32, (128, 1), 0)
    contract = (((1,), (1,)), ((), ()))

    def scores(kv_ref):
        return factor * lax.dot_general(q, kv_ref[:, :128], contract, preferred_element_type=F32)

    own_ok = (ring <= q_at) & (ring + yl * 512 < length)
    bias = jnp.where(jnp.broadcast_to(own_ok, (128, 512)), 0.0, NEG_LARGE)
    own = (scores(own_ref).reshape(4, 128, 512) + bias[None]).reshape(shape)
    top = jnp.max(own, axis=-1, keepdims=True)

    def store(total, blended):
        blended = (blended / total).astype(BF16)
        for h in range(4):
            out_ref[:, 128 * h : 128 * h + 128] = blended[128 * h : 128 * h + 128]

    @pl.when(yl == 0)
    def _():
        weights = jnp.exp2(own - top)
        store(
            jnp.sum(weights, axis=-1, keepdims=True), dot(weights.astype(BF16), own_ref[:, 128:])
        )

    @pl.when(yl == 1)
    def _():
        far = scores(far_ref) + jnp.where(ring < length, 0.0, NEG_LARGE)
        highest = jnp.maximum(top, jnp.max(far, axis=-1, keepdims=True))
        own_weights = jnp.exp2(own - highest)
        far_weights = jnp.exp2(far - highest)
        total = jnp.sum(own_weights, axis=-1, keepdims=True) + jnp.sum(
            far_weights, axis=-1, keepdims=True
        )
        store(
            total,
            dot(own_weights.astype(BF16), own_ref[:, 128:])
            + dot(far_weights.astype(BF16), far_ref[:, 128:]),
        )


def attend(place, heads, far_kv):
    return pl.pallas_call(
        attend_kernel,
        grid_spec=pltpu.PrefetchScalarGridSpec(
            num_scalar_prefetch=1,
            grid=(4,),
            in_specs=[
                pl.BlockSpec((128, 512), lambda j, at: (j, 0)),
                pl.BlockSpec((512, 256), lambda j, at: (0, 2)),
                pl.BlockSpec((512, 256), lambda j, at: (0, 0)),
            ],
            out_specs=pl.BlockSpec((128, 512), lambda j, at: (j, 0)),
        ),
        out_shape=jax.ShapeDtypeStruct((512, 512), BF16),
        compiler_params=PARAMS,
    )(place, heads, heads, far_kv)


def layer_kernel(at_ref, student_ref, *refs):
    *parts, out_ref = refs
    total = parts[0][...].astype(F32)
    for part in parts[1:]:
        total = total + part[...].astype(F32)
    layer = (student_ref[...].astype(F32) + total).astype(BF16)
    even = [layer[:, 512 * i : 512 * i + 256] for i in range(8)]
    odd = [layer[:, 512 * i + 256 : 512 * i + 512] for i in range(8)]

    @pl.when(at_ref[3] == 0)
    def _():
        out_ref[...] = jnp.concatenate(even + odd, axis=1)

    @pl.when(at_ref[3] == 1)
    def _():
        out_ref[...] = jnp.concatenate(odd + even, axis=1)


def make_layer(place, student_in, parts):
    spec = pl.BlockSpec((32, 4096), lambda i, at: (i, 0))
    return pl.pallas_call(
        layer_kernel,
        grid_spec=pltpu.PrefetchScalarGridSpec(
            num_scalar_prefetch=1, grid=(4,), in_specs=[spec] * 5, out_specs=spec
        ),
        out_shape=jax.ShapeDtypeStruct((128, 4096), BF16),
        compiler_params=PARAMS,
    )(place, student_in, *parts)


def out_kernel(at_ref, own, far, w, w0, w1, w2, w3, *refs):
    *out_refs, x_ref = refs

    @pl.when(pl.program_id(0) == 0)
    def _():
        x_ref[:, :512] = own[...]
        for k in range(2):
            source = ((at_ref[3] + k) % 2) * 256
            x_ref[:, 512 + 256 * k : 768 + 256 * k] = far[:, pl.ds(pl.multiple_of(source, 256), 256)]

    weights = jnp.concatenate([ref[...] for ref in (w, w0, w1, w2, w3)], axis=0)
    total = dot(x_ref[...], weights)
    for j, ref in enumerate(out_refs):
        ref[...] = total[128 * j : 128 * j + 128].astype(BF16)


def out_blocks(place, own, far, w_out, quarters):
    att = pl.BlockSpec((512, 512), lambda n, at: (0, 0))
    quarter = pl.BlockSpec((128, 1024), lambda n, at: (0, n))
    fetched = [pl.BlockSpec((v.shape[0], 1024), lambda n, at: (0, n)) for v in quarters]
    return pl.pallas_call(
        out_kernel,
        grid_spec=pltpu.PrefetchScalarGridSpec(
            num_scalar_prefetch=1,
            grid=(4,),
            in_specs=[att, att, pl.BlockSpec((512, 1024), lambda n, at: (0, n))] + fetched,
            out_specs=[quarter] * 4,
            scratch_shapes=[pltpu.VMEM((512, 1024), BF16)],
        ),
        out_shape=[jax.ShapeDtypeStruct((128, 4096), BF16)] * 4,
        compiler_params=PARAMS,
    )(place, own, far, w_out, *quarters)


def error_kernel(first, rows, kept, at_ref, *refs):
    layers = refs[kept:-13] if rows < 512 else refs[:2]
    p_own, f0, f1, f2, f3, t_own, t_far, err_ref, sum_ref = refs[len(layers) + kept :][:9]
    x_ref, n_ref = refs[-2:]
    step = pl.program_id(0)
    z, yl, length, core = at_ref[0], at_ref[1], at_ref[2], at_ref[3]

    @pl.when(step == 0)
    def _():
        if rows == 512:
            x_ref[:, :2048] = layers[0][...]
            x_ref[:, 2048:] = layers[1][...]
        else:
            for here, ref in placed(layers):
                x_ref[here, :] = ref[...]
            refs[-4][...] = x_ref[:, :2048]
            refs[-3][...] = x_ref[:, 2048:]
        for i in range(16):
            block = i // 2 + 8 * ((core + i) % 2)
            n_ref[:, 256 * i : 256 * i + 256] = x_ref[
                :, pl.ds(pl.multiple_of(block * 256, 256), 256)
            ]
        sum_ref[...] = refs[3][...] if kept else jnp.zeros((1, 1), F32)

    index = 128 * first + lax.broadcasted_iota(jnp.int32, (rows, 1), 0)
    pos = yl * 512 + ring_position(index, z)
    live = jnp.broadcast_to(pos < length, (rows, 256))

    def part(columns, predicted, t_ref):
        teacher = [
            t_ref[pl.ds(pl.multiple_of(((z + ring_step(first + j)) % 4) * 128, 128), 128), :]
            for j in range(rows // 128)
        ]
        residue = predicted - jnp.concatenate(teacher, axis=0).astype(F32)
        residue = jnp.where(live, residue, 0.0)
        err_ref[:, columns] = (residue / length.astype(F32)).astype(BF16)
        sum_ref[...] += jnp.sum(residue * residue).reshape(1, 1)

    part(slice(0, 256), dot(n_ref[...], p_own[...]), t_own)
    predicted = dot(x_ref[:, :1024], f0[...])
    for k, ref in ((1, f1), (2, f2), (3, f3)):
        predicted = predicted + dot(x_ref[:, 1024 * k : 1024 * k + 1024], ref[...])
    part(slice(256, 512), predicted, t_far)


def errors(half, place, layers, projection, p_far, t_own, t_far, earlier=()):
    rows = 512 if layers[0].shape[0] == 512 else sum(v.shape[0] for v in layers)
    first, kept = (3, 4) if earlier else (0, 0)

    def columns(n, at):
        return (0, 2 * half + n)

    def own_rows(n, at):
        return (at[1], 2 * half + n)

    def constant(n, at):
        return (0, 0)

    anywhere = pl.BlockSpec(memory_space=pl.ANY)
    kept_specs = [anywhere] * 3 + [pl.BlockSpec((1, 1), constant)] if earlier else []
    out_specs = [
        pl.BlockSpec((rows, 512), lambda n, at: (first, n)),
        pl.BlockSpec((1, 1), constant),
    ]
    out_shape = [
        jax.ShapeDtypeStruct((512, 1024), BF16),
        jax.ShapeDtypeStruct((1, 1), F32),
    ]
    if rows < 512:
        out_specs += [pl.BlockSpec((rows, 2048), lambda n, at: (first, 0))] * 2
        out_shape += [jax.ShapeDtypeStruct((512, 2048), BF16)] * 2
    if earlier:
        err, total, left, right = earlier
        earlier = (err, left, right, total)
    return pl.pallas_call(
        functools.partial(error_kernel, first, rows, kept),
        grid_spec=pltpu.PrefetchScalarGridSpec(
            num_scalar_prefetch=1,
            grid=(2,),
            in_specs=kept_specs
            + [pl.BlockSpec(v.shape, constant) for v in layers]
            + [pl.BlockSpec((4096, 256), columns)]
            + [pl.BlockSpec((1024, 256), columns)] * 4
            + [pl.BlockSpec((512, 256), own_rows), pl.BlockSpec((512, 256), columns)],
            out_specs=out_specs,
            scratch_shapes=[pltpu.VMEM((rows, 4096), BF16)] * 2,
        ),
        out_shape=out_shape,
        input_output_aliases={1: 0, 2: 2, 3: 3} if earlier else {},
        compiler_params=PARAMS,
    )(place, *earlier, *layers, projection, *p_far, t_own, t_far)


def split_columns(product):
    own = jnp.concatenate([product[:, :256], product[:, 512:768]], axis=1)
    far = jnp.concatenate([product[:, 256:512], product[:, 768:]], axis=1)
    return own, far


def by_y(at_ref, own, far, store):
    for t in (0, 1):
        this, that = slice(256 * t, 256 * t + 256), slice(256 - 256 * t, 512 - 256 * t)

        @pl.when(at_ref[5] == t)
        def _():
            store(0, own[this])
            store(1, own[that])

        @pl.when(at_ref[6] == t)
        def _():
            store(2, far[this])
            store(3, far[that])


def gradient_kernel(by_x, at_ref, mine, theirs, e_mine, e_theirs, *out_refs):
    contract = (((0,), (0,)), ((), ()))
    product = lax.dot_general(mine[...], e_mine[...], contract, preferred_element_type=F32)
    product = product + lax.dot_general(
        theirs[...], e_theirs[...], contract, preferred_element_type=F32
    )
    product = product.astype(BF16)
    if by_x:
        for k, ref in enumerate(out_refs):

            @pl.when(pl.program_id(0) == k)
            def _():
                ref[...] = product
    else:

        def store(k, value):
            out_refs[k][0] = value

        by_y(at_ref, *split_columns(product), store)


def gradient(by_x, place, mine, theirs, e_mine, e_theirs):
    rows = pl.BlockSpec((512, 512), lambda k, at: (0, (at[4] + k) % 4))
    error = pl.BlockSpec((512, 1024), lambda k, at: (0, 0))
    if by_x:
        out_spec = pl.BlockSpec((512, 1024), lambda k, at: (0, 0))
        shape = (512, 1024)
    else:
        out_spec = pl.BlockSpec((1, 256, 512), lambda k, at: (k, 0, 0))
        shape = (4, 256, 512)
    return pl.pallas_call(
        functools.partial(gradient_kernel, by_x),
        grid_spec=pltpu.PrefetchScalarGridSpec(
            num_scalar_prefetch=1,
            grid=(4,),
            in_specs=[rows, rows, error, error],
            out_specs=[out_spec] * 4,
        ),
        out_shape=[jax.ShapeDtypeStruct(shape, BF16)] * 4,
        compiler_params=PARAMS,
    )(place, mine, theirs, e_mine, e_theirs)


def total_of(refs):
    total = refs[0][...].astype(F32)
    for ref in refs[1:]:
        total = total + ref[...].astype(F32)
    return total


def sum_x_kernel(at_ref, *refs):
    def store(k, value):
        refs[4 + k][...] = value

    by_y(at_ref, *split_columns(total_of(refs[:4]).astype(BF16)), store)


def sum_y_kernel(at_ref, *refs):
    total = total_of(refs[:4]).astype(BF16)
    for k in range(4):
        refs[4 + k][...] = total[k]


def partial_sums(kernel, place, arrays):
    return pl.pallas_call(
        kernel,
        grid_spec=pltpu.PrefetchScalarGridSpec(
            num_scalar_prefetch=1,
            grid=(1,),
            in_specs=[pl.BlockSpec(memory_space=pltpu.VMEM)] * 4,
            out_specs=[pl.BlockSpec(memory_space=pltpu.VMEM)] * 4,
        ),
        out_shape=[jax.ShapeDtypeStruct((256, 512), BF16)] * 4,
        compiler_params=PARAMS,
    )(place, *arrays)


def last_kernel(*refs):
    refs[8][:, :512] = total_of(refs[:4])
    refs[8][:, 512:] = total_of(refs[4:8])


def last_sum(arrays):
    return pl.pallas_call(
        last_kernel,
        out_shape=jax.ShapeDtypeStruct((256, 1024), F32),
        compiler_params=PARAMS,
    )(*arrays)


def fetch(plus, minus):
    return shift_y(plus, 1), shift_y(minus, -1)


def swap(pair):
    return tuple(shift(v, "c", 1) for v in pair)


def shards(
    student_in, norm_gain, w_query, w_key, w_value, w_out, projection, teacher_rows, lengths
):
    x, yh, c, yl, z = (lax.axis_index(a) for a in AXES)
    length = lengths[0]
    to_up = jnp.where(yl == 0, yh, 1 - yh)
    place = jnp.stack([z, yl, length, c, x, yh, to_up])

    def around(own):
        near, back = shift(own, "z", -1), shift(own, "z", 1)
        return [own, near, back], [shift(back[:64], "z", 1), shift(near[64:], "z", -1)]

    kv_own = jnp.concatenate([w_key, w_value], axis=1)

    def quarter(at):
        return jnp.concatenate([rows_of(w, at, 1024) for w in (w_query, w_key, w_value)], axis=1)

    quarters = quarter(c * 2048), quarter(c * 2048 + 1024)
    first = fetch(*quarters)
    inverse = ROPE_BASE ** (-2.0 * jnp.arange(HEAD_DIM // 2).astype(F32) / HEAD_DIM)
    pos = yl * 512 + ring_position(jnp.arange(512), z)
    angles = pos.astype(F32)[:, None] * inverse
    cosine, sine = jnp.cos(angles), jnp.sin(angles)
    cosine = jnp.concatenate([cosine, cosine], axis=1)
    sine = jnp.concatenate([-sine, sine], axis=1)
    pieces, ends = around(root_norm(after(student_in, *quarters), norm_gain))
    pieces = list(lax.optimization_barrier((*pieces, cosine, sine, kv_own))[:3])
    near_heads = own_heads_of(pieces, w_query, kv_own, cosine, sine)
    first = tuple(after(v, *ends, near_heads) for v in first)
    first_sib = swap(first)
    out_part = after(rows_of(w_out, c * 256, 256), *first)
    second = shift(out_part[:96], "yl", 1), cross_y(out_part[96:])
    ends = [after(v, near_heads) for v in ends]
    own_heads = own_heads_of(ends, w_query, kv_own, cosine, sine, near_heads)
    kv_early = shift(own_heads[:, 512:], "yl", 1)
    far_weights = [*first, *(after(v, own_heads) for v in first_sib)]
    far_heads = far_heads_of(place, pieces + ends, far_weights, cosine, sine)
    kv_late = shift(far_heads[:, 512:], "yl", 1)
    att_far = attend(place, far_heads, kv_early)
    second = tuple(after(v, att_far) for v in second)
    second_sib = swap(second)
    kv_late = after(kv_late, att_far)
    att_own = attend(place, own_heads, kv_late)
    b0, b1, b2, b3 = out_blocks(place, att_own, att_far, w_out, [*second, *second_sib])

    proj_c = pick(projection.reshape(8, 2, 256, 1024), c, 1).reshape(2048, 1024)
    sends = lax.optimization_barrier((proj_c[:1024], proj_c[1024:], ends[0]))[:2]
    third = fetch(*(after(v, kv_late, *second) for v in sends))

    parts = [b0, shift(b3, "z", 2), shift(b1, "z", 1), shift(b2, "z", -1)]
    third_up, third_down, *parts = lax.optimization_barrier((*third, *parts))
    own_layer = make_layer(place, student_in, parts)
    teach_far = shift(after(rows_of(teacher_rows, (1 - yl) * 512, 512), own_layer), "yl", 1)
    layers, ends = around(own_layer)
    p_far = [third_up, third_down, shift(third_up, "c", 1), shift(third_down, "c", 1)]
    same = (projection, p_far, teacher_rows, teach_far)
    near = errors(1, place, layers, *same)
    ends = [after(v, near[0]) for v in ends]
    err_b, sq_b, mine, other = errors(1, place, ends, *same, earlier=near)
    theirs = shift(other, "c", 1)
    err_b_sib = shift(err_b, "c", 1)
    err_a, sq_a = errors(0, place, [mine, after(other, err_b)], *same)
    err_a_sib = shift(err_a, "c", 1)

    gb = gradient(False, place, mine, theirs, after(err_b, err_a), err_b_sib)
    squared = after(sq_a + sq_b, gb[0])
    squared = squared + shift(squared, "z", 1)
    ga = gradient(True, place, mine, theirs, after(err_a, gb[0], squared), err_a_sib)
    ga = [ga[0]] + [shift(ga[k], "x", k) for k in (1, 2, 3)]
    squared = squared + shift(squared, "z", 2)
    squared = squared + shift(squared, "yl", 1)
    seq_loss = squared.reshape(1) / (lengths.astype(F32) * DT)
    ga[0] = after(ga[0], seq_loss)
    gb = [gb[0], shift_y(gb[1], 2), shift_y(gb[2], 1), shift_y(gb[3], -1)]
    a = partial_sums(sum_x_kernel, place, ga)
    a = [a[0], shift_y(a[1], 2), shift_y(a[2], 1), shift_y(a[3], -1)]
    b = partial_sums(sum_y_kernel, place, gb)
    b = [b[0]] + [shift(b[k], "x", k) for k in (1, 2, 3)]
    return last_sum(a + b), seq_loss


def solution(mesh):
    split = Mesh(mesh.devices.reshape(4, 2, 2, 2, 4), AXES)
    dp, tensor = ("x", "yh", "c"), ("yl", "z")
    placed = (
        P(dp + tensor, None),
        P(),
        P(None, tensor),
        P(None, tensor),
        P(None, tensor),
        P(tensor, None),
        P(None, tensor),
        P(dp, tensor),
        P(dp),
    )
    return jax.shard_map(
        shards, mesh=split, in_specs=placed, out_specs=(P(dp, tensor), P(dp)), check_vma=False
    )
```

```python
import functools
import math

import jax
import jax.numpy as jnp
from jax import lax
from jax.experimental import pallas as pl
from jax.experimental.pallas import tpu as pltpu
from jax.sharding import Mesh, PartitionSpec as P

HEAD_DIM = 128
DT = 8192
EPSILON = 1e-05
ROPE_BASE = 500000.0
NEG_LARGE = -1e30
AXES = ("x", "yh", "c", "yl", "z")
SIZES = {"x": 4, "yh": 2, "c": 2, "yl": 2, "z": 4}
F32 = jnp.float32
BF16 = jnp.bfloat16
PARAMS = pltpu.CompilerParams(vmem_limit_bytes=48 * 2**20)


def shift(value, axis, step):
    count = SIZES[axis]
    return lax.ppermute(value, axis, [(i, (i + step) % count) for i in range(count)])


def shift_y(value, step):
    return lax.ppermute(value, ("yh", "yl"), [(i, (i + step) % 4) for i in range(4)])


def cross_y(value):
    return lax.ppermute(value, ("yh", "yl"), [(0, 3), (3, 0), (1, 2), (2, 1)])


def after(value, *others):
    return lax.optimization_barrier((value, *others))[0]


def rows_of(array, start, count):
    return lax.dynamic_slice_in_dim(array, start, count, 0)


def pick(array, at, axis):
    return lax.dynamic_index_in_dim(array, at, axis, keepdims=False)


def dot(left, right):
    return jnp.dot(left, right, preferred_element_type=F32)


def norm_kernel(in_ref, gain_ref, out_ref):
    widened = in_ref[...].astype(F32)
    mean_square = jnp.mean(widened * widened, axis=-1, keepdims=True)
    out_ref[...] = (widened * lax.rsqrt(mean_square + EPSILON) * gain_ref[...]).astype(BF16)


def root_norm(inputs, norm_gain):
    return pl.pallas_call(
        norm_kernel,
        grid=(4,),
        in_specs=[
            pl.BlockSpec((32, 4096), lambda i: (i, 0)),
            pl.BlockSpec((1, 4096), lambda i: (0, 0)),
        ],
        out_specs=pl.BlockSpec((32, 4096), lambda i: (i, 0)),
        out_shape=jax.ShapeDtypeStruct((128, 4096), BF16),
        compiler_params=PARAMS,
    )(inputs, norm_gain.reshape(1, 4096))


def ring_step(block):
    return block ^ (block // 2)


def ring_position(index, z):
    return ((z + ring_step(index // 128)) % 4) * 128 + index % 128


def turned(product, cosine, sine, last):
    def turn(head):
        return head * cosine + pltpu.roll(head, 64, 1) * sine

    left, right = product[:, :128], product[:, 128:]
    right = jnp.where(last, right, turn(right))
    return jnp.concatenate([turn(left), right], axis=1).astype(BF16)


def own_heads_kernel(*refs):
    *x_refs, q_ref, kv_ref, cos_ref, sin_ref, out_ref = refs
    x = jnp.concatenate([ref[...] for ref in x_refs if ref.shape[1] == 4096], axis=0)
    last = pl.program_id(0) == 2

    def finish(w_ref):
        out_ref[...] = turned(dot(x, w_ref[...]), cos_ref[...], sin_ref[...], last)

    pl.when(pl.program_id(0) < 2)(lambda: finish(q_ref))
    pl.when(last)(lambda: finish(kv_ref))


def own_heads_of(pieces, w_query, kv_own, cosine, sine, earlier=None):
    rows, at = sum(v.shape[0] for v in pieces), 0 if earlier is None else 3
    turn = pl.BlockSpec((rows, 128), lambda n: (at, 0))
    kept, alias = [], {}
    if earlier is not None:
        kept, alias = [earlier], {0: 0}
    return pl.pallas_call(
        own_heads_kernel,
        grid=(3,),
        in_specs=[pl.BlockSpec(memory_space=pl.ANY)] * len(kept)
        + [pl.BlockSpec(v.shape, lambda n: (0, 0)) for v in pieces]
        + [
            pl.BlockSpec((4096, 256), lambda n: (0, jnp.minimum(n, 1))),
            pl.BlockSpec((4096, 256), lambda n: (0, 0)),
            turn,
            turn,
        ],
        out_specs=pl.BlockSpec((rows, 256), lambda n: (at, n)),
        out_shape=jax.ShapeDtypeStruct((512, 768), BF16),
        input_output_aliases=alias,
        compiler_params=PARAMS,
    )(*kept, *pieces, w_query, kv_own, cosine, sine)


def placed(refs):
    start = 0
    for ref in refs:
        yield slice(start, start + ref.shape[0]), ref
        start += ref.shape[0]


def far_heads_kernel(at_ref, *refs):
    *pieces, w0, w1, w2, w3, cos_ref, sin_ref, out_ref, x_ref = refs
    core = at_ref[3]

    @pl.when(pl.program_id(0) == 0)
    def _():
        for here, ref in placed(pieces):
            for k in range(4):
                source = ((core + k // 2) % 2) * 2048 + (k % 2) * 1024
                x_ref[here, 1024 * k : 1024 * k + 1024] = ref[
                    :, pl.ds(pl.multiple_of(source, 1024), 1024)
                ]

    product = dot(x_ref[:, :1024], w0[...])
    for k, ref in ((1, w1), (2, w2), (3, w3)):
        product = product + dot(x_ref[:, 1024 * k : 1024 * k + 1024], ref[...])
    out_ref[...] = turned(product, cos_ref[...], sin_ref[...], pl.program_id(0) == 2)


def far_heads_of(place, pieces, quarters, cosine, sine):
    whole = [pl.BlockSpec(v.shape, lambda n, at: (0, 0)) for v in pieces]
    weight = pl.BlockSpec((1024, 256), lambda n, at: (0, n))
    turn = pl.BlockSpec((512, 128), lambda n, at: (0, 0))
    return pl.pallas_call(
        far_heads_kernel,
        grid_spec=pltpu.PrefetchScalarGridSpec(
            num_scalar_prefetch=1,
            grid=(3,),
            in_specs=whole + [weight] * 4 + [turn] * 2,
            out_specs=pl.BlockSpec((512, 256), lambda n, at: (0, n)),
            scratch_shapes=[pltpu.VMEM((512, 4096), BF16)],
        ),
        out_shape=jax.ShapeDtypeStruct((512, 768), BF16),
        compiler_params=PARAMS,
    )(place, *pieces, *quarters, cosine, sine)


def attend_kernel(at_ref, q_ref, own_ref, far_ref, out_ref):
    z, yl, length = at_ref[0], at_ref[1], at_ref[2]
    factor = math.log2(math.e) / math.sqrt(HEAD_DIM)
    q = jnp.concatenate([q_ref[:, 128 * h : 128 * h + 128] for h in range(4)], axis=0)
    shape = (512, 512)
    ring = ring_position(lax.broadcasted_iota(jnp.int32, (1, 512), 1), z)
    q_at = ((z + ring_step(pl.program_id(0))) % 4) * 128
    q_at = q_at + lax.broadcasted_iota(jnp.int32, (128, 1), 0)
    contract = (((1,), (1,)), ((), ()))

    def scores(kv_ref):
        return factor * lax.dot_general(q, kv_ref[:, :128], contract, preferred_element_type=F32)

    own_ok = (ring <= q_at) & (ring + yl * 512 < length)
    bias = jnp.where(jnp.broadcast_to(own_ok, (128, 512)), 0.0, NEG_LARGE)
    own = (scores(own_ref).reshape(4, 128, 512) + bias[None]).reshape(shape)
    top = jnp.max(own, axis=-1, keepdims=True)

    def store(total, blended):
        blended = (blended / total).astype(BF16)
        for h in range(4):
            out_ref[:, 128 * h : 128 * h + 128] = blended[128 * h : 128 * h + 128]

    @pl.when(yl == 0)
    def _():
        weights = jnp.exp2(own - top)
        store(
            jnp.sum(weights, axis=-1, keepdims=True), dot(weights.astype(BF16), own_ref[:, 128:])
        )

    @pl.when(yl == 1)
    def _():
        far = scores(far_ref) + jnp.where(ring < length, 0.0, NEG_LARGE)
        highest = jnp.maximum(top, jnp.max(far, axis=-1, keepdims=True))
        own_weights = jnp.exp2(own - highest)
        far_weights = jnp.exp2(far - highest)
        total = jnp.sum(own_weights, axis=-1, keepdims=True) + jnp.sum(
            far_weights, axis=-1, keepdims=True
        )
        store(
            total,
            dot(own_weights.astype(BF16), own_ref[:, 128:])
            + dot(far_weights.astype(BF16), far_ref[:, 128:]),
        )


def attend(place, heads, far_kv):
    return pl.pallas_call(
        attend_kernel,
        grid_spec=pltpu.PrefetchScalarGridSpec(
            num_scalar_prefetch=1,
            grid=(4,),
            in_specs=[
                pl.BlockSpec((128, 512), lambda j, at: (j, 0)),
                pl.BlockSpec((512, 256), lambda j, at: (0, 2)),
                pl.BlockSpec((512, 256), lambda j, at: (0, 0)),
            ],
            out_specs=pl.BlockSpec((128, 512), lambda j, at: (j, 0)),
        ),
        out_shape=jax.ShapeDtypeStruct((512, 512), BF16),
        compiler_params=PARAMS,
    )(place, heads, heads, far_kv)


def layer_kernel(at_ref, student_ref, *refs):
    *parts, out_ref = refs
    total = parts[0][...].astype(F32)
    for part in parts[1:]:
        total = total + part[...].astype(F32)
    layer = (student_ref[...].astype(F32) + total).astype(BF16)
    even = [layer[:, 512 * i : 512 * i + 256] for i in range(8)]
    odd = [layer[:, 512 * i + 256 : 512 * i + 512] for i in range(8)]

    @pl.when(at_ref[3] == 0)
    def _():
        out_ref[...] = jnp.concatenate(even + odd, axis=1)

    @pl.when(at_ref[3] == 1)
    def _():
        out_ref[...] = jnp.concatenate(odd + even, axis=1)


def make_layer(place, student_in, parts):
    spec = pl.BlockSpec((32, 4096), lambda i, at: (i, 0))
    return pl.pallas_call(
        layer_kernel,
        grid_spec=pltpu.PrefetchScalarGridSpec(
            num_scalar_prefetch=1, grid=(4,), in_specs=[spec] * 5, out_specs=spec
        ),
        out_shape=jax.ShapeDtypeStruct((128, 4096), BF16),
        compiler_params=PARAMS,
    )(place, student_in, *parts)


def out_kernel(at_ref, own, far, w, w0, w1, w2, w3, *refs):
    *out_refs, x_ref = refs

    @pl.when(pl.program_id(0) == 0)
    def _():
        x_ref[:, :512] = own[...]
        for k in range(2):
            source = ((at_ref[3] + k) % 2) * 256
            x_ref[:, 512 + 256 * k : 768 + 256 * k] = far[:, pl.ds(pl.multiple_of(source, 256), 256)]

    weights = jnp.concatenate([ref[...] for ref in (w, w0, w1, w2, w3)], axis=0)
    total = dot(x_ref[...], weights)
    for j, ref in enumerate(out_refs):
        ref[...] = total[128 * j : 128 * j + 128].astype(BF16)


def out_blocks(place, own, far, w_out, quarters):
    att = pl.BlockSpec((512, 512), lambda n, at: (0, 0))
    quarter = pl.BlockSpec((128, 1024), lambda n, at: (0, n))
    fetched = [pl.BlockSpec((v.shape[0], 1024), lambda n, at: (0, n)) for v in quarters]
    return pl.pallas_call(
        out_kernel,
        grid_spec=pltpu.PrefetchScalarGridSpec(
            num_scalar_prefetch=1,
            grid=(4,),
            in_specs=[att, att, pl.BlockSpec((512, 1024), lambda n, at: (0, n))] + fetched,
            out_specs=[quarter] * 4,
            scratch_shapes=[pltpu.VMEM((512, 1024), BF16)],
        ),
        out_shape=[jax.ShapeDtypeStruct((128, 4096), BF16)] * 4,
        compiler_params=PARAMS,
    )(place, own, far, w_out, *quarters)


def error_kernel(first, rows, kept, at_ref, *refs):
    layers = refs[kept:-13] if rows < 512 else refs[:2]
    p_own, f0, f1, f2, f3, t_own, t_far, err_ref, sum_ref = refs[len(layers) + kept :][:9]
    x_ref, n_ref = refs[-2:]
    step = pl.program_id(0)
    z, yl, length, core = at_ref[0], at_ref[1], at_ref[2], at_ref[3]

    @pl.when(step == 0)
    def _():
        if rows == 512:
            x_ref[:, :2048] = layers[0][...]
            x_ref[:, 2048:] = layers[1][...]
        else:
            for here, ref in placed(layers):
                x_ref[here, :] = ref[...]
            refs[-4][...] = x_ref[:, :2048]
            refs[-3][...] = x_ref[:, 2048:]
        for i in range(16):
            block = i // 2 + 8 * ((core + i) % 2)
            n_ref[:, 256 * i : 256 * i + 256] = x_ref[
                :, pl.ds(pl.multiple_of(block * 256, 256), 256)
            ]
        sum_ref[...] = refs[3][...] if kept else jnp.zeros((1, 1), F32)

    index = 128 * first + lax.broadcasted_iota(jnp.int32, (rows, 1), 0)
    pos = yl * 512 + ring_position(index, z)
    live = jnp.broadcast_to(pos < length, (rows, 256))

    def part(columns, predicted, t_ref):
        teacher = [
            t_ref[pl.ds(pl.multiple_of(((z + ring_step(first + j)) % 4) * 128, 128), 128), :]
            for j in range(rows // 128)
        ]
        residue = predicted - jnp.concatenate(teacher, axis=0).astype(F32)
        residue = jnp.where(live, residue, 0.0)
        err_ref[:, columns] = (residue / length.astype(F32)).astype(BF16)
        sum_ref[...] += jnp.sum(residue * residue).reshape(1, 1)

    part(slice(0, 256), dot(n_ref[...], p_own[...]), t_own)
    predicted = dot(x_ref[:, :1024], f0[...])
    for k, ref in ((1, f1), (2, f2), (3, f3)):
        predicted = predicted + dot(x_ref[:, 1024 * k : 1024 * k + 1024], ref[...])
    part(slice(256, 512), predicted, t_far)


def errors(half, place, layers, projection, p_far, t_own, t_far, earlier=()):
    rows = 512 if layers[0].shape[0] == 512 else sum(v.shape[0] for v in layers)
    first, kept = (3, 4) if earlier else (0, 0)

    def columns(n, at):
        return (0, 2 * half + n)

    def own_rows(n, at):
        return (at[1], 2 * half + n)

    def constant(n, at):
        return (0, 0)

    anywhere = pl.BlockSpec(memory_space=pl.ANY)
    kept_specs = [anywhere] * 3 + [pl.BlockSpec((1, 1), constant)] if earlier else []
    out_specs = [
        pl.BlockSpec((rows, 512), lambda n, at: (first, n)),
        pl.BlockSpec((1, 1), constant),
    ]
    out_shape = [
        jax.ShapeDtypeStruct((512, 1024), BF16),
        jax.ShapeDtypeStruct((1, 1), F32),
    ]
    if rows < 512:
        out_specs += [pl.BlockSpec((rows, 2048), lambda n, at: (first, 0))] * 2
        out_shape += [jax.ShapeDtypeStruct((512, 2048), BF16)] * 2
    if earlier:
        err, total, left, right = earlier
        earlier = (err, left, right, total)
    return pl.pallas_call(
        functools.partial(error_kernel, first, rows, kept),
        grid_spec=pltpu.PrefetchScalarGridSpec(
            num_scalar_prefetch=1,
            grid=(2,),
            in_specs=kept_specs
            + [pl.BlockSpec(v.shape, constant) for v in layers]
            + [pl.BlockSpec((4096, 256), columns)]
            + [pl.BlockSpec((1024, 256), columns)] * 4
            + [pl.BlockSpec((512, 256), own_rows), pl.BlockSpec((512, 256), columns)],
            out_specs=out_specs,
            scratch_shapes=[pltpu.VMEM((rows, 4096), BF16)] * 2,
        ),
        out_shape=out_shape,
        input_output_aliases={1: 0, 2: 2, 3: 3} if earlier else {},
        compiler_params=PARAMS,
    )(place, *earlier, *layers, projection, *p_far, t_own, t_far)


def split_columns(product):
    own = jnp.concatenate([product[:, :256], product[:, 512:768]], axis=1)
    far = jnp.concatenate([product[:, 256:512], product[:, 768:]], axis=1)
    return own, far


def by_y(at_ref, own, far, store):
    for t in (0, 1):
        this, that = slice(256 * t, 256 * t + 256), slice(256 - 256 * t, 512 - 256 * t)

        @pl.when(at_ref[5] == t)
        def _():
            store(0, own[this])
            store(1, own[that])

        @pl.when(at_ref[6] == t)
        def _():
            store(2, far[this])
            store(3, far[that])


def gradient_kernel(by_x, at_ref, mine, theirs, e_mine, e_theirs, *out_refs):
    contract = (((0,), (0,)), ((), ()))
    product = lax.dot_general(mine[...], e_mine[...], contract, preferred_element_type=F32)
    product = product + lax.dot_general(
        theirs[...], e_theirs[...], contract, preferred_element_type=F32
    )
    product = product.astype(BF16)
    if by_x:
        for k, ref in enumerate(out_refs):

            @pl.when(pl.program_id(0) == k)
            def _():
                ref[...] = product
    else:

        def store(k, value):
            out_refs[k][0] = value

        by_y(at_ref, *split_columns(product), store)


def gradient(by_x, place, mine, theirs, e_mine, e_theirs):
    rows = pl.BlockSpec((512, 512), lambda k, at: (0, (at[4] + k) % 4))
    error = pl.BlockSpec((512, 1024), lambda k, at: (0, 0))
    if by_x:
        out_spec = pl.BlockSpec((512, 1024), lambda k, at: (0, 0))
        shape = (512, 1024)
    else:
        out_spec = pl.BlockSpec((1, 256, 512), lambda k, at: (k, 0, 0))
        shape = (4, 256, 512)
    return pl.pallas_call(
        functools.partial(gradient_kernel, by_x),
        grid_spec=pltpu.PrefetchScalarGridSpec(
            num_scalar_prefetch=1,
            grid=(4,),
            in_specs=[rows, rows, error, error],
            out_specs=[out_spec] * 4,
        ),
        out_shape=[jax.ShapeDtypeStruct(shape, BF16)] * 4,
        compiler_params=PARAMS,
    )(place, mine, theirs, e_mine, e_theirs)


def total_of(refs):
    total = refs[0][...].astype(F32)
    for ref in refs[1:]:
        total = total + ref[...].astype(F32)
    return total


def sum_x_kernel(at_ref, *refs):
    def store(k, value):
        refs[4 + k][...] = value

    by_y(at_ref, *split_columns(total_of(refs[:4]).astype(BF16)), store)


def sum_y_kernel(at_ref, *refs):
    total = total_of(refs[:4]).astype(BF16)
    for k in range(4):
        refs[4 + k][...] = total[k]


def partial_sums(kernel, place, arrays):
    return pl.pallas_call(
        kernel,
        grid_spec=pltpu.PrefetchScalarGridSpec(
            num_scalar_prefetch=1,
            grid=(1,),
            in_specs=[pl.BlockSpec(memory_space=pltpu.VMEM)] * 4,
            out_specs=[pl.BlockSpec(memory_space=pltpu.VMEM)] * 4,
        ),
        out_shape=[jax.ShapeDtypeStruct((256, 512), BF16)] * 4,
        compiler_params=PARAMS,
    )(place, *arrays)


def last_kernel(*refs):
    refs[8][:, :512] = total_of(refs[:4])
    refs[8][:, 512:] = total_of(refs[4:8])


def last_sum(arrays):
    return pl.pallas_call(
        last_kernel,
        out_shape=jax.ShapeDtypeStruct((256, 1024), F32),
        compiler_params=PARAMS,
    )(*arrays)


def fetch(plus, minus):
    return shift_y(plus, 1), shift_y(minus, -1)


def swap(pair):
    return tuple(shift(v, "c", 1) for v in pair)


def shards(
    student_in, norm_gain, w_query, w_key, w_value, w_out, projection, teacher_rows, lengths
):
    x, yh, c, yl, z = (lax.axis_index(a) for a in AXES)
    length = lengths[0]
    to_up = jnp.where(yl == 0, yh, 1 - yh)
    place = jnp.stack([z, yl, length, c, x, yh, to_up])

    def around(own):
        near, back = shift(own, "z", -1), shift(own, "z", 1)
        return [own, near, back], [shift(back[:64], "z", 1), shift(near[64:], "z", -1)]

    kv_own = jnp.concatenate([w_key, w_value], axis=1)

    def quarter(at):
        return jnp.concatenate([rows_of(w, at, 1024) for w in (w_query, w_key, w_value)], axis=1)

    quarters = quarter(c * 2048), quarter(c * 2048 + 1024)
    first = fetch(*quarters)
    inverse = ROPE_BASE ** (-2.0 * jnp.arange(HEAD_DIM // 2).astype(F32) / HEAD_DIM)
    pos = yl * 512 + ring_position(jnp.arange(512), z)
    angles = pos.astype(F32)[:, None] * inverse
    cosine, sine = jnp.cos(angles), jnp.sin(angles)
    cosine = jnp.concatenate([cosine, cosine], axis=1)
    sine = jnp.concatenate([-sine, sine], axis=1)
    pieces, ends = around(root_norm(after(student_in, *quarters), norm_gain))
    proj_c = pick(projection.reshape(8, 2, 256, 1024), c, 1).reshape(2048, 1024)
    sends = proj_c[:1024], proj_c[1024:]
    out_sends = rows_of(w_out, c * 256, 96), rows_of(w_out, c * 256 + 96, 160)
    *pieces, cosine, sine, kv_own, s0, s1, o0, o1 = lax.optimization_barrier(
        (*pieces, cosine, sine, kv_own, *sends, *out_sends)
    )
    sends, out_sends = (s0, s1), (o0, o1)
    near_heads = own_heads_of(pieces, w_query, kv_own, cosine, sine)
    first = tuple(after(v, *ends, near_heads) for v in first)
    first_sib = swap(first)
    out_sends = [after(v, *first) for v in out_sends]
    second = shift(out_sends[0], "yl", 1), cross_y(out_sends[1])
    ends = [after(v, near_heads) for v in ends]
    own_heads = own_heads_of(ends, w_query, kv_own, cosine, sine, near_heads)
    kv_early = shift(own_heads[:, 512:], "yl", 1)
    far_weights = [*first, *(after(v, own_heads) for v in first_sib)]
    far_heads = far_heads_of(place, pieces + ends, far_weights, cosine, sine)
    kv_late = shift(far_heads[:, 512:], "yl", 1)
    att_far = attend(place, far_heads, kv_early)
    second = tuple(after(v, att_far) for v in second)
    second_sib = swap(second)
    kv_late = after(kv_late, att_far)
    att_own = attend(place, own_heads, kv_late)
    b0, b1, b2, b3 = out_blocks(place, att_own, att_far, w_out, [*second, *second_sib])

    third = fetch(*(after(v, kv_late, *second) for v in sends))

    parts = [b0, shift(b3, "z", 2), shift(b1, "z", 1), shift(b2, "z", -1)]
    third_up, third_down, *parts = lax.optimization_barrier((*third, *parts))
    own_layer = make_layer(place, student_in, parts)
    teach_far = shift(after(rows_of(teacher_rows, (1 - yl) * 512, 512), own_layer), "yl", 1)
    layers, ends = around(own_layer)
    p_far = [third_up, third_down, shift(third_up, "c", 1), shift(third_down, "c", 1)]
    same = (projection, p_far, teacher_rows, teach_far)
    near = errors(1, place, layers, *same)
    ends = [after(v, near[0]) for v in ends]
    err_b, sq_b, mine, other = errors(1, place, ends, *same, earlier=near)
    theirs = shift(other, "c", 1)
    err_b_sib = shift(err_b, "c", 1)
    err_a, sq_a = errors(0, place, [mine, after(other, err_b)], *same)
    err_a_sib = shift(err_a, "c", 1)

    gb = gradient(False, place, mine, theirs, after(err_b, err_a), err_b_sib)
    squared = after(sq_a + sq_b, gb[0])
    squared = squared + shift(squared, "z", 1)
    ga = gradient(True, place, mine, theirs, after(err_a, gb[0], squared), err_a_sib)
    ga = [ga[0]] + [shift(ga[k], "x", k) for k in (1, 2, 3)]
    squared = squared + shift(squared, "z", 2)
    squared = squared + shift(squared, "yl", 1)
    seq_loss = squared.reshape(1) / (lengths.astype(F32) * DT)
    ga[0] = after(ga[0], seq_loss)
    gb = [gb[0], shift_y(gb[1], 2), shift_y(gb[2], 1), shift_y(gb[3], -1)]
    a = partial_sums(sum_x_kernel, place, ga)
    a = [a[0], shift_y(a[1], 2), shift_y(a[2], 1), shift_y(a[3], -1)]
    b = partial_sums(sum_y_kernel, place, gb)
    b = [b[0]] + [shift(b[k], "x", k) for k in (1, 2, 3)]
    return last_sum(a + b), seq_loss


def solution(mesh):
    split = Mesh(mesh.devices.reshape(4, 2, 2, 2, 4), AXES)
    dp, tensor = ("x", "yh", "c"), ("yl", "z")
    placed = (
        P(dp + tensor, None),
        P(),
        P(None, tensor),
        P(None, tensor),
        P(None, tensor),
        P(tensor, None),
        P(None, tensor),
        P(dp, tensor),
        P(dp),
    )
    return jax.shard_map(
        shards, mesh=split, in_specs=placed, out_specs=(P(dp, tensor), P(dp)), check_vma=False
    )
```

```python
import functools
import math

import jax
import jax.numpy as jnp
from jax import lax
from jax.experimental import pallas as pl
from jax.experimental.pallas import tpu as pltpu
from jax.sharding import Mesh, PartitionSpec as P

HEAD_DIM = 128
DT = 8192
EPSILON = 1e-05
ROPE_BASE = 500000.0
NEG_LARGE = -1e30
AXES = ("x", "yh", "c", "yl", "z")
SIZES = {"x": 4, "yh": 2, "c": 2, "yl": 2, "z": 4}
F32 = jnp.float32
BF16 = jnp.bfloat16
PARAMS = pltpu.CompilerParams(vmem_limit_bytes=48 * 2**20)


def shift(value, axis, step):
    count = SIZES[axis]
    return lax.ppermute(value, axis, [(i, (i + step) % count) for i in range(count)])


def shift_y(value, step):
    return lax.ppermute(value, ("yh", "yl"), [(i, (i + step) % 4) for i in range(4)])


def cross_y(value):
    return lax.ppermute(value, ("yh", "yl"), [(0, 3), (3, 0), (1, 2), (2, 1)])


def after(value, *others):
    return lax.optimization_barrier((value, *others))[0]


def rows_of(array, start, count):
    return lax.dynamic_slice_in_dim(array, start, count, 0)


def pick(array, at, axis):
    return lax.dynamic_index_in_dim(array, at, axis, keepdims=False)


def dot(left, right):
    return jnp.dot(left, right, preferred_element_type=F32)


def norm_kernel(in_ref, gain_ref, out_ref):
    widened = in_ref[...].astype(F32)
    mean_square = jnp.mean(widened * widened, axis=-1, keepdims=True)
    out_ref[...] = (widened * lax.rsqrt(mean_square + EPSILON) * gain_ref[...]).astype(BF16)


def root_norm(inputs, norm_gain):
    return pl.pallas_call(
        norm_kernel,
        grid=(4,),
        in_specs=[
            pl.BlockSpec((32, 4096), lambda i: (i, 0)),
            pl.BlockSpec((1, 4096), lambda i: (0, 0)),
        ],
        out_specs=pl.BlockSpec((32, 4096), lambda i: (i, 0)),
        out_shape=jax.ShapeDtypeStruct((128, 4096), BF16),
        compiler_params=PARAMS,
    )(inputs, norm_gain.reshape(1, 4096))


def ring_step(block):
    return block ^ (block // 2)


def ring_position(index, z):
    return ((z + ring_step(index // 128)) % 4) * 128 + index % 128


def turned(product, cosine, sine, last):
    def turn(head):
        return head * cosine + pltpu.roll(head, 64, 1) * sine

    left, right = product[:, :128], product[:, 128:]
    right = jnp.where(last, right, turn(right))
    return jnp.concatenate([turn(left), right], axis=1).astype(BF16)


def own_heads_kernel(*refs):
    *x_refs, q_ref, kv_ref, cos_ref, sin_ref, out_ref = refs
    x = jnp.concatenate([ref[...] for ref in x_refs if ref.shape[1] == 4096], axis=0)
    last = pl.program_id(0) == 2

    def finish(w_ref):
        out_ref[...] = turned(dot(x, w_ref[...]), cos_ref[...], sin_ref[...], last)

    pl.when(pl.program_id(0) < 2)(lambda: finish(q_ref))
    pl.when(last)(lambda: finish(kv_ref))


def own_heads_of(pieces, w_query, kv_own, cosine, sine, earlier=None):
    rows, at = sum(v.shape[0] for v in pieces), 0 if earlier is None else 3
    turn = pl.BlockSpec((rows, 128), lambda n: (at, 0))
    kept, alias = [], {}
    if earlier is not None:
        kept, alias = [earlier], {0: 0}
    return pl.pallas_call(
        own_heads_kernel,
        grid=(3,),
        in_specs=[pl.BlockSpec(memory_space=pl.ANY)] * len(kept)
        + [pl.BlockSpec(v.shape, lambda n: (0, 0)) for v in pieces]
        + [
            pl.BlockSpec((4096, 256), lambda n: (0, jnp.minimum(n, 1))),
            pl.BlockSpec((4096, 256), lambda n: (0, 0)),
            turn,
            turn,
        ],
        out_specs=pl.BlockSpec((rows, 256), lambda n: (at, n)),
        out_shape=jax.ShapeDtypeStruct((512, 768), BF16),
        input_output_aliases=alias,
        compiler_params=PARAMS,
    )(*kept, *pieces, w_query, kv_own, cosine, sine)


def placed(refs):
    start = 0
    for ref in refs:
        yield slice(start, start + ref.shape[0]), ref
        start += ref.shape[0]


def far_heads_kernel(at_ref, *refs):
    *pieces, w0, w1, w2, w3, cos_ref, sin_ref, out_ref, x_ref = refs
    core = at_ref[3]

    @pl.when(pl.program_id(0) == 0)
    def _():
        for here, ref in placed(pieces):
            for k in range(4):
                source = ((core + k // 2) % 2) * 2048 + (k % 2) * 1024
                x_ref[here, 1024 * k : 1024 * k + 1024] = ref[
                    :, pl.ds(pl.multiple_of(source, 1024), 1024)
                ]

    product = dot(x_ref[:, :1024], w0[...])
    for k, ref in ((1, w1), (2, w2), (3, w3)):
        product = product + dot(x_ref[:, 1024 * k : 1024 * k + 1024], ref[...])
    out_ref[...] = turned(product, cos_ref[...], sin_ref[...], pl.program_id(0) == 2)


def far_heads_of(place, pieces, quarters, cosine, sine):
    whole = [pl.BlockSpec(v.shape, lambda n, at: (0, 0)) for v in pieces]
    weight = pl.BlockSpec((1024, 256), lambda n, at: (0, n))
    turn = pl.BlockSpec((512, 128), lambda n, at: (0, 0))
    return pl.pallas_call(
        far_heads_kernel,
        grid_spec=pltpu.PrefetchScalarGridSpec(
            num_scalar_prefetch=1,
            grid=(3,),
            in_specs=whole + [weight] * 4 + [turn] * 2,
            out_specs=pl.BlockSpec((512, 256), lambda n, at: (0, n)),
            scratch_shapes=[pltpu.VMEM((512, 4096), BF16)],
        ),
        out_shape=jax.ShapeDtypeStruct((512, 768), BF16),
        compiler_params=PARAMS,
    )(place, *pieces, *quarters, cosine, sine)


def attend_kernel(at_ref, q_ref, own_ref, far_ref, out_ref):
    z, yl, length = at_ref[0], at_ref[1], at_ref[2]
    factor = math.log2(math.e) / math.sqrt(HEAD_DIM)
    q = jnp.concatenate([q_ref[:, 128 * h : 128 * h + 128] for h in range(4)], axis=0)
    shape = (512, 512)
    ring = ring_position(lax.broadcasted_iota(jnp.int32, (1, 512), 1), z)
    q_at = ((z + ring_step(pl.program_id(0))) % 4) * 128
    q_at = q_at + lax.broadcasted_iota(jnp.int32, (128, 1), 0)
    contract = (((1,), (1,)), ((), ()))

    def scores(kv_ref):
        return factor * lax.dot_general(q, kv_ref[:, :128], contract, preferred_element_type=F32)

    own_ok = (ring <= q_at) & (ring + yl * 512 < length)
    bias = jnp.where(jnp.broadcast_to(own_ok, (128, 512)), 0.0, NEG_LARGE)
    own = (scores(own_ref).reshape(4, 128, 512) + bias[None]).reshape(shape)
    top = jnp.max(own, axis=-1, keepdims=True)

    def store(total, blended):
        blended = (blended / total).astype(BF16)
        for h in range(4):
            out_ref[:, 128 * h : 128 * h + 128] = blended[128 * h : 128 * h + 128]

    @pl.when(yl == 0)
    def _():
        weights = jnp.exp2(own - top)
        store(
            jnp.sum(weights, axis=-1, keepdims=True), dot(weights.astype(BF16), own_ref[:, 128:])
        )

    @pl.when(yl == 1)
    def _():
        far = scores(far_ref) + jnp.where(ring < length, 0.0, NEG_LARGE)
        highest = jnp.maximum(top, jnp.max(far, axis=-1, keepdims=True))
        own_weights = jnp.exp2(own - highest)
        far_weights = jnp.exp2(far - highest)
        total = jnp.sum(own_weights, axis=-1, keepdims=True) + jnp.sum(
            far_weights, axis=-1, keepdims=True
        )
        store(
            total,
            dot(own_weights.astype(BF16), own_ref[:, 128:])
            + dot(far_weights.astype(BF16), far_ref[:, 128:]),
        )


def attend(place, heads, far_kv):
    return pl.pallas_call(
        attend_kernel,
        grid_spec=pltpu.PrefetchScalarGridSpec(
            num_scalar_prefetch=1,
            grid=(4,),
            in_specs=[
                pl.BlockSpec((128, 512), lambda j, at: (j, 0)),
                pl.BlockSpec((512, 256), lambda j, at: (0, 2)),
                pl.BlockSpec((512, 256), lambda j, at: (0, 0)),
            ],
            out_specs=pl.BlockSpec((128, 512), lambda j, at: (j, 0)),
        ),
        out_shape=jax.ShapeDtypeStruct((512, 512), BF16),
        compiler_params=PARAMS,
    )(place, heads, heads, far_kv)


def layer_kernel(at_ref, student_ref, *refs):
    *parts, out_ref = refs
    total = parts[0][...].astype(F32)
    for part in parts[1:]:
        total = total + part[...].astype(F32)
    layer = (student_ref[...].astype(F32) + total).astype(BF16)
    even = [layer[:, 512 * i : 512 * i + 256] for i in range(8)]
    odd = [layer[:, 512 * i + 256 : 512 * i + 512] for i in range(8)]

    @pl.when(at_ref[3] == 0)
    def _():
        out_ref[...] = jnp.concatenate(even + odd, axis=1)

    @pl.when(at_ref[3] == 1)
    def _():
        out_ref[...] = jnp.concatenate(odd + even, axis=1)


def make_layer(place, student_in, parts):
    spec = pl.BlockSpec((32, 4096), lambda i, at: (i, 0))
    return pl.pallas_call(
        layer_kernel,
        grid_spec=pltpu.PrefetchScalarGridSpec(
            num_scalar_prefetch=1, grid=(4,), in_specs=[spec] * 5, out_specs=spec
        ),
        out_shape=jax.ShapeDtypeStruct((128, 4096), BF16),
        compiler_params=PARAMS,
    )(place, student_in, *parts)


def out_kernel(at_ref, own, far, w, w0, w1, w2, w3, *refs):
    *out_refs, x_ref = refs

    @pl.when(pl.program_id(0) == 0)
    def _():
        x_ref[:, :512] = own[...]
        for k in range(2):
            source = ((at_ref[3] + k) % 2) * 256
            x_ref[:, 512 + 256 * k : 768 + 256 * k] = far[:, pl.ds(pl.multiple_of(source, 256), 256)]

    weights = jnp.concatenate([ref[...] for ref in (w, w0, w1, w2, w3)], axis=0)
    total = dot(x_ref[...], weights)
    for j, ref in enumerate(out_refs):
        ref[...] = total[128 * j : 128 * j + 128].astype(BF16)


def out_blocks(place, own, far, w_out, quarters):
    att = pl.BlockSpec((512, 512), lambda n, at: (0, 0))
    quarter = pl.BlockSpec((128, 1024), lambda n, at: (0, n))
    fetched = [pl.BlockSpec((v.shape[0], 1024), lambda n, at: (0, n)) for v in quarters]
    return pl.pallas_call(
        out_kernel,
        grid_spec=pltpu.PrefetchScalarGridSpec(
            num_scalar_prefetch=1,
            grid=(4,),
            in_specs=[att, att, pl.BlockSpec((512, 1024), lambda n, at: (0, n))] + fetched,
            out_specs=[quarter] * 4,
            scratch_shapes=[pltpu.VMEM((512, 1024), BF16)],
        ),
        out_shape=[jax.ShapeDtypeStruct((128, 4096), BF16)] * 4,
        compiler_params=PARAMS,
    )(place, own, far, w_out, *quarters)


def error_kernel(first, rows, kept, at_ref, *refs):
    layers = refs[kept:-13] if rows < 512 else refs[:2]
    p_own, f0, f1, f2, f3, t_own, t_far, err_ref, sum_ref = refs[len(layers) + kept :][:9]
    x_ref, n_ref = refs[-2:]
    step = pl.program_id(0)
    z, yl, length, core = at_ref[0], at_ref[1], at_ref[2], at_ref[3]

    @pl.when(step == 0)
    def _():
        if rows == 512:
            x_ref[:, :2048] = layers[0][...]
            x_ref[:, 2048:] = layers[1][...]
        else:
            for here, ref in placed(layers):
                x_ref[here, :] = ref[...]
            refs[-4][...] = x_ref[:, :2048]
            refs[-3][...] = x_ref[:, 2048:]
        for i in range(16):
            block = i // 2 + 8 * ((core + i) % 2)
            n_ref[:, 256 * i : 256 * i + 256] = x_ref[
                :, pl.ds(pl.multiple_of(block * 256, 256), 256)
            ]
        sum_ref[...] = refs[3][...] if kept else jnp.zeros((1, 1), F32)

    index = 128 * first + lax.broadcasted_iota(jnp.int32, (rows, 1), 0)
    pos = yl * 512 + ring_position(index, z)
    live = jnp.broadcast_to(pos < length, (rows, 256))

    def part(columns, predicted, t_ref):
        teacher = [
            t_ref[pl.ds(pl.multiple_of(((z + ring_step(first + j)) % 4) * 128, 128), 128), :]
            for j in range(rows // 128)
        ]
        residue = predicted - jnp.concatenate(teacher, axis=0).astype(F32)
        residue = jnp.where(live, residue, 0.0)
        err_ref[:, columns] = (residue / length.astype(F32)).astype(BF16)
        sum_ref[...] += jnp.sum(residue * residue).reshape(1, 1)

    part(slice(0, 256), dot(n_ref[...], p_own[...]), t_own)
    predicted = dot(x_ref[:, :1024], f0[...])
    for k, ref in ((1, f1), (2, f2), (3, f3)):
        predicted = predicted + dot(x_ref[:, 1024 * k : 1024 * k + 1024], ref[...])
    part(slice(256, 512), predicted, t_far)


def errors(half, place, layers, projection, p_far, t_own, t_far, earlier=()):
    rows = 512 if layers[0].shape[0] == 512 else sum(v.shape[0] for v in layers)
    first, kept = (3, 4) if earlier else (0, 0)

    def columns(n, at):
        return (0, 2 * half + n)

    def own_rows(n, at):
        return (at[1], 2 * half + n)

    def constant(n, at):
        return (0, 0)

    anywhere = pl.BlockSpec(memory_space=pl.ANY)
    kept_specs = [anywhere] * 3 + [pl.BlockSpec((1, 1), constant)] if earlier else []
    out_specs = [
        pl.BlockSpec((rows, 512), lambda n, at: (first, n)),
        pl.BlockSpec((1, 1), constant),
    ]
    out_shape = [
        jax.ShapeDtypeStruct((512, 1024), BF16),
        jax.ShapeDtypeStruct((1, 1), F32),
    ]
    if rows < 512:
        out_specs += [pl.BlockSpec((rows, 2048), lambda n, at: (first, 0))] * 2
        out_shape += [jax.ShapeDtypeStruct((512, 2048), BF16)] * 2
    if earlier:
        err, total, left, right = earlier
        earlier = (err, left, right, total)
    return pl.pallas_call(
        functools.partial(error_kernel, first, rows, kept),
        grid_spec=pltpu.PrefetchScalarGridSpec(
            num_scalar_prefetch=1,
            grid=(2,),
            in_specs=kept_specs
            + [pl.BlockSpec(v.shape, constant) for v in layers]
            + [pl.BlockSpec((4096, 256), columns)]
            + [pl.BlockSpec((1024, 256), columns)] * 4
            + [pl.BlockSpec((512, 256), own_rows), pl.BlockSpec((512, 256), columns)],
            out_specs=out_specs,
            scratch_shapes=[pltpu.VMEM((rows, 4096), BF16)] * 2,
        ),
        out_shape=out_shape,
        input_output_aliases={1: 0, 2: 2, 3: 3} if earlier else {},
        compiler_params=PARAMS,
    )(place, *earlier, *layers, projection, *p_far, t_own, t_far)


def split_columns(product):
    own = jnp.concatenate([product[:, :256], product[:, 512:768]], axis=1)
    far = jnp.concatenate([product[:, 256:512], product[:, 768:]], axis=1)
    return own, far


def by_y(at_ref, own, far, store):
    for t in (0, 1):
        this, that = slice(256 * t, 256 * t + 256), slice(256 - 256 * t, 512 - 256 * t)

        @pl.when(at_ref[5] == t)
        def _():
            store(0, own[this])
            store(1, own[that])

        @pl.when(at_ref[6] == t)
        def _():
            store(2, far[this])
            store(3, far[that])


def gradient_kernel(by_x, at_ref, mine, theirs, e_mine, e_theirs, *out_refs):
    contract = (((0,), (0,)), ((), ()))
    product = lax.dot_general(mine[...], e_mine[...], contract, preferred_element_type=F32)
    product = product + lax.dot_general(
        theirs[...], e_theirs[...], contract, preferred_element_type=F32
    )
    product = product.astype(BF16)
    if by_x:
        for k, ref in enumerate(out_refs):

            @pl.when(pl.program_id(0) == k)
            def _():
                ref[...] = product
    else:

        def store(k, value):
            out_refs[k][0] = value

        by_y(at_ref, *split_columns(product), store)


def gradient(by_x, place, mine, theirs, e_mine, e_theirs):
    rows = pl.BlockSpec((512, 512), lambda k, at: (0, (at[4] + k) % 4))
    error = pl.BlockSpec((512, 1024), lambda k, at: (0, 0))
    if by_x:
        out_spec = pl.BlockSpec((512, 1024), lambda k, at: (0, 0))
        shape = (512, 1024)
    else:
        out_spec = pl.BlockSpec((1, 256, 512), lambda k, at: (k, 0, 0))
        shape = (4, 256, 512)
    return pl.pallas_call(
        functools.partial(gradient_kernel, by_x),
        grid_spec=pltpu.PrefetchScalarGridSpec(
            num_scalar_prefetch=1,
            grid=(4,),
            in_specs=[rows, rows, error, error],
            out_specs=[out_spec] * 4,
        ),
        out_shape=[jax.ShapeDtypeStruct(shape, BF16)] * 4,
        compiler_params=PARAMS,
    )(place, mine, theirs, e_mine, e_theirs)


def total_of(refs):
    total = refs[0][...].astype(F32)
    for ref in refs[1:]:
        total = total + ref[...].astype(F32)
    return total


def sum_x_kernel(at_ref, *refs):
    def store(k, value):
        refs[4 + k][...] = value

    by_y(at_ref, *split_columns(total_of(refs[:4]).astype(BF16)), store)


def sum_y_kernel(at_ref, *refs):
    total = total_of(refs[:4]).astype(BF16)
    for k in range(4):
        refs[4 + k][...] = total[k]


def partial_sums(kernel, place, arrays):
    return pl.pallas_call(
        kernel,
        grid_spec=pltpu.PrefetchScalarGridSpec(
            num_scalar_prefetch=1,
            grid=(1,),
            in_specs=[pl.BlockSpec(memory_space=pltpu.VMEM)] * 4,
            out_specs=[pl.BlockSpec(memory_space=pltpu.VMEM)] * 4,
        ),
        out_shape=[jax.ShapeDtypeStruct((256, 512), BF16)] * 4,
        compiler_params=PARAMS,
    )(place, *arrays)


def last_kernel(*refs):
    refs[8][:, :512] = total_of(refs[:4])
    refs[8][:, 512:] = total_of(refs[4:8])


def last_sum(arrays):
    return pl.pallas_call(
        last_kernel,
        out_shape=jax.ShapeDtypeStruct((256, 1024), F32),
        compiler_params=PARAMS,
    )(*arrays)


def fetch(plus, minus):
    return shift_y(plus, 1), shift_y(minus, -1)


def swap(pair):
    return tuple(shift(v, "c", 1) for v in pair)


def shards(
    student_in, norm_gain, w_query, w_key, w_value, w_out, projection, teacher_rows, lengths
):
    x, yh, c, yl, z = (lax.axis_index(a) for a in AXES)
    length = lengths[0]
    to_up = jnp.where(yl == 0, yh, 1 - yh)
    place = jnp.stack([z, yl, length, c, x, yh, to_up])

    def around(own):
        near, back = shift(own, "z", -1), shift(own, "z", 1)
        return [own, near, back], [shift(back[:64], "z", 1), shift(near[64:], "z", -1)]

    kv_own = jnp.concatenate([w_key, w_value], axis=1)

    def quarter(at):
        return jnp.concatenate([rows_of(w, at, 1024) for w in (w_query, w_key, w_value)], axis=1)

    quarters = quarter(c * 2048), quarter(c * 2048 + 1024)
    first = fetch(*quarters)
    inverse = ROPE_BASE ** (-2.0 * jnp.arange(HEAD_DIM // 2).astype(F32) / HEAD_DIM)
    pos = yl * 512 + ring_position(jnp.arange(512), z)
    angles = pos.astype(F32)[:, None] * inverse
    cosine, sine = jnp.cos(angles), jnp.sin(angles)
    cosine = jnp.concatenate([cosine, cosine], axis=1)
    sine = jnp.concatenate([-sine, sine], axis=1)
    pieces, ends = around(root_norm(after(student_in, *quarters), norm_gain))
    proj_c = pick(projection.reshape(8, 2, 256, 1024), c, 1).reshape(2048, 1024)
    sends = proj_c[:1024], proj_c[1024:]
    out_sends = rows_of(w_out, c * 256, 96), rows_of(w_out, c * 256 + 96, 160)
    *pieces, cosine, sine, kv_own, s0, s1, o0, o1 = lax.optimization_barrier(
        (*pieces, cosine, sine, kv_own, *sends, *out_sends)
    )
    sends, out_sends = (s0, s1), (o0, o1)
    near_heads = own_heads_of(pieces, w_query, kv_own, cosine, sine)
    first = tuple(after(v, *ends, near_heads) for v in first)
    first_sib = swap(first)
    out_sends = [after(v, *first) for v in out_sends]
    second = shift(out_sends[0], "yl", 1), cross_y(out_sends[1])
    ends = [after(v, near_heads) for v in ends]
    own_heads = own_heads_of(ends, w_query, kv_own, cosine, sine, near_heads)
    kv_early = shift(own_heads[:, 512:], "yl", 1)
    far_weights = [*first, *(after(v, own_heads) for v in first_sib)]
    far_heads = far_heads_of(place, pieces + ends, far_weights, cosine, sine)
    kv_late = shift(far_heads[:, 512:], "yl", 1)
    att_far = attend(place, far_heads, kv_early)
    second = tuple(after(v, att_far) for v in second)
    second_sib = swap(second)
    kv_late = after(kv_late, att_far)
    att_own = attend(place, own_heads, kv_late)
    b0, b1, b2, b3 = out_blocks(place, att_own, att_far, w_out, [*second, *second_sib])

    third = fetch(*(after(v, kv_late, *second) for v in sends))

    parts = [b0, shift(b3, "z", 2), shift(b1, "z", 1), shift(b2, "z", -1)]
    third_up, third_down, *parts = lax.optimization_barrier((*third, *parts))
    own_layer = make_layer(place, student_in, parts)
    teach_far = shift(after(rows_of(teacher_rows, (1 - yl) * 512, 512), own_layer), "yl", 1)
    layers, ends = around(own_layer)
    p_far = [third_up, third_down, shift(third_up, "c", 1), shift(third_down, "c", 1)]
    same = (projection, p_far, teacher_rows, teach_far)
    near = errors(1, place, layers, *same)
    ends = [after(v, near[0]) for v in ends]
    err_b, sq_b, mine, other = errors(1, place, ends, *same, earlier=near)
    theirs = shift(other, "c", 1)
    err_b_sib = shift(err_b, "c", 1)
    err_a, sq_a = errors(0, place, [mine, after(other, err_b)], *same)
    err_a_sib = shift(err_a, "c", 1)

    gb = gradient(False, place, mine, theirs, after(err_b, err_a), err_b_sib)
    squared = after(sq_a + sq_b, gb[0])
    squared = squared + shift(squared, "z", 1)
    ga = gradient(True, place, mine, theirs, after(err_a, gb[0], squared), err_a_sib)
    ga = [ga[0]] + [shift(ga[k], "x", k) for k in (1, 2, 3)]
    squared = squared + shift(squared, "z", 2)
    gb = [gb[0], shift_y(gb[1], 2), shift_y(gb[2], 1), shift_y(gb[3], -1)]
    gb[0] = after(gb[0], squared)
    squared = after(squared, gb[2])
    squared = squared + shift(squared, "yl", 1)
    seq_loss = squared.reshape(1) / (lengths.astype(F32) * DT)
    ga[0] = after(ga[0], seq_loss)
    a = partial_sums(sum_x_kernel, place, ga)
    a = [a[0], shift_y(a[1], 2), shift_y(a[2], 1), shift_y(a[3], -1)]
    b = partial_sums(sum_y_kernel, place, gb)
    b = [b[0]] + [shift(b[k], "x", k) for k in (1, 2, 3)]
    return last_sum(a + b), seq_loss


def solution(mesh):
    split = Mesh(mesh.devices.reshape(4, 2, 2, 2, 4), AXES)
    dp, tensor = ("x", "yh", "c"), ("yl", "z")
    placed = (
        P(dp + tensor, None),
        P(),
        P(None, tensor),
        P(None, tensor),
        P(None, tensor),
        P(tensor, None),
        P(None, tensor),
        P(dp, tensor),
        P(dp),
    )
    return jax.shard_map(
        shards, mesh=split, in_specs=placed, out_specs=(P(dp, tensor), P(dp)), check_vma=False
    )
```
